128 devices in a mesh: dp: 64 (over y_hi, x, z, core), tensor: 2 (over y_lo).
Axes of the slice: x: 4, y: 4 (y_hi: 2, y_lo: 2; y = y_hi * 2 + y_lo), z: 4, core: 2. Of those that a mesh axis runs over, the one named last changes fastest.
Arguments:
- tokens_in: bfloat16 [32768, 1536], P(('dp', 'tensor')), may hold values from -6 to 6
- routes: int32 [32768, 4], P('dp'), may hold values from 0 to 7, all different within a row; in each aligned block of 512 rows (0 to 511, 512 to 1023, ...) at most 320 rows name the same one
- cotangent: bfloat16 [32768, 1536], P(('dp', 'tensor')), may hold values from -6 to 6
- attn_gain: bfloat16 [1536], P('dp'), may hold values from 0.5 to 1.5
- query_proj: bfloat16 [1536, 1536], P('dp', 'tensor'), may hold values from -0.15625 to 0.15625
- key_proj: bfloat16 [1536, 256], P('dp', 'tensor'), may hold values from -0.15625 to 0.15625
- value_proj: bfloat16 [1536, 256], P('dp', 'tensor'), may hold values from -0.15625 to 0.15625
- output_proj: bfloat16 [1536, 1536], P('dp', 'tensor'), may hold values from -0.625 to 0.625
- ffn_gain: bfloat16 [1536], P('dp'), may hold values from 0.5 to 1.5
- router_proj: bfloat16 [1536, 8], P('dp'), may hold values from -0.078125 to 0.078125
- expert_gate: bfloat16 [1536, 8, 768], P('dp', None, 'tensor'), may hold values from -0.15625 to 0.15625
- expert_up: bfloat16 [1536, 8, 768], P('dp', None, 'tensor'), may hold values from -0.15625 to 0.15625
- expert_down: bfloat16 [1536, 8, 768], P('dp', None, 'tensor'), may hold values from -0.4375 to 0.4375
Outputs:
- layer_output: bfloat16 [32768, 1536], P(('dp', 'tensor'))
- grad_input: bfloat16 [32768, 1536], P(('dp', 'tensor'))
- grad_attn_gain: float32 [1536], P(('dp', 'tensor'))
- grad_query: float32 [1536, 1536], P('dp', 'tensor')
- grad_key: float32 [1536, 256], P('dp', 'tensor')
- grad_value: float32 [1536, 256], P('dp', 'tensor')
- grad_output_proj: float32 [1536, 1536], P('dp', 'tensor')
- grad_ffn_gain: float32 [1536], P(('dp', 'tensor'))
- grad_router: float32 [1536, 8], P(('dp', 'tensor'))
- grad_expert_gate: float32 [1536, 8, 768], P('dp', None, 'tensor')
- grad_expert_up: float32 [1536, 8, 768], P('dp', None, 'tensor')
- grad_expert_down: float32 [1536, 8, 768], P('dp', None, 'tensor')
The draws below stay inside these ranges and needn't reach their ends.
Inputs may be any that keep to these rules, and one draw needn't show every extreme that they name: `routes`: each row names 4 different experts; in each aligned block of 512 rows (one sequence) no expert is named by more than 320 rows, and one is named by exactly 320.
All inputs are finite; a program needn't handle non-finite values.
Results may differ from the reference program's by a relative error of at most 0.02.
Values may be sent and summed in bfloat16 or wider, within the bound.
A program may use at most 256 MiB of HBM per device.

```python
import math
import jax
import jax.numpy as jnp
import numpy as np
from jax import lax

D = 1536
H = 12
KV = 2
HD = 128
FF = 768
E = 8
TOP = 4
SEQ = 512
CAP = 320
TOKENS = 32768
N_DP = 64


def block_levels(stream_key, dims, pieces, smallest, high):
    def one(axis_at, blocks):
        draws = jax.random.uniform(jax.random.fold_in(jax.random.fold_in(stream_key, 6), axis_at), (blocks,), jnp.float32, smallest / len(pieces), high / len(pieces))
        return jnp.repeat(jnp.exp(draws), dims[axis_at] // blocks).reshape((-1,) + (1,) * (len(dims) - axis_at - 1))

    factor_of = one(*pieces[0])
    for cut in pieces[1:]:
        factor_of = factor_of * one(*cut)
    return factor_of


def routed_block(stream_key, own, number, rows, amount, top, most, lean):
    order = jax.random.permutation(stream_key, amount)
    heavy_load, common = load_shares(amount, rows * top, most, lean, True), load_shares(amount, rows * top, most, lean, False)
    places = jnp.arange(amount)

    def named(tallies, rotation):
        used = int((tallies > 0).sum())
        fixed = max(1, used // 4)
        passed = fixed + (places - fixed + rotation * (used - fixed)) % max(1, amount - fixed)
        return jnp.zeros((amount,), jnp.int32).at[order[jnp.where(places < fixed, places, passed)]].set(jnp.asarray(tallies, jnp.int32))

    tallies = jnp.where(number % 4 == 0, named(heavy_load, number // 4), named(common, number - number // 4 - 1))
    mixed = jax.random.permutation(jax.random.fold_in(own, 3), amount)
    source_of, receiver = mixed[0:amount // 2 * 2:2], mixed[1:amount // 2 * 2:2]
    slack = jnp.minimum(tallies[source_of] - 1, most - tallies[receiver]) // 2
    slack = jnp.where((source_of == order[0]) | (receiver == order[0]) | (tallies[receiver] == 0), 0, jnp.maximum(slack, 0))
    passed = jax.random.randint(jax.random.fold_in(own, 4), (amount // 2,), 0, 1 << 20) % (slack + 1)
    tallies = tallies.at[source_of].add(-passed).at[receiver].add(passed)
    labels = jnp.searchsorted(jnp.cumsum(tallies), jnp.arange(rows * top), side="right").astype(jnp.int32)
    table = labels.reshape(top, rows).T
    table = table[jax.random.permutation(jax.random.fold_in(own, 1), rows)]
    rotation = jax.random.randint(jax.random.fold_in(own, 2), (rows, 1), 0, top)
    return jnp.take_along_axis(table, (jnp.arange(top)[None, :] + rotation) % top, axis=1)


def load_shares(amount, total, most, lean, full):
    loads = [(1 << 20) // math.isqrt(grade ** lean) + 1 for grade in range(1, amount + 1)]
    largest = most if full else min(most, max(-(-total // amount), total * loads[0] // sum(loads)))
    least = 1 if total - largest >= amount - 1 else 0
    given, spare = [largest] + [least] * (amount - 1), total - largest - least * (amount - 1)
    while spare > 0:
        movable = [i for i in range(1, amount) if given[i] < largest] or [i for i in range(1, amount) if given[i] < most]
        whole, budget = sum([loads[i] for i in movable]), spare
        for i in movable:
            addition = min(most - given[i], max(1, budget * loads[i] // whole), spare)
            given[i] = given[i] + addition
            spare = spare - addition
    return np.array(given)


def gaussian(key, extent, scale, limit, cuts=(), kind=jnp.bfloat16):
    values = jax.random.normal(key, extent, jnp.float32) * scale
    if len(cuts) > 0:
        values = block_levels(key, extent, cuts, -0.22, 0.18) * values
    return jnp.clip(values, min=-limit, max=limit).astype(kind)


def setup_inputs(seed: int = 0) -> dict:
    key_of = jax.random.split(jax.random.key(seed), 14)
    tokens_in = gaussian(key_of[0], (TOKENS, D), 1.0, 6.0, ((0, 128),))
    routes_keys = jax.random.split(jax.random.fold_in(key_of[1], 1), TOKENS // SEQ)
    routes_turns = jax.random.permutation(jax.random.fold_in(key_of[1], 3), TOKENS // SEQ)
    routes = jax.vmap(lambda own, number: routed_block(jax.random.fold_in(key_of[1], 2), own, number, SEQ, E, TOP, CAP, 1))(routes_keys, routes_turns).reshape((TOKENS, TOP))
    cotangent = gaussian(key_of[2], (TOKENS, D), 1.0, 6.0, ((0, 128),))
    attn_gain = jnp.clip(1.0 + 0.1 * jax.random.normal(key_of[3], (D,), jnp.float32), 0.5, 1.5).astype(jnp.bfloat16)
    query_proj = gaussian(key_of[4], (D, H * HD), D ** -0.5, 0.15625, ((0, 64), (1, 2)))
    key_proj = gaussian(key_of[5], (D, KV * HD), D ** -0.5, 0.15625, ((0, 64), (1, 2)))
    value_proj = gaussian(key_of[6], (D, KV * HD), D ** -0.5, 0.15625, ((0, 64), (1, 2)))
    output_proj = gaussian(key_of[7], (D, H * HD), (H * HD // 16) ** -0.5, 0.625, ((0, 64), (1, 2)))
    ffn_gain = jnp.clip(1.0 + 0.1 * jax.random.normal(key_of[8], (D,), jnp.float32), 0.5, 1.5).astype(jnp.bfloat16)
    router_proj = gaussian(key_of[9], (D, E), (4 * D) ** -0.5, 0.078125, ((0, 64),))
    expert_gate = gaussian(key_of[10], (D, E, FF), D ** -0.5, 0.15625, ((0, 64), (2, 2)))
    expert_up = gaussian(key_of[11], (D, E, FF), D ** -0.5, 0.15625, ((0, 64), (2, 2)))
    expert_down = gaussian(key_of[12], (D, E, FF), (FF // 4) ** -0.5, 0.4375, ((0, 64), (2, 2)))
    return dict(tokens_in=tokens_in, routes=routes, cotangent=cotangent, attn_gain=attn_gain, query_proj=query_proj, key_proj=key_proj, value_proj=value_proj, output_proj=output_proj, ffn_gain=ffn_gain, router_proj=router_proj, expert_gate=expert_gate, expert_up=expert_up, expert_down=expert_down)


NORM_EPSILON = 1e-06
ROPE_BASE = 1000000.0
HIGHEST_MODE = lax.Precision.HIGHEST

@jax.custom_vjp
def low(v):
    return lax.optimization_barrier(v.astype(jnp.bfloat16)).astype(jnp.float32)

@jax.custom_vjp
def low_back(v):
    return v

def low_keep(v):
    return (low(v), None)

def low_pass(kept, grad):
    return (grad,)

def back_keep(v):
    return (v, None)

def back_low(kept, grad):
    return (low(grad),)
low.defvjp(low_keep, low_pass)
low_back.defvjp(back_keep, back_low)

def rope_tables(length, head_size):
    half_size = head_size // 2
    frequency = ROPE_BASE ** (-(2.0 * jnp.arange(half_size, dtype=jnp.float32)) / head_size)
    angles = jnp.arange(length, dtype=jnp.float32)[:, None] * frequency[None, :]
    angles = jnp.concatenate([angles, angles], axis=1)
    return (jnp.cos(angles), jnp.sin(angles))

def rotate(values, cosine, sine_table):
    half_size = values.shape[-1] // 2
    turned = jnp.concatenate([-values[..., half_size:], values[..., :half_size]], axis=-1)
    return values * cosine[:, None, :] + turned * sine_table[:, None, :]

def layer_forward(tokens, route_rows, attn_gain, query_proj, key_proj, value_proj, output_proj, ffn_gain, router_proj, expert_gate, expert_up, expert_down):
    length = tokens.shape[0]
    group_size = H // KV
    inverse_one = lax.rsqrt(lax.optimization_barrier(jnp.mean(tokens * tokens, axis=1, keepdims=True)) + NORM_EPSILON)
    normed_one = low(tokens * inverse_one * attn_gain)
    query_lin = low_back(jnp.dot(normed_one, query_proj, precision=HIGHEST_MODE)).reshape(length, H, HD)
    key_lin = low_back(jnp.dot(normed_one, key_proj, precision=HIGHEST_MODE)).reshape(length, KV, HD)
    values = low(low_back(jnp.dot(normed_one, value_proj, precision=HIGHEST_MODE))).reshape(length, KV, HD)
    cosine, sine_table = rope_tables(length, HD)
    queries = low(rotate(query_lin, cosine, sine_table)).reshape(length, KV, group_size, HD)
    keys = low(rotate(key_lin, cosine, sine_table))
    scores = low_back(jnp.einsum('qkgd,skd->kgqs', queries, keys, precision=HIGHEST_MODE) * HD ** (-0.5))
    position = jnp.arange(length)
    allowed = position[:, None] >= position[None, :]
    scores = jnp.where(allowed, scores, -1e+30)
    attn_probs = low(jax.nn.softmax(scores, axis=-1))
    attended = jnp.einsum('kgqs,skd->qkgd', attn_probs, values, precision=HIGHEST_MODE).reshape(length, H * HD)
    attended = low(low_back(attended))
    branch = low_back(jnp.einsum('sh,dh->sd', attended, output_proj, precision=HIGHEST_MODE))
    residual = tokens + branch
    inverse_two = lax.rsqrt(lax.optimization_barrier(jnp.mean(residual * residual, axis=1, keepdims=True)) + NORM_EPSILON)
    normed_two = low(residual * inverse_two * ffn_gain)
    logits = jnp.dot(normed_two, router_proj, precision=HIGHEST_MODE)
    gate_probs = jax.nn.softmax(jnp.take_along_axis(logits, route_rows, axis=1), axis=1)
    chosen = (route_rows[:, :, None] == jnp.arange(E)[None, None, :]).astype(jnp.float32)
    mixing = lax.optimization_barrier(jnp.sum(gate_probs[:, :, None] * chosen, axis=1))
    gate_in = low_back(jnp.einsum('sd,def->esf', normed_two, expert_gate, precision=HIGHEST_MODE))
    up_in = low_back(jnp.einsum('sd,def->esf', normed_two, expert_up, precision=HIGHEST_MODE))
    hidden = low(jax.nn.silu(gate_in) * up_in)
    expert_out = low_back(jnp.einsum('esf,def->esd', hidden, expert_down, precision=HIGHEST_MODE))
    return residual + jnp.einsum('se,esd->sd', mixing, expert_out, precision=HIGHEST_MODE)

def reference(tokens_in, routes, cotangent, attn_gain, query_proj, key_proj, value_proj, output_proj, ffn_gain, router_proj, expert_gate, expert_up, expert_down):
    params = tuple((item.astype(jnp.float32) for item in (attn_gain, query_proj, key_proj, value_proj, output_proj, ffn_gain, router_proj, expert_gate, expert_up, expert_down)))
    route_blocks = routes.reshape(N_DP, SEQ, TOP)

    def whole_batch(tokens, weights):

        def scan_step(carry, scan_item):
            return (carry, jax.checkpoint(layer_forward)(scan_item[0], scan_item[1], *weights))
        _, outputs = lax.scan(scan_step, None, (tokens.reshape(N_DP, SEQ, D), route_blocks))
        return outputs.reshape(N_DP * SEQ, D)
    layer_out, pullback = jax.vjp(whole_batch, tokens_in.astype(jnp.float32), params)
    grad_tokens, grads = pullback(cotangent.astype(jnp.float32))
    return (layer_out.astype(jnp.bfloat16), grad_tokens.astype(jnp.bfloat16), grads[0], grads[1], grads[2], grads[3], grads[4], grads[5], grads[6], grads[7], grads[8], grads[9])
```

```python
import functools

import jax
import jax.numpy as jnp
from jax import lax
from jax.experimental import pallas as pl
from jax.experimental.pallas import tpu as pltpu
from jax.sharding import PartitionSpec as P

HD = 128
E = 8
D = 1536
SEQ = 512
OWN = 256
HALF = 768
QKV = 1024
ATT = 1792
WIDE = 1920
NORM_EPSILON = 1e-06
ROPE_BASE = 1000000.0
MESH = pl.DeviceIdType.MESH
BF = jnp.bfloat16
F32 = jnp.float32
ANY = pl.BlockSpec(memory_space=pl.ANY)
VMEM = pl.BlockSpec(memory_space=pltpu.VMEM)
MIB = 1 << 20


def place():
    d = lax.axis_index("dp")
    t = lax.axis_index("tensor")
    c = lax.rem(d, 2)
    z = lax.rem(lax.div(d, 2), 4)
    x = lax.rem(lax.div(d, 8), 4)
    yh = lax.div(d, 32)
    return yh, x, z, c, t


def device(yh, x, z, c, t):
    return (((yh * 4 + x) * 4 + z) * 2 + c, t)


def up4(v, k):
    return lax.rem(v + k, 4)


def up2(v, k):
    return lax.rem(v + k, 2)


class Links:
    def __init__(self, send_sems, local_sems):
        self.me = place()
        self.send_sems, self.local_sems = send_sems, local_sems
        self.sent, self.local = [], []

    def at(self, dy=0, dx=0, dz=0, dc=0):
        yh, x, z, c, t = self.me
        y = up4(yh * 2 + t, dy)
        return device(lax.div(y, 2), up4(x, dx), up4(z, dz), up2(c, dc), lax.rem(y, 2))

    def flip(self, dyh=0, dt=0, dc=0):
        yh, x, z, c, t = self.me
        return device(up2(yh, dyh), x, z, up2(c, dc), up2(t, dt))

    def barrier(self, partners):
        sem = pltpu.get_barrier_semaphore()
        for partner in partners:
            pl.semaphore_signal(sem, inc=1, device_id=partner, device_id_type=MESH)
        pl.semaphore_wait(sem, len(partners))

    def send(self, src, dst, recv_sem, target):
        copy = pltpu.make_async_remote_copy(
            src_ref=src,
            dst_ref=dst,
            send_sem=self.send_sems.at[len(self.sent)],
            recv_sem=recv_sem,
            device_id=target,
            device_id_type=MESH,
        )
        copy.start()
        self.sent.append(copy)
        return copy

    def keep(self, src, dst):
        copy = pltpu.make_async_copy(src, dst, self.local_sems.at[len(self.local)])
        copy.start()
        self.local.append(copy)
        return copy

    def finish(self):
        for copy in self.sent:
            copy.wait_send()


ALONG = [dict(dx=k) for k in (1, 2, 3)] + [dict(dz=k) for k in (1, 2, 3)]
RING = [dict(dy=k) for k in (1, 2, 3)]


def plane_gather(links, block, own_block, sems, arrived):
    _, x, z, _, _ = links.me
    pending = {}

    def hop(h, da, db, src, dst, k, second):
        along_x = (h == 0) != second
        target = links.at(dx=k) if along_x else links.at(dz=k)
        key = (h, da, (4 - k) % 4) if second else (h, (4 - k) % 4, 0)
        pending[key] = links.send(src, dst, sems.at[(key[0] * 4 + key[1]) * 4 + key[2]], target)

    def spot(h, da, db):
        return block(h, up4(x, da), up4(z, db)) if h == 0 else block(h, up4(x, db), up4(z, da))

    for k in (1, 3, 2):
        for h in (0, 1):
            hop(h, 0, 0, own_block(h), spot(h, 0, 0), k, False)
    for k in (1, 3, 2):
        for h in (0, 1):
            hop(h, 0, 0, own_block(h), spot(h, 0, 0), k, True)
    for da in (1, 3, 2):
        for h in (0, 1):
            pending[(h, da, 0)].wait_recv()
            for k in (1, 3, 2):
                hop(h, da, 0, spot(h, da, 0), spot(h, da, 0), k, True)
            arrived(h, spot(h, da, 0), da, 0)
    for da in (0, 1, 3, 2):
        for db in (1, 3, 2):
            for h in (0, 1):
                pending[(h, da, db)].wait_recv()
                arrived(h, spot(h, da, db), da, db)


def gather_attention_kernel(
    a, e, tok, cot, a_all, e_mine, tok_pair, cot_all,
    send_sems, local_sems, ring_sems, plane_sems, twin_sems, expert_sems, token_sems, cot_sems, cot_twin_sems,
):
    links = Links(send_sems, local_sems)
    yh, x, z, c, t = links.me
    y = yh * 2 + t
    cross = [dict(dy=k, dc=1) for k in (1, 2, 3)]
    links.barrier([links.at(**w) for w in ALONG + RING + cross + [dict(dc=1)]])

    ring = {}
    here = a_all.at[t, yh, x, z, c]
    for k in (1, 3, 2):
        ring[(4 - k) % 4] = links.send(a, here, ring_sems.at[(4 - k) % 4], links.at(dy=k))
    kept = [links.keep(a, here)]

    experts = []
    columns = pl.ds(pl.multiple_of(t * 384, 384), 384)
    slot = e_mine.at[:, yh, c, :, columns]
    for dy in range(4):
        for dc in range(2):
            src = e.at[up4(y, dy) * 2 + up2(c, dc)]
            if dy == 0 and dc == 0:
                kept.append(links.keep(src, slot))
            else:
                index = ((4 - dy) % 4) * 2 + dc
                experts.append(links.send(src, slot, expert_sems.at[index], links.at(dy=dy, dc=dc)))
    partner = links.flip(dt=1)
    kept.append(links.keep(tok, tok_pair.at[t]))
    token = links.send(tok, tok_pair.at[t], token_sems.at[0], partner)
    cots = {}
    for k in (1, 3, 2):
        cots[(4 - k) % 4] = links.send(cot, cot_all.at[y, c], cot_sems.at[(4 - k) % 4], links.at(dy=k))
    kept.append(links.keep(cot, cot_all.at[y, c]))
    twin = links.at(dc=1)
    twins = [links.send(cot, cot_all.at[y, c], cot_twin_sems.at[0], twin)]

    for copy in kept[:1]:
        copy.wait()
    for k in (1, 3, 2):
        ring[k].wait_recv()
    twins.append(links.send(a_all.at[:, :, x, z, c], a_all.at[:, :, x, z, c], twin_sems.at[0], twin))

    def arrived(h, ref, da, db):
        twins.append(links.send(ref, ref, twin_sems.at[(h * 4 + da) * 4 + db + 1], twin))

    def block(h, xo, zo):
        return a_all.at[h, :, xo, zo, c]

    plane_gather(links, block, lambda h: block(h, x, z), plane_sems, arrived)
    for k in (1, 3, 2):
        cots[k].wait_recv()
        ref = cot_all.at[up4(y, k), c]
        twins.append(links.send(ref, ref, cot_twin_sems.at[k], twin))
    token.wait_recv()
    for copy in experts:
        copy.wait_recv()
    for copy in twins:
        copy.wait_recv()
    for copy in kept[1:]:
        copy.wait()
    links.finish()


def gather_attention(a, e, tok, cot):
    return pl.pallas_call(
        gather_attention_kernel,
        out_shape=(
            jax.ShapeDtypeStruct((2, 2, 4, 4, 2, 24, WIDE), BF),
            jax.ShapeDtypeStruct((3, 2, 2, 24, 768), BF),
            jax.ShapeDtypeStruct((2, OWN, D), BF),
            jax.ShapeDtypeStruct((4, 2, OWN, D), BF),
        ),
        in_specs=[ANY] * 4,
        out_specs=(ANY,) * 4,
        scratch_shapes=[pltpu.SemaphoreType.DMA((n,)) for n in (96, 8, 4, 32, 33, 8, 1, 4, 4)],
        compiler_params=pltpu.CompilerParams(collective_id=1, has_side_effects=True),
        name="gather_attention",
    )(a, e, tok, cot)


def gather_experts_kernel(
    e_mine, tok, gates, e_all, tok_all, gates_all,
    send_sems, local_sems, plane_sems, token_sems, token_twin_sems, gate_sems, gate_twin_sems,
):
    links = Links(send_sems, local_sems)
    yh, x, z, c, t = links.me
    y = yh * 2 + t
    links.barrier([links.at(**w) for w in ALONG + RING + [dict(dc=1)]])
    twin = links.at(dc=1)
    tokens, gate = {}, {}
    for k in (1, 3, 2):
        j = (4 - k) % 4
        gate[j] = links.send(gates, gates_all.at[y, c], gate_sems.at[j], links.at(dy=k))
        tokens[j] = links.send(tok, tok_all.at[y, c], token_sems.at[j], links.at(dy=k))
    twins = [
        links.send(gates, gates_all.at[y, c], gate_twin_sems.at[0], twin),
        links.send(tok, tok_all.at[y, c], token_twin_sems.at[0], twin),
    ]
    kept = [links.keep(tok, tok_all.at[y, c]), links.keep(gates, gates_all.at[y, c])]
    kept.append(links.keep(e_mine, e_all.at[:, :, x, z]))

    def block(h, xo, zo):
        return e_all.at[:, h, xo, zo]

    plane_gather(links, block, lambda h: e_mine.at[:, h], plane_sems, lambda h, ref, da, db: None)
    for k in (1, 3, 2):
        gate[k].wait_recv()
        ref = gates_all.at[up4(y, k), c]
        twins.append(links.send(ref, ref, gate_twin_sems.at[k], twin))
        tokens[k].wait_recv()
        ref = tok_all.at[up4(y, k), c]
        twins.append(links.send(ref, ref, token_twin_sems.at[k], twin))
    for copy in twins:
        copy.wait_recv()
    for copy in kept:
        copy.wait()
    links.finish()


def gather_experts(e_mine, tok, gates):
    return pl.pallas_call(
        gather_experts_kernel,
        out_shape=(
            jax.ShapeDtypeStruct((3, 2, 4, 4, 2, 24, 768), BF),
            jax.ShapeDtypeStruct((4, 2, OWN, D), BF),
            jax.ShapeDtypeStruct((4, 2, 8, OWN), F32),
        ),
        in_specs=[ANY] * 3,
        out_specs=(ANY,) * 3,
        scratch_shapes=[pltpu.SemaphoreType.DMA((n,)) for n in (48, 4, 32, 4, 4, 4, 4)],
        compiler_params=pltpu.CompilerParams(collective_id=2, has_side_effects=True),
        name="gather_experts",
    )(e_mine, tok, gates)


class TokenSum:
    SCRATCH = [
        pltpu.VMEM((4, OWN, D), BF),
        pltpu.VMEM((4, OWN, D), BF),
        pltpu.VMEM((3, OWN, D), BF),
        pltpu.SemaphoreType.DMA((4,)),
        pltpu.SemaphoreType.DMA((4,)),
    ]

    def __init__(self, links, src, own, twin, ring, twin_sems, ring_sems):
        self.links, self.own, self.twin, self.ring, self.ring_sems = links, own, twin, ring, ring_sems
        yh, _, _, c, t = links.me
        y = yh * 2 + t
        self.order = (2, 1, 3, 0)
        self.twins, self.kept = {}, {}
        for k in self.order:
            self.twins[k] = links.send(src.at[up4(y, k), 1 - c], twin.at[k], twin_sems.at[k], links.at(dc=1))
            self.kept[k] = links.keep(src.at[up4(y, k), c], own.at[k])

    def spread(self):
        self.sent = {}
        for k in self.order:
            self.kept[k].wait()
            self.twins[k].wait_recv()

            def add(i, carry):
                rows = pl.ds(pl.multiple_of(i * 64, 64), 64)
                self.own[k, rows, :] = (self.own[k, rows, :].astype(F32) + self.twin[k, rows, :].astype(F32)).astype(BF)
                return carry

            lax.fori_loop(0, OWN // 64, add, 0)
            if k:
                j = (4 - k) % 4
                self.sent[j] = self.links.send(
                    self.own.at[k], self.ring.at[j - 1], self.ring_sems.at[j], self.links.at(dy=k)
                )

    def total(self, out):
        for j in (1, 3, 2):
            self.sent[j].wait_recv()

        def add(i, carry):
            rows = pl.ds(pl.multiple_of(i * 64, 64), 64)
            part = self.own[0, rows, :].astype(F32)
            for j in range(3):
                part = part + self.ring[j, rows, :].astype(F32)
            out[rows, :] = part
            return carry

        lax.fori_loop(0, OWN // 64, add, 0)


def add_blocks(refs, out, count):
    def body(i, carry):
        part = refs[0][i].astype(F32)
        for ref in refs[1:]:
            part = part + ref[i].astype(F32)
        out[i] = part.astype(out.dtype)
        return carry

    lax.fori_loop(0, count, body, 0)


def reduce_experts_kernel(
    g, gx, ge, gx_out,
    own, first, mid, second, last,
    tok_own, tok_twin, tok_ring, tok_twin_sems, tok_ring_sems,
    send_sems, local_sems, first_sems, second_sems, expert_sems,
):
    links = Links(send_sems, local_sems)
    yh, x, z, c, t = links.me
    y = yh * 2 + t
    cross = [dict(dy=k, dc=1) for k in (1, 2, 3)]
    links.barrier([links.at(**w) for w in ALONG + RING + cross + [dict(dc=1)]])
    tokens = TokenSum(links, gx, tok_own, tok_twin, tok_ring, tok_twin_sems, tok_ring_sems)

    arrive = {}
    for k in (2, 1, 3):
        j = (4 - k) % 4
        arrive[(0, j)] = links.send(
            g.at[:, 0, :, up4(z, k)], first.at[0, j - 1], first_sems.at[j - 1], links.at(dz=k)
        )
        arrive[(1, j)] = links.send(
            g.at[:, 1, up4(x, k)], first.at[1, j - 1], first_sems.at[3 + j - 1], links.at(dx=k)
        )
    kept = [links.keep(g.at[:, 0, :, z], own.at[0]), links.keep(g.at[:, 1, x], own.at[1])]
    tokens.spread()
    for copy in kept:
        copy.wait()
    for j in (1, 3, 2):
        for h in (0, 1):
            arrive[(h, j)].wait_recv()
    final = {}
    for k in (2, 1, 3, 0):
        for h in (0, 1):
            place_of = up4(x, k) if h == 0 else up4(z, k)

            def body(i, carry):
                part = own[h, i, place_of].astype(F32)
                for j in range(3):
                    part = part + first[h, j, i, place_of].astype(F32)
                mid[h, k, i] = part.astype(BF)
                return carry

            lax.fori_loop(0, 3, body, 0)
            if k:
                j = (4 - k) % 4
                target = links.at(dx=k) if h == 0 else links.at(dz=k)
                final[(h, j)] = links.send(
                    mid.at[h, k], second.at[h, j - 1], second_sems.at[h * 3 + j - 1], target
                )
    tokens.total(gx_out)
    for h in (0, 1):
        for j in (1, 3, 2):
            final[(h, j)].wait_recv()
        add_blocks([mid.at[h, 0], second.at[h, 0], second.at[h, 1], second.at[h, 2]], last.at[h], 3)
    back, slot = [], y * 2 + c
    for dyh in range(2):
        for dt in range(2):
            for dc in range(2):
                columns = pl.ds(pl.multiple_of(up2(t, dt) * 384, 384), 384)
                src = last.at[up2(yh, dyh), :, up2(c, dc), :, columns]
                if dyh + dt + dc == 0:
                    stay = links.keep(src, ge.at[slot])
                else:
                    index = (dyh * 2 + dt) * 2 + dc
                    back.append(
                        links.send(src, ge.at[slot], expert_sems.at[index], links.flip(dyh=dyh, dt=dt, dc=dc))
                    )
    for copy in back:
        copy.wait_recv()
    stay.wait()
    links.finish()


def reduce_experts(g, gx):
    return pl.pallas_call(
        reduce_experts_kernel,
        out_shape=(
            jax.ShapeDtypeStruct((8, 3, 24, 384), BF),
            jax.ShapeDtypeStruct((OWN, D), F32),
        ),
        in_specs=[ANY] * 2,
        out_specs=(ANY, VMEM),
        scratch_shapes=[
            pltpu.VMEM((2, 3, 4, 2, 24, 768), BF),
            pltpu.VMEM((2, 3, 3, 4, 2, 24, 768), BF),
            pltpu.VMEM((2, 4, 3, 2, 24, 768), BF),
            pltpu.VMEM((2, 3, 3, 2, 24, 768), BF),
            pltpu.VMEM((2, 3, 2, 24, 768), BF),
        ]
        + TokenSum.SCRATCH
        + [pltpu.SemaphoreType.DMA((n,)) for n in (32, 8, 6, 6, 8)],
        compiler_params=pltpu.CompilerParams(
            collective_id=3, has_side_effects=True, vmem_limit_bytes=48 * MIB
        ),
        name="reduce_experts",
    )(g, gx)


def reduce_attention_kernel(
    g, mix, small, g_out, mix_out, small_out,
    own, twin, first, mid, second, last, ring,
    s_twin, s_one, s_first, s_two, s_second, s_three, s_ring,
    tok_own, tok_twin, tok_ring, tok_twin_sems, tok_ring_sems,
    send_sems, local_sems, twin_sems, first_sems, second_sems, ring_sems, small_sems,
):
    links = Links(send_sems, local_sems)
    yh, x, z, c, t = links.me
    links.barrier([links.at(**w) for w in ALONG + RING + [dict(dc=1)]])
    other = links.at(dc=1)
    order = (2, 1, 3, 0)

    def piece(h, k, core):
        return g.at[0, :, :, up4(z, k), core] if h == 0 else g.at[1, :, up4(x, k), :, core]

    s_copy = links.send(small, s_twin, small_sems.at[0], other)
    twins, kept = {}, {}
    for k in order:
        for h in (0, 1):
            twins[(h, k)] = links.send(piece(h, k, 1 - c), twin.at[h, k], twin_sems.at[h * 4 + k], other)
            kept[(h, k)] = links.keep(piece(h, k, c), own.at[h, k])
    tokens = TokenSum(links, mix, tok_own, tok_twin, tok_ring, tok_twin_sems, tok_ring_sems)
    s_copy.wait_recv()
    s_one[...] = small[...] + s_twin[...]
    s_copies = {}
    for k in (1, 2, 3):
        j = (4 - k) % 4
        s_copies[j] = links.send(s_one.at[:, up4(z, k)], s_first.at[j - 1], small_sems.at[j], links.at(dz=k))
    arrive = {}
    for k in order:
        for h in (0, 1):
            kept[(h, k)].wait()
            twins[(h, k)].wait_recv()
            for i in range(2):
                add_blocks([own.at[h, k, i], twin.at[h, k, i]], own.at[h, k, i], 4)
            if k:
                j = (4 - k) % 4
                target = links.at(dz=k) if h == 0 else links.at(dx=k)
                arrive[(h, j)] = links.send(
                    own.at[h, k], first.at[h, j - 1], first_sems.at[h * 3 + j - 1], target
                )
    tokens.spread()
    for j in (1, 2, 3):
        s_copies[j].wait_recv()
    s_two[...] = s_one[:, z] + s_first[0] + s_first[1] + s_first[2]
    for k in (1, 2, 3):
        j = (4 - k) % 4
        s_copies[j] = links.send(s_two.at[up4(x, k)], s_second.at[j - 1], small_sems.at[3 + j], links.at(dx=k))
    for j in (1, 3, 2):
        for h in (0, 1):
            arrive[(h, j)].wait_recv()
    final = {}
    for k in order:
        for h in (0, 1):
            place_of = up4(x, k) if h == 0 else up4(z, k)

            def body(i, carry):
                part = own[h, 0, i, place_of].astype(F32)
                for j in range(3):
                    part = part + first[h, j, i, place_of].astype(F32)
                mid[h, k, i] = part.astype(BF)
                return carry

            lax.fori_loop(0, 2, body, 0)
            if k:
                j = (4 - k) % 4
                target = links.at(dx=k) if h == 0 else links.at(dz=k)
                final[(h, j)] = links.send(
                    mid.at[h, k], second.at[h, j - 1], second_sems.at[h * 3 + j - 1], target
                )
    for j in (1, 2, 3):
        s_copies[j].wait_recv()
    s_three[...] = s_two[x] + s_second[0] + s_second[1] + s_second[2]
    for k in (1, 2, 3):
        j = (4 - k) % 4
        s_copies[j] = links.send(s_three, s_ring.at[j - 1], small_sems.at[6 + j], links.at(dy=k))
    tokens.total(mix_out)
    for h in (0, 1):
        for j in (1, 3, 2):
            final[(h, j)].wait_recv()
        add_blocks([mid.at[h, 0], second.at[h, 0], second.at[h, 1], second.at[h, 2]], last.at[h], 2)
    around = []
    for dyh, dt in ((1, 0), (0, 1), (1, 1)):
        index = dyh * 2 + dt - 1
        around.append(
            links.send(
                last.at[up2(t, dt), up2(yh, dyh)], ring.at[index], ring_sems.at[index], links.flip(dyh=dyh, dt=dt)
            )
        )
    for j in (1, 2, 3):
        s_copies[j].wait_recv()
    small_out[...] = s_three[...] + s_ring[0] + s_ring[1] + s_ring[2]
    for copy in around:
        copy.wait_recv()
    total = last[t, yh].astype(F32)
    for j in range(3):
        total = total + ring[j].astype(F32)
    g_out[...] = total
    links.finish()


def reduce_attention(g, mix, small):
    return pl.pallas_call(
        reduce_attention_kernel,
        out_shape=(
            jax.ShapeDtypeStruct((24, ATT), F32),
            jax.ShapeDtypeStruct((OWN, D), F32),
            jax.ShapeDtypeStruct((8, 128), F32),
        ),
        in_specs=[ANY, ANY, VMEM],
        out_specs=(VMEM, VMEM, VMEM),
        scratch_shapes=[
            pltpu.VMEM((2, 4, 2, 4, 24, ATT), BF),
            pltpu.VMEM((2, 4, 2, 4, 24, ATT), BF),
            pltpu.VMEM((2, 3, 2, 4, 24, ATT), BF),
            pltpu.VMEM((2, 4, 2, 24, ATT), BF),
            pltpu.VMEM((2, 3, 2, 24, ATT), BF),
            pltpu.VMEM((2, 2, 24, ATT), BF),
            pltpu.VMEM((3, 24, ATT), BF),
            pltpu.VMEM((4, 4, 8, 128), F32),
            pltpu.VMEM((4, 4, 8, 128), F32),
            pltpu.VMEM((3, 4, 8, 128), F32),
            pltpu.VMEM((4, 8, 128), F32),
            pltpu.VMEM((3, 8, 128), F32),
            pltpu.VMEM((8, 128), F32),
            pltpu.VMEM((3, 8, 128), F32),
        ]
        + TokenSum.SCRATCH
        + [pltpu.SemaphoreType.DMA((n,)) for n in (48, 16, 8, 6, 6, 3, 10)],
        compiler_params=pltpu.CompilerParams(
            collective_id=4, has_side_effects=True, vmem_limit_bytes=56 * MIB
        ),
        name="reduce_attention",
    )(g, mix, small)


def rope_tables(first, length, head_size):
    half_size = head_size // 2
    frequency = ROPE_BASE ** (-(2.0 * jnp.arange(half_size, dtype=F32)) / head_size)
    position = (first + jnp.arange(length)).astype(F32)
    angles = position[:, None] * frequency[None, :]
    angles = jnp.concatenate([angles, angles], axis=1)
    return (jnp.cos(angles), jnp.sin(angles))


def rotate(values, cosine, sine_table):
    half_size = values.shape[-1] // 2
    turned = jnp.concatenate([-values[..., half_size:], values[..., :half_size]], axis=-1)
    return values * cosine[:, None, :] + turned * sine_table[:, None, :]


def unrotate(gradient, cosine, sine_table):
    half_size = gradient.shape[-1] // 2
    carried = gradient * sine_table[:, None, :]
    turned = jnp.concatenate([-carried[..., half_size:], carried[..., :half_size]], axis=-1)
    return gradient * cosine[:, None, :] - turned


def norm_forward(tokens, gain_vec):
    inverse = lax.rsqrt(jnp.mean(tokens * tokens, axis=1, keepdims=True) + NORM_EPSILON)
    return (tokens * inverse * gain_vec, inverse)


def norm_backward(tokens, inverse, gain_vec, gradient):
    scaled = gradient * gain_vec
    gain_grad = jnp.sum(gradient * tokens * inverse, axis=0)
    token_grad = inverse * scaled - tokens * inverse**3 * jnp.mean(
        scaled * tokens, axis=1, keepdims=True
    )
    return (token_grad, gain_grad)


def mm(a, b, dims):
    return lax.dot_general(a, b, (dims, ((), ())), preferred_element_type=F32)


def shards(
    tokens_in, routes, cotangent, attn_gain, query_proj, key_proj, value_proj, output_proj,
    ffn_gain, router_proj, expert_gate, expert_up, expert_down,
):
    yh, x, z, c, t = place()
    extra = jnp.concatenate(
        [router_proj, attn_gain[:, None], ffn_gain[:, None], jnp.zeros((24, WIDE - ATT - 10), BF)], axis=1
    )
    a_block = jnp.concatenate([query_proj, key_proj, value_proj, output_proj, extra], axis=1)
    e_block = jnp.stack([expert_gate, expert_up, expert_down]).transpose(2, 0, 1, 3)
    a_all, e_mine, tok_pair, cot_all = gather_attention(a_block, e_block, tokens_in, cotangent)

    weights = a_all.reshape(2, D, WIDE)
    router = weights[0, :, ATT : ATT + 8]
    gain_attn = weights[0, :, ATT + 8].astype(F32)
    gain_ffn = weights[0, :, ATT + 9].astype(F32)
    inputs = tokens_in.astype(F32)
    normed_own, inverse_attn = norm_forward(inputs, gain_attn)
    normed_own = normed_own.astype(BF)
    normed_pair = norm_forward(tok_pair.reshape(SEQ, D).astype(F32), gain_attn)[0].astype(BF)
    cos_own, sin_own = rope_tables(OWN * t, OWN, HD)
    cos_all, sin_all = rope_tables(0, SEQ, HD)
    allowed = (OWN * t + jnp.arange(OWN))[:, None] >= jnp.arange(SEQ)[None, :]
    scale = HD ** (-0.5)
    queries, keys, values, logs, attended = [], [], [], [], []
    branch = 0.0
    for j in range(2):
        w = weights[j]
        q = mm(normed_own, w[:, :HALF], ((1,), (0,))).reshape(OWN, 6, HD)
        k = mm(normed_pair, w[:, HALF : HALF + HD], ((1,), (0,))).reshape(SEQ, 1, HD)
        v = mm(normed_pair, w[:, HALF + HD : QKV], ((1,), (0,))).astype(BF)
        q = rotate(q, cos_own, sin_own).astype(BF)
        k = rotate(k, cos_all, sin_all).astype(BF).reshape(SEQ, HD)
        scores = jnp.einsum("qgd,sd->gqs", q, k, preferred_element_type=F32) * scale
        scores = jnp.where(allowed[None], scores, -1e30)
        row_max = jnp.max(scores, axis=-1, keepdims=True)
        shifted = jnp.exp(scores - row_max)
        row_total = jnp.sum(shifted, axis=-1, keepdims=True)
        probs = (shifted / row_total).astype(BF)
        att = jnp.einsum("gqs,sd->qgd", probs, v, preferred_element_type=F32).astype(BF).reshape(OWN, HALF)
        branch = branch + mm(att, w[:, QKV:ATT], ((1,), (1,)))
        queries.append(q)
        keys.append(k)
        values.append(v)
        logs.append(row_max + jnp.log(row_total))
        attended.append(att)
    residual = inputs + branch
    normed_ffn, inverse_ffn = norm_forward(residual, gain_ffn)
    normed_ffn = normed_ffn.astype(BF)
    logits = mm(normed_ffn, router, ((1,), (0,)))
    own_routes = lax.dynamic_slice(routes, (OWN * t, 0), (OWN, 4))
    chosen = jnp.any(own_routes[:, :, None] == jnp.arange(E)[None, None, :], axis=1)
    masked = jnp.where(chosen, logits, -1e30)
    raised = jnp.where(chosen, jnp.exp(masked - jnp.max(masked, axis=1, keepdims=True)), 0.0)
    gates_own = raised / jnp.sum(raised, axis=1, keepdims=True)
    e_all, tok_all, gates_all = gather_experts(e_mine, normed_ffn, gates_own.T)

    rows = 8 * OWN
    experts = e_all.reshape(3, D, 768)
    tokens = tok_all.reshape(rows, D)
    cots = cot_all.reshape(rows, D)
    gates = gates_all.transpose(0, 1, 3, 2).reshape(rows, E)
    mine = (jnp.arange(E) == (yh * 2 + t) * 2 + c).astype(F32)
    gate = jnp.sum(gates * mine[None, :], axis=1, keepdims=True)
    gate_in = mm(tokens, experts[0], ((1,), (0,)))
    up_in = mm(tokens, experts[1], ((1,), (0,)))
    back = mm(cots, experts[2], ((1,), (0,)))
    sig = jax.nn.sigmoid(gate_in)
    act = gate_in * sig
    hidden = act * up_in
    grad_gate = jnp.sum(hidden * back, axis=1, keepdims=True)
    grad_logits = (gate * grad_gate * (mine[None, :] - gates)).astype(BF)
    weighted = (gate * hidden).astype(BF)
    grad_hidden = gate * back
    grad_gate_in = (grad_hidden * up_in * sig * (1.0 + gate_in * (1.0 - sig))).astype(BF)
    grad_up_in = (grad_hidden * act).astype(BF)
    mixture = mm(weighted, experts[2], ((1,), (1,))).astype(BF)
    grad_tokens = (
        mm(grad_gate_in, experts[0], ((1,), (1,)))
        + mm(grad_up_in, experts[1], ((1,), (1,)))
        + mm(grad_logits, router, ((1,), (1,)))
    ).astype(BF)
    grad_experts = jnp.stack(
        [
            mm(tokens, grad_gate_in, ((0,), (0,))).astype(BF),
            mm(tokens, grad_up_in, ((0,), (0,))).astype(BF),
            mm(cots, weighted, ((0,), (0,))).astype(BF),
        ]
    )
    grad_router = mm(tokens, grad_logits, ((0,), (0,)))
    ge, grad_normed_ffn = reduce_experts(
        grad_experts.reshape(3, 2, 4, 4, 2, 24, 768), grad_tokens.reshape(4, 2, OWN, D)
    )
    ge = ge.astype(F32).transpose(1, 2, 0, 3)

    grad_norm, grad_gain_ffn = norm_backward(residual, inverse_ffn, gain_ffn, grad_normed_ffn)
    grad_residual = cotangent.astype(F32) + grad_norm
    grad_branch = grad_residual.astype(BF)
    grad_q, grad_k, grad_v, grad_o = [], [], [], []
    for j in range(2):
        w = weights[j]
        q, k, v = queries[j], keys[j], values[j]
        grad_att = mm(grad_branch, w[:, QKV:ATT], ((1,), (0,))).astype(BF).reshape(OWN, 6, HD)
        scores = jnp.einsum("qgd,sd->gqs", q, k, preferred_element_type=F32) * scale
        scores = jnp.where(allowed[None], scores, -1e30)
        exact = jnp.exp(scores - logs[j])
        probs = exact.astype(BF)
        grad_probs = jnp.einsum("qgd,sd->gqs", grad_att, v, preferred_element_type=F32)
        centred = jnp.sum(exact * grad_probs, axis=-1, keepdims=True)
        grad_scores = (exact * (grad_probs - centred)).astype(BF)
        grad_q.append(jnp.einsum("gqs,sd->qgd", grad_scores, k, preferred_element_type=F32) * scale)
        grad_k.append(jnp.einsum("gqs,qgd->sd", grad_scores, q, preferred_element_type=F32) * scale)
        grad_v.append(jnp.einsum("gqs,qgd->sd", probs, grad_att, preferred_element_type=F32))
        grad_o.append(mm(grad_branch, attended[j], ((0,), (0,))).astype(BF))
    grad_kv = jnp.concatenate([grad_k[0], grad_k[1], grad_v[0], grad_v[1]], axis=1)
    theirs = lax.dynamic_slice(grad_kv, (OWN * (1 - t), 0), (OWN, 4 * HD)).astype(BF)
    received = lax.ppermute(theirs, "tensor", [(0, 1), (1, 0)])
    grad_kv = lax.dynamic_slice(grad_kv, (OWN * t, 0), (OWN, 4 * HD)) + received.astype(F32)
    grad_normed = 0.0
    grad_a = []
    for j in range(2):
        w = weights[j]
        gq = unrotate(grad_q[j], cos_own, sin_own).astype(BF).reshape(OWN, HALF)
        gk = unrotate(grad_kv[:, HD * j : HD * (j + 1)].reshape(OWN, 1, HD), cos_own, sin_own)
        gk = gk.astype(BF).reshape(OWN, HD)
        gv = grad_kv[:, HD * (2 + j) : HD * (3 + j)].astype(BF)
        lin = jnp.concatenate([gq, gk, gv], axis=1)
        grad_normed = grad_normed + mm(lin, w[:, :QKV], ((1,), (1,)))
        grad_a.append(jnp.concatenate([mm(normed_own, lin, ((0,), (0,))).astype(BF), grad_o[j]], axis=1))
    grad_input_norm, grad_gain_attn = norm_backward(inputs, inverse_attn, gain_attn, grad_normed)
    grad_input = (grad_residual + grad_input_norm).astype(BF)

    small = jnp.concatenate([grad_router, grad_gain_attn[:, None], grad_gain_ffn[:, None]], axis=1)
    small = small.reshape(2, 4, 4, 2, 24, 10).transpose(1, 2, 0, 3, 4, 5).reshape(16, 960)
    small = jnp.pad(small, ((0, 0), (0, 64))).reshape(4, 4, 8, 128)
    ga, mix, small = reduce_attention(
        jnp.stack(grad_a).reshape(2, 2, 4, 4, 2, 24, ATT), mixture.reshape(4, 2, OWN, D), small
    )
    layer_output = (residual + mix).astype(BF)
    small = small.reshape(1024)[:960].reshape(2, 2, 2, 12, 10)
    small = lax.dynamic_slice(small, (yh, c, t, 0, 0), (1, 1, 1, 12, 10)).reshape(12, 10)
    return (
        layer_output,
        grad_input,
        small[:, 8],
        ga[:, :HALF],
        ga[:, HALF : HALF + HD],
        ga[:, HALF + HD : QKV],
        ga[:, QKV:],
        small[:, 9],
        small[:, :8],
        ge[0],
        ge[1],
        ge[2],
    )


def solution(mesh):
    return jax.shard_map(
        shards,
        mesh=mesh,
        in_specs=(
            P(("dp", "tensor"), None),
            P("dp", None),
            P(("dp", "tensor"), None),
            P("dp"),
            P("dp", "tensor"),
            P("dp", "tensor"),
            P("dp", "tensor"),
            P("dp", "tensor"),
            P("dp"),
            P("dp", None),
            P("dp", None, "tensor"),
            P("dp", None, "tensor"),
            P("dp", None, "tensor"),
        ),
        out_specs=(
            P(("dp", "tensor"), None),
            P(("dp", "tensor"), None),
            P(("dp", "tensor")),
            P("dp", "tensor"),
            P("dp", "tensor"),
            P("dp", "tensor"),
            P("dp", "tensor"),
            P(("dp", "tensor")),
            P(("dp", "tensor"), None),
            P("dp", None, "tensor"),
            P("dp", None, "tensor"),
            P("dp", None, "tensor"),
        ),
        check_vma=False,
    )
```

```python
import functools

import jax
import jax.numpy as jnp
import numpy as np
from jax import lax
from jax.experimental import pallas as pl
from jax.experimental.pallas import tpu as pltpu
from jax.sharding import PartitionSpec as P

HD = 128
E = 8
D = 1536
SEQ = 512
OWN = 256
HALF = 768
PART = 896
WIDE = 1024
NORM_EPSILON = 1e-06
ROPE_BASE = 1000000.0
SCALE = HD ** (-0.5)
MESH = pl.DeviceIdType.MESH
BF = jnp.bfloat16
F32 = jnp.float32
ANY = pl.BlockSpec(memory_space=pl.ANY)
VMEM = pl.BlockSpec(memory_space=pltpu.VMEM)
MIB = 1 << 20


def place():
    d = lax.axis_index("dp")
    t = lax.axis_index("tensor")
    c = lax.rem(d, 2)
    z = lax.rem(lax.div(d, 2), 4)
    x = lax.rem(lax.div(d, 8), 4)
    yh = lax.div(d, 32)
    return yh, x, z, c, t


def device(yh, x, z, c, t):
    return (((yh * 4 + x) * 4 + z) * 2 + c, t)


def up4(v, k):
    return lax.rem(v + k, 4)


def up2(v, k):
    return lax.rem(v + k, 2)


def rows_of(b, size=OWN):
    return pl.ds(pl.multiple_of(b * size, size), size)


def nn(a, b):
    return jnp.dot(a, b, preferred_element_type=F32)


def nt(a, b):
    return lax.dot_general(a, b, (((1,), (1,)), ((), ())), preferred_element_type=F32)


def tn(a, b):
    return lax.dot_general(a, b, (((0,), (0,)), ((), ())), preferred_element_type=F32)


class Links:
    def __init__(self, send_sems, local_sems):
        self.me = place()
        self.send_sems, self.local_sems = send_sems, local_sems
        self.sent, self.local = [], []

    def at(self, dy=0, dx=0, dz=0, dc=0):
        yh, x, z, c, t = self.me
        y = up4(yh * 2 + t, dy)
        return device(lax.div(y, 2), up4(x, dx), up4(z, dz), up2(c, dc), lax.rem(y, 2))

    def flip(self, dyh=0, dt=0, dc=0):
        yh, x, z, c, t = self.me
        return device(up2(yh, dyh), x, z, up2(c, dc), up2(t, dt))

    def barrier(self, partners):
        sem = pltpu.get_barrier_semaphore()
        for partner in partners:
            pl.semaphore_signal(sem, inc=1, device_id=partner, device_id_type=MESH)
        pl.semaphore_wait(sem, len(partners))

    def send(self, src, dst, recv_sem, target):
        copy = pltpu.make_async_remote_copy(
            src_ref=src,
            dst_ref=dst,
            send_sem=self.send_sems.at[len(self.sent)],
            recv_sem=recv_sem,
            device_id=target,
            device_id_type=MESH,
        )
        copy.start()
        self.sent.append(copy)
        return copy

    def keep(self, src, dst):
        copy = pltpu.make_async_copy(src, dst, self.local_sems.at[len(self.local)])
        copy.start()
        self.local.append(copy)
        return copy

    def finish(self):
        for copy in self.sent:
            copy.wait_send()


ALONG = [dict(dx=k) for k in (1, 2, 3)] + [dict(dz=k) for k in (1, 2, 3)]
NEAR = [dict(dx=k) for k in (1, 3)] + [dict(dz=k) for k in (1, 3)]
RING = [dict(dy=k) for k in (1, 2, 3)]
CROSS = [dict(dy=k, dc=1) for k in (1, 2, 3)]
TWIN = [dict(dc=1)]


def plane_gather(links, whole, piece, own, sems, arrived):
    _, x, z, _, _ = links.me
    got = {}

    def spot(fn, h, da, db, *i):
        xo, zo = (up4(x, da), up4(z, db)) if h == 0 else (up4(x, db), up4(z, da))
        return fn(h, xo, zo, *i)

    def target(h, second, k):
        return links.at(dx=k) if (h == 0) != second else links.at(dz=k)

    def sem(h, da, db, i=0):
        return sems.at[((h * 4 + da) * 4 + db) * 2 + i]

    def push(h, da, second):
        dst = spot(whole, h, da, 0)
        src = own(h) if da == 0 else dst
        for k in (1, 3):
            key = (h, da, 4 - k) if second else (h, 4 - k, 0)
            got[key] = links.send(src, dst, sem(*key), target(h, second, k))

    def take(h, da, db, second):
        got[(h, da, db)].wait_recv()
        i, k = (0, 1) if (db if second else da) == 3 else (1, 3)
        key = (h, da, 2, i) if second else (h, 2, 0, i)
        ref = spot(piece, h, da, db, i)
        got[key] = links.send(ref, ref, sem(*key), target(h, second, k))

    def far(h, da, db):
        for i in (0, 1):
            got[(h, da, db, i)].wait_recv()

    for h in (0, 1):
        push(h, 0, False)
    for h in (0, 1):
        push(h, 0, True)
    yield
    for da in (3, 1):
        for h in (0, 1):
            take(h, da, 0, False)
            push(h, da, True)
            arrived(spot(whole, h, da, 0), h, da, 0)
        yield
    for db in (3, 1):
        for h in (0, 1):
            take(h, 0, db, True)
            arrived(spot(whole, h, 0, db), h, 0, db)
    yield
    for h in (0, 1):
        far(h, 2, 0)
        push(h, 2, True)
        arrived(spot(whole, h, 2, 0), h, 2, 0)
    yield
    for da in (3, 1, 2):
        for db in (3, 1):
            for h in (0, 1):
                take(h, da, db, True)
                arrived(spot(whole, h, da, db), h, da, db)
        yield
    for da in (0, 3, 1, 2):
        for h in (0, 1):
            far(h, da, 2)
            arrived(spot(whole, h, da, 2), h, da, 2)
        yield


def ring_gather(links, src, block, sems, arrived):
    got = {}

    def part(ref, i):
        return ref.at[pl.ds(128 * i, 128), :]

    for i in (0, 1):
        for k in (1, 3):
            half = i if k == 1 else 1 - i
            j = 4 - k
            got[(j, half)] = links.send(
                part(src, half), part(block(0), half), sems.at[j * 2 + half], links.at(dy=k)
            )
    yield
    for j, half, k in ((3, 0, 1), (1, 1, 3)):
        got[(j, half)].wait_recv()
        ref = part(block(j), half)
        got[(2, half)] = links.send(ref, ref, sems.at[4 + half], links.at(dy=k))
    yield
    for j, half in ((3, 1), (1, 0)):
        got[(j, half)].wait_recv()
        arrived(block(j), j)
    yield
    for half in (0, 1):
        got[(2, half)].wait_recv()
    arrived(block(2), 2)
    yield


def advance(steps, count=1):
    for _ in range(count):
        next(steps, None)


def drain(steps):
    for _ in steps:
        pass


def roped(u, cosine, sine):
    return u * cosine + pltpu.roll(u, 64, 1) * sine


def unroped(u, cosine, sine):
    return u * cosine - pltpu.roll(u, 64, 1) * sine


def causal_bias(t):
    row = lax.broadcasted_iota(jnp.int32, (OWN, SEQ), 0) + OWN * t
    column = lax.broadcasted_iota(jnp.int32, (OWN, SEQ), 1)
    return jnp.where(row >= column, 0.0, -1e30).astype(F32)


def inverse_norm(v):
    return lax.rsqrt(jnp.mean(v * v, axis=1, keepdims=True) + NORM_EPSILON)


def gain_rows(w):
    tables = [w[0, 0, i, :, PART:].astype(F32).T for i in (0, 1)]
    both = jnp.concatenate(tables, axis=1)
    return both[8:9, :], both[9:10, :]


def forward_kernel(
    a, e, tok, cot, chosen, cosine, sine,
    w_out, e_all, tok_all, cot_all, gates_all, normed_out, q_out, k_out, v_out, att_out, residual_out,
    w, a_pair, a_own, e_pair, e_own, pair, normed, tok_two, gates,
    send_sems, local_sems, a_sems, ring_sems, plane_sems, twin_sems, expert_sems, token_sems,
    cot_sems, cot_twin_sems, e_sems, x_sems, x_twin_sems, g_sems, g_twin_sems,
):
    links = Links(send_sems, local_sems)
    yh, x, z, c, t = links.me
    y = yh * 2 + t
    twin = links.at(dc=1)
    here = pl.ds(pl.multiple_of(192 * x + 48 * z, 48), 48)
    links.barrier([links.at(**p) for p in NEAR + RING + CROSS + TWIN])

    kept = [links.keep(a.at[c], a_pair.at[c])]
    a_copy = links.send(a.at[1 - c], a_pair.at[c], a_sems.at[0], twin)
    columns = pl.ds(pl.multiple_of(t * 384, 384), 384)
    slot = e_pair.at[:, yh, c, :, columns]
    kept[0].wait()
    a_copy.wait_recv()
    a_own[...] = jnp.concatenate([a_pair[0].astype(F32), a_pair[1].astype(F32)], axis=0).astype(BF)
    mine = w.at[t, c, yh, here, :]
    ring = {}
    for k in (1, 3, 2):
        ring[4 - k] = links.send(a_own, mine, ring_sems.at[4 - k], links.at(dy=k))
    w_kept = links.keep(a_own, mine)
    experts = []
    for dy in range(4):
        for dc in range(2):
            src = e.at[up4(y, dy) * 2 + up2(c, dc)]
            if dy + dc == 0:
                e_kept = links.keep(src, slot)
            else:
                index = ((4 - dy) % 4) * 2 + dc
                experts.append(links.send(src, slot, expert_sems.at[index], links.at(dy=dy, dc=dc)))
    kept = [links.keep(tok, pair.at[t]), links.keep(cot, cot_all.at[y * 2 + c])]
    token = links.send(tok, pair.at[t], token_sems.at[0], links.flip(dt=1))
    twins = []

    def cot_arrived(ref, j):
        twins.append(links.send(ref, ref, cot_twin_sems.at[j], twin))

    twins.append(links.send(cot, cot_all.at[y * 2 + c], cot_twin_sems.at[0], twin))
    cots = ring_gather(links, cot, lambda j: cot_all.at[up4(y, j) * 2 + c], cot_sems, cot_arrived)
    advance(cots)

    w_kept.wait()
    for j in (1, 3, 2):
        ring[j].wait_recv()
    w_twins = []

    def w_arrived(ref, h, da, db):
        w_twins.append(links.send(ref, ref, twin_sems.at[(h * 4 + da) * 4 + db], twin))

    def w_whole(h, xo, zo):
        return w.at[h, c, :, pl.ds(pl.multiple_of(192 * xo + 48 * zo, 48), 48), :]

    def w_piece(h, xo, zo, i):
        return w.at[h, c, i, pl.ds(pl.multiple_of(192 * xo + 48 * zo, 48), 48), :]

    weights = plane_gather(links, w_whole, w_piece, lambda h: w_whole(h, x, z), plane_sems, w_arrived)
    advance(weights)
    for h in (0, 1):
        w_arrived(w_whole(h, x, z), h, 0, 0)
    e_kept.wait()
    for copy in experts:
        copy.wait_recv()
    for n in range(3):
        for i in range(2):
            e_own[n, i] = jnp.concatenate(
                [e_pair[n, i, 0].astype(F32), e_pair[n, i, 1].astype(F32)], axis=0
            ).astype(BF)
    kept.append(links.keep(e_own, e_all.at[:, :, here, :]))

    def e_whole(h, xo, zo):
        return e_all.at[:, h, pl.ds(pl.multiple_of(192 * xo + 48 * zo, 48), 48), :]

    def e_piece(h, xo, zo, i):
        return e_all.at[:, h, pl.ds(pl.multiple_of(192 * xo + 48 * zo, 48), 48), pl.ds(384 * i, 384)]

    expert = plane_gather(
        links, e_whole, e_piece, lambda h: e_own.at[:, h], e_sems, lambda ref, h, da, db: None
    )
    advance(weights, 3)
    advance(cots)
    advance(weights, 4)
    advance(expert)
    drain(weights)
    advance(cots)
    token.wait_recv()
    for copy in kept[:2]:
        copy.wait()
    for copy in w_twins:
        copy.wait_recv()
    w_dump = links.keep(w, w_out)

    gain_one, gain_two = gain_rows(w)
    for i in (0, 1):
        v = pair[i].astype(F32)
        normed[pl.ds(OWN * i, OWN), :] = (v * inverse_norm(v) * gain_one).astype(BF)
    own = rows_of(t)
    normed_out[...] = normed[own, :]
    bias = causal_bias(t)
    cos_own, sin_own = cosine[own, :], sine[own, :]
    residual_out[...] = pair[t].astype(F32)
    for j in (0, 1):
        q = nn(normed_out[:, :HALF], w[j, 0, 0, :, :HALF]) + nn(normed_out[:, HALF:], w[j, 0, 1, :, :HALF])
        k = nn(normed[:, :HALF], w[j, 0, 0, :, HALF:PART]) + nn(normed[:, HALF:], w[j, 0, 1, :, HALF:PART])
        v = nn(normed[:, :HALF], w[j, 1, 0, :, :HD]) + nn(normed[:, HALF:], w[j, 1, 1, :, :HD])
        v = v.astype(BF)
        k = roped(k, cosine[...], sine[...]).astype(BF)
        k_out[j] = k
        v_out[j] = v
        for g in range(6):
            lanes = slice(HD * g, HD * (g + 1))
            qh = roped(q[:, lanes], cos_own, sin_own).astype(BF)
            q_out[j, :, lanes] = qh
            scores = nt(qh, k) * SCALE + bias
            raised = jnp.exp(scores - jnp.max(scores, axis=1, keepdims=True))
            probs = (raised * (1.0 / jnp.sum(raised, axis=1, keepdims=True))).astype(BF)
            att_out[j, :, lanes] = nn(probs, v).astype(BF)
            if g == 2 or g == 5:
                advance(expert)
        for i in (0, 1):
            columns = pl.ds(HALF * i, HALF)
            residual_out[:, columns] += nt(att_out[j], w[j, 1, i, :, HD:PART])
        if j == 0:
            advance(cots)
    residual = residual_out[...]
    tok_two[...] = (residual * inverse_norm(residual) * gain_two).astype(BF)
    block = tok_all.at[y * 2 + c]
    kept.append(links.keep(tok_two, block))

    def x_arrived(ref, j):
        twins.append(links.send(ref, ref, x_twin_sems.at[j], twin))

    tokens = ring_gather(links, tok_two, lambda j: tok_all.at[up4(y, j) * 2 + c], x_sems, x_arrived)
    advance(tokens)
    twins.append(links.send(tok_two, block, x_twin_sems.at[0], twin))
    logits = nn(tok_two[:, :HALF], w[0, 0, 0, :, PART:]) + nn(tok_two[:, HALF:], w[0, 0, 1, :, PART:])
    masked = jnp.where(chosen[...] > 0.5, logits, -1e30)
    raised = jnp.where(chosen[...] > 0.5, jnp.exp(masked - jnp.max(masked, axis=1, keepdims=True)), 0.0)
    table = raised * (1.0 / jnp.sum(raised, axis=1, keepdims=True))
    gates[...] = table.T[:8, :]
    kept.append(links.keep(gates, gates_all.at[y * 2 + c]))
    gate = {}
    for k in (1, 3, 2):
        gate[4 - k] = links.send(gates, gates_all.at[y * 2 + c], g_sems.at[4 - k], links.at(dy=k))
    twins.append(links.send(gates, gates_all.at[y * 2 + c], g_twin_sems.at[0], twin))
    advance(expert, 2)
    advance(tokens)
    drain(expert)
    drain(tokens)
    drain(cots)
    for j in (1, 3, 2):
        gate[j].wait_recv()
        ref = gates_all.at[up4(y, j) * 2 + c]
        twins.append(links.send(ref, ref, g_twin_sems.at[j], twin))
    for copy in twins:
        copy.wait_recv()
    for copy in kept[2:]:
        copy.wait()
    w_dump.wait()
    links.finish()


def forward(a, e, tok, cot, chosen, cosine, sine):
    dma = [pltpu.SemaphoreType.DMA((n,)) for n in (192, 12, 1, 4, 64, 32, 8, 1, 8, 4, 64, 8, 4, 4, 4)]
    return pl.pallas_call(
        forward_kernel,
        out_shape=(
            jax.ShapeDtypeStruct((2, 2, 2, HALF, WIDE), BF),
            jax.ShapeDtypeStruct((3, 2, HALF, HALF), BF),
            jax.ShapeDtypeStruct((8, OWN, D), BF),
            jax.ShapeDtypeStruct((8, OWN, D), BF),
            jax.ShapeDtypeStruct((8, 8, OWN), F32),
            jax.ShapeDtypeStruct((OWN, D), BF),
            jax.ShapeDtypeStruct((2, OWN, HALF), BF),
            jax.ShapeDtypeStruct((2, SEQ, HD), BF),
            jax.ShapeDtypeStruct((2, SEQ, HD), BF),
            jax.ShapeDtypeStruct((2, OWN, HALF), BF),
            jax.ShapeDtypeStruct((OWN, D), F32),
        ),
        in_specs=[ANY, ANY, ANY, ANY, VMEM, VMEM, VMEM],
        out_specs=(ANY,) * 5 + (VMEM,) * 6,
        scratch_shapes=[
            pltpu.VMEM((2, 2, 2, HALF, WIDE), BF),
            pltpu.VMEM((2, 24, WIDE), BF),
            pltpu.VMEM((48, WIDE), BF),
            pltpu.VMEM((3, 2, 2, 24, HALF), BF),
            pltpu.VMEM((3, 2, 48, HALF), BF),
            pltpu.VMEM((2, OWN, D), BF),
            pltpu.VMEM((SEQ, D), BF),
            pltpu.VMEM((OWN, D), BF),
            pltpu.VMEM((8, OWN), F32),
        ]
        + dma,
        compiler_params=pltpu.CompilerParams(
            collective_id=1, has_side_effects=True, vmem_limit_bytes=48 * MIB
        ),
        name="forward",
    )(a, e, tok, cot, chosen, cosine, sine)


def expert_kernel(
    w, x_all, c_all, gates, router, gx_out, mix_out, dw_out, router_out,
    xs, cs, hidden, d_gate, d_up, d_logit, own, theirs, twin, ring, staged, even, odd,
    send_sems, load_sems, mix_sems, dw_sems, twin_sems, ring_sems,
):
    links = Links(send_sems, None)
    yh, _, _, c, t = links.me
    y = yh * 2 + t
    loads = {}
    for i, k in enumerate((2, 1, 3, 0)):
        for core in (1, 0):
            b = up4(y, k) * 2 + up2(c, core)
            for n, (src, dst) in enumerate(((x_all, xs), (c_all, cs))):
                copy = pltpu.make_async_copy(src.at[b], dst.at[rows_of(b), :], load_sems.at[(k * 2 + core) * 2 + n])
                copy.start()
                loads[(k, core, n)] = copy
    links.barrier([links.at(**w_) for w_ in RING + [dict(dc=1)]])
    lane = lax.broadcasted_iota(jnp.int32, (OWN, 128), 1)
    mine = (lane == y * 2 + c).astype(F32)

    def inputs(b, f):
        rows = rows_of(b)
        xb = xs[rows, :]
        f[0] = nn(xb, w[0])
        f[1] = nn(xb, w[1])
        f[2] = nn(cs[rows, :], w[2])

    def middle(b, f):
        rows = rows_of(b)
        gate_in, up_in, back = f[0], f[1], f[2]
        table = jnp.concatenate([gates[b], jnp.zeros((120, OWN), F32)], axis=0).T
        gate = jnp.sum(table * mine, axis=1, keepdims=True)
        sig = jax.nn.sigmoid(gate_in)
        act = gate_in * sig
        hid = act * up_in
        grad_gate = jnp.sum(hid * back, axis=1, keepdims=True)
        grad_hidden = gate * back
        d_logit[rows, :] = (gate * grad_gate * (mine - table)).astype(BF)
        d_gate[rows, :] = (grad_hidden * up_in * sig * (1.0 + gate_in * (1.0 - sig))).astype(BF)
        d_up[rows, :] = (grad_hidden * act).astype(BF)
        hidden[rows, :] = (gate * hid).astype(BF)

    def outputs(b, out):
        rows = rows_of(b)
        out[...] = (nt(d_gate[rows, :], w[0]) + nt(d_up[rows, :], w[1]) + nt(d_logit[rows, :], router[...])).astype(BF)

    order = [(k, core) for k in (2, 1, 3, 0) for core in (1, 0)]
    block_of = lambda k, core: up4(y, k) * 2 + up2(c, core)
    twins, sent = {}, {}

    def after(k, core):
        if core:
            twins[k] = links.send(theirs.at[k], twin.at[k], twin_sems.at[k], links.at(dc=1))

    def pass_on(k):
        twins[k].wait_recv()
        own[k] = (own[k].astype(F32) + twin[k].astype(F32)).astype(BF)
        if k:
            j = (4 - k) % 4
            sent[j] = links.send(own.at[k], ring.at[j - 1], ring_sems.at[j], links.at(dy=k))

    for n in range(9):
        if n < 8:
            k, core = order[n]
            loads[(k, core, 0)].wait()
            loads[(k, core, 1)].wait()
            inputs(block_of(k, core), (even, odd)[n % 2])
        if n > 0:
            k, core = order[n - 1]
            b = block_of(k, core)
            middle(b, (even, odd)[(n - 1) % 2])
            outputs(b, theirs.at[k] if core else own.at[k])
            after(k, core)
            if not core and n > 2:
                pass_on(order[n - 3][0])
    pass_on(0)

    def strip(i, carry):
        columns = rows_of(i)
        xt = xs[:, columns]
        for n, (left, right) in enumerate(((xt, d_gate), (xt, d_up), (cs[:, columns], hidden))):
            staged[n, columns, :] = tn(left, right[...]).astype(BF)
        router_out[columns, :] = tn(xt, d_logit[...])
        for n in range(3):
            pltpu.make_async_copy(staged.at[n, columns], dw_out.at[n, columns], dw_sems.at[n * 6 + i]).start()
        return carry

    lax.fori_loop(0, 6, strip, 0)

    def mix(b, carry):
        rows = rows_of(b)
        xs[rows, :] = nt(hidden[rows, :], w[2]).astype(BF)
        pltpu.make_async_copy(xs.at[rows, :], mix_out.at[b], mix_sems.at[b]).start()
        return carry

    lax.fori_loop(0, 8, mix, 0)
    for j in (1, 3, 2):
        sent[j].wait_recv()
    total = own[0].astype(F32)
    for j in range(3):
        total = total + ring[j].astype(F32)
    gx_out[...] = total
    for b in range(8):
        pltpu.make_async_copy(xs.at[rows_of(b), :], mix_out.at[b], mix_sems.at[b]).wait()
    for n in range(3):
        for i in range(6):
            pltpu.make_async_copy(
                staged.at[n, rows_of(i)], dw_out.at[n, rows_of(i)], dw_sems.at[n * 6 + i]
            ).wait()
    links.finish()


def run_expert(w, x_all, c_all, gates, router):
    return pl.pallas_call(
        expert_kernel,
        out_shape=(
            jax.ShapeDtypeStruct((OWN, D), F32),
            jax.ShapeDtypeStruct((8, OWN, D), BF),
            jax.ShapeDtypeStruct((3, D, 768), BF),
            jax.ShapeDtypeStruct((D, 128), F32),
        ),
        in_specs=[VMEM, ANY, ANY, VMEM, VMEM],
        out_specs=(VMEM, ANY, ANY, VMEM),
        scratch_shapes=[
            pltpu.VMEM((8 * OWN, D), BF),
            pltpu.VMEM((8 * OWN, D), BF),
            pltpu.VMEM((8 * OWN, 768), BF),
            pltpu.VMEM((8 * OWN, 768), BF),
            pltpu.VMEM((8 * OWN, 768), BF),
            pltpu.VMEM((8 * OWN, 128), BF),
            pltpu.VMEM((4, OWN, D), BF),
            pltpu.VMEM((4, OWN, D), BF),
            pltpu.VMEM((4, OWN, D), BF),
            pltpu.VMEM((3, OWN, D), BF),
            pltpu.VMEM((3, D, 768), BF),
            pltpu.VMEM((3, OWN, 768), F32),
            pltpu.VMEM((3, OWN, 768), F32),
        ]
        + [pltpu.SemaphoreType.DMA((n,)) for n in (8, 16, 8, 18, 4, 4)],
        compiler_params=pltpu.CompilerParams(
            collective_id=5, has_side_effects=True, vmem_limit_bytes=62 * MIB
        ),
        name="expert",
    )(w, x_all, c_all, gates, router)


class TokenSum:
    SCRATCH = [
        pltpu.VMEM((4, OWN, D), BF),
        pltpu.VMEM((4, OWN, D), BF),
        pltpu.VMEM((3, OWN, D), BF),
        pltpu.SemaphoreType.DMA((4,)),
        pltpu.SemaphoreType.DMA((4,)),
    ]

    def __init__(self, links, src, own, twin, ring, twin_sems, ring_sems):
        self.links, self.own, self.twin, self.ring, self.ring_sems = links, own, twin, ring, ring_sems
        yh, _, _, c, t = links.me
        y = yh * 2 + t
        self.order = (2, 1, 3, 0)
        self.twins, self.kept = {}, {}
        for k in self.order:
            self.twins[k] = links.send(src.at[up4(y, k), 1 - c], twin.at[k], twin_sems.at[k], links.at(dc=1))
            self.kept[k] = links.keep(src.at[up4(y, k), c], own.at[k])

    def spread(self):
        self.sent = {}
        for k in self.order:
            self.kept[k].wait()
            self.twins[k].wait_recv()

            def add(i, carry):
                rows = pl.ds(pl.multiple_of(i * 64, 64), 64)
                self.own[k, rows, :] = (self.own[k, rows, :].astype(F32) + self.twin[k, rows, :].astype(F32)).astype(BF)
                return carry

            lax.fori_loop(0, OWN // 64, add, 0)
            if k:
                j = (4 - k) % 4
                self.sent[j] = self.links.send(
                    self.own.at[k], self.ring.at[j - 1], self.ring_sems.at[j], self.links.at(dy=k)
                )

    def total(self, out):
        for j in (1, 3, 2):
            self.sent[j].wait_recv()

        def add(i, carry):
            rows = pl.ds(pl.multiple_of(i * 64, 64), 64)
            part = self.own[0, rows, :].astype(F32)
            for j in range(3):
                part = part + self.ring[j, rows, :].astype(F32)
            out[rows, :] = part
            return carry

        lax.fori_loop(0, OWN // 64, add, 0)


def add_blocks(refs, out, count):
    def body(i, carry):
        part = refs[0][i].astype(F32)
        for ref in refs[1:]:
            part = part + ref[i].astype(F32)
        out[i] = part.astype(out.dtype)
        return carry

    lax.fori_loop(0, count, body, 0)


def reduce_experts_kernel(
    g, ge,
    own, first, mid, second, last,
    send_sems, local_sems, first_sems, second_sems, expert_sems,
):
    links = Links(send_sems, local_sems)
    yh, x, z, c, t = links.me
    y = yh * 2 + t
    cross = [dict(dy=k, dc=1) for k in (1, 2, 3)]
    links.barrier([links.at(**w) for w in ALONG + RING + cross + [dict(dc=1)]])

    arrive = {}
    for k in (2, 1, 3):
        j = (4 - k) % 4
        arrive[(0, j)] = links.send(
            g.at[:, 0, :, up4(z, k)], first.at[0, j - 1], first_sems.at[j - 1], links.at(dz=k)
        )
        arrive[(1, j)] = links.send(
            g.at[:, 1, up4(x, k)], first.at[1, j - 1], first_sems.at[3 + j - 1], links.at(dx=k)
        )
    kept = [links.keep(g.at[:, 0, :, z], own.at[0]), links.keep(g.at[:, 1, x], own.at[1])]
    for copy in kept:
        copy.wait()
    for j in (1, 3, 2):
        for h in (0, 1):
            arrive[(h, j)].wait_recv()
    final = {}
    for k in (2, 1, 3, 0):
        for h in (0, 1):
            place_of = up4(x, k) if h == 0 else up4(z, k)

            def body(i, carry):
                part = own[h, i, place_of].astype(F32)
                for j in range(3):
                    part = part + first[h, j, i, place_of].astype(F32)
                mid[h, k, i] = part.astype(BF)
                return carry

            lax.fori_loop(0, 3, body, 0)
            if k:
                j = (4 - k) % 4
                target = links.at(dx=k) if h == 0 else links.at(dz=k)
                final[(h, j)] = links.send(
                    mid.at[h, k], second.at[h, j - 1], second_sems.at[h * 3 + j - 1], target
                )
    for h in (0, 1):
        for j in (1, 3, 2):
            final[(h, j)].wait_recv()
        add_blocks([mid.at[h, 0], second.at[h, 0], second.at[h, 1], second.at[h, 2]], last.at[h], 3)
    back, slot = [], y * 2 + c
    for dyh in range(2):
        for dt in range(2):
            for dc in range(2):
                columns = pl.ds(pl.multiple_of(up2(t, dt) * 384, 384), 384)
                src = last.at[up2(yh, dyh), :, up2(c, dc), :, columns]
                if dyh + dt + dc == 0:
                    stay = links.keep(src, ge.at[slot])
                else:
                    index = (dyh * 2 + dt) * 2 + dc
                    back.append(
                        links.send(src, ge.at[slot], expert_sems.at[index], links.flip(dyh=dyh, dt=dt, dc=dc))
                    )
    for copy in back:
        copy.wait_recv()
    stay.wait()
    links.finish()


def reduce_experts(g):
    return pl.pallas_call(
        reduce_experts_kernel,
        out_shape=jax.ShapeDtypeStruct((8, 3, 24, 384), BF),
        in_specs=[ANY],
        out_specs=ANY,
        scratch_shapes=[
            pltpu.VMEM((2, 3, 4, 2, 24, 768), BF),
            pltpu.VMEM((2, 3, 3, 4, 2, 24, 768), BF),
            pltpu.VMEM((2, 4, 3, 2, 24, 768), BF),
            pltpu.VMEM((2, 3, 3, 2, 24, 768), BF),
            pltpu.VMEM((2, 3, 2, 24, 768), BF),
        ]
        + [pltpu.SemaphoreType.DMA((n,)) for n in (32, 8, 6, 6, 8)],
        compiler_params=pltpu.CompilerParams(
            collective_id=3, has_side_effects=True, vmem_limit_bytes=48 * MIB
        ),
        name="reduce_experts",
    )(g)


def reduce_attention_kernel(
    g, mix, small, g_out, mix_out, small_out,
    own, twin, first, mid, second, last, ring,
    s_twin, s_one, s_first, s_two, s_second, s_three, s_ring,
    tok_own, tok_twin, tok_ring, tok_twin_sems, tok_ring_sems,
    send_sems, local_sems, twin_sems, first_sems, second_sems, ring_sems, small_sems,
):
    links = Links(send_sems, local_sems)
    yh, x, z, c, t = links.me
    links.barrier([links.at(**w) for w in ALONG + RING + [dict(dc=1)]])
    other = links.at(dc=1)
    order = (2, 1, 3, 0)

    def piece(h, k, core):
        return g.at[0, :, :, up4(z, k), core] if h == 0 else g.at[1, :, up4(x, k), :, core]

    s_copy = links.send(small, s_twin, small_sems.at[0], other)
    twins, kept = {}, {}
    for k in order:
        for h in (0, 1):
            twins[(h, k)] = links.send(piece(h, k, 1 - c), twin.at[h, k], twin_sems.at[h * 4 + k], other)
            kept[(h, k)] = links.keep(piece(h, k, c), own.at[h, k])
    tokens = TokenSum(links, mix, tok_own, tok_twin, tok_ring, tok_twin_sems, tok_ring_sems)
    s_copy.wait_recv()
    s_one[...] = small[...] + s_twin[...]
    s_copies = {}
    for k in (1, 2, 3):
        j = (4 - k) % 4
        s_copies[j] = links.send(s_one.at[:, up4(z, k)], s_first.at[j - 1], small_sems.at[j], links.at(dz=k))
    arrive = {}
    for k in order:
        for h in (0, 1):
            kept[(h, k)].wait()
            twins[(h, k)].wait_recv()
            for i in range(2):
                add_blocks([own.at[h, k, i], twin.at[h, k, i]], own.at[h, k, i], 4)
            if k:
                j = (4 - k) % 4
                target = links.at(dz=k) if h == 0 else links.at(dx=k)
                arrive[(h, j)] = links.send(
                    own.at[h, k], first.at[h, j - 1], first_sems.at[h * 3 + j - 1], target
                )
    tokens.spread()
    for j in (1, 2, 3):
        s_copies[j].wait_recv()
    s_two[...] = s_one[:, z] + s_first[0] + s_first[1] + s_first[2]
    for k in (1, 2, 3):
        j = (4 - k) % 4
        s_copies[j] = links.send(s_two.at[up4(x, k)], s_second.at[j - 1], small_sems.at[3 + j], links.at(dx=k))
    for j in (1, 3, 2):
        for h in (0, 1):
            arrive[(h, j)].wait_recv()
    final = {}
    for k in order:
        for h in (0, 1):
            place_of = up4(x, k) if h == 0 else up4(z, k)

            def body(i, carry):
                part = own[h, 0, i, place_of].astype(F32)
                for j in range(3):
                    part = part + first[h, j, i, place_of].astype(F32)
                mid[h, k, i] = part.astype(BF)
                return carry

            lax.fori_loop(0, 2, body, 0)
            if k:
                j = (4 - k) % 4
                target = links.at(dx=k) if h == 0 else links.at(dz=k)
                final[(h, j)] = links.send(
                    mid.at[h, k], second.at[h, j - 1], second_sems.at[h * 3 + j - 1], target
                )
    for j in (1, 2, 3):
        s_copies[j].wait_recv()
    s_three[...] = s_two[x] + s_second[0] + s_second[1] + s_second[2]
    for k in (1, 2, 3):
        j = (4 - k) % 4
        s_copies[j] = links.send(s_three, s_ring.at[j - 1], small_sems.at[6 + j], links.at(dy=k))
    tokens.total(mix_out)
    for h in (0, 1):
        for j in (1, 3, 2):
            final[(h, j)].wait_recv()
        add_blocks([mid.at[h, 0], second.at[h, 0], second.at[h, 1], second.at[h, 2]], last.at[h], 2)
    around = []
    for dyh, dt in ((1, 0), (0, 1), (1, 1)):
        index = dyh * 2 + dt - 1
        around.append(
            links.send(
                last.at[up2(t, dt), up2(yh, dyh)], ring.at[index], ring_sems.at[index], links.flip(dyh=dyh, dt=dt)
            )
        )
    for j in (1, 2, 3):
        s_copies[j].wait_recv()
    small_out[...] = s_three[...] + s_ring[0] + s_ring[1] + s_ring[2]
    for copy in around:
        copy.wait_recv()
    total = last[t, yh].astype(F32)
    for j in range(3):
        total = total + ring[j].astype(F32)
    g_out[...] = total
    links.finish()


def reduce_attention(g, mix, small):
    return pl.pallas_call(
        reduce_attention_kernel,
        out_shape=(
            jax.ShapeDtypeStruct((24, 1792), F32),
            jax.ShapeDtypeStruct((OWN, D), F32),
            jax.ShapeDtypeStruct((8, 128), F32),
        ),
        in_specs=[ANY, ANY, VMEM],
        out_specs=(VMEM, VMEM, VMEM),
        scratch_shapes=[
            pltpu.VMEM((2, 4, 2, 4, 24, 1792), BF),
            pltpu.VMEM((2, 4, 2, 4, 24, 1792), BF),
            pltpu.VMEM((2, 3, 2, 4, 24, 1792), BF),
            pltpu.VMEM((2, 4, 2, 24, 1792), BF),
            pltpu.VMEM((2, 3, 2, 24, 1792), BF),
            pltpu.VMEM((2, 2, 24, 1792), BF),
            pltpu.VMEM((3, 24, 1792), BF),
            pltpu.VMEM((4, 4, 8, 128), F32),
            pltpu.VMEM((4, 4, 8, 128), F32),
            pltpu.VMEM((3, 4, 8, 128), F32),
            pltpu.VMEM((4, 8, 128), F32),
            pltpu.VMEM((3, 8, 128), F32),
            pltpu.VMEM((8, 128), F32),
            pltpu.VMEM((3, 8, 128), F32),
        ]
        + TokenSum.SCRATCH
        + [pltpu.SemaphoreType.DMA((n,)) for n in (48, 16, 8, 6, 6, 3, 10)],
        compiler_params=pltpu.CompilerParams(
            collective_id=4, has_side_effects=True, vmem_limit_bytes=56 * MIB
        ),
        name="reduce_attention",
    )(g, mix, small)


def rope_tables():
    half_size = HD // 2
    exponent = -(np.float32(2.0) * np.arange(half_size, dtype=np.float32)) / np.float32(HD)
    frequency = np.power(np.float32(ROPE_BASE), exponent, dtype=np.float32)
    angles = np.arange(SEQ, dtype=np.float32)[:, None] * frequency[None, :]
    cosine, sine = np.cos(angles), np.sin(angles)
    return np.concatenate([cosine, cosine], axis=1), np.concatenate([-sine, sine], axis=1)


def norm_backward(tokens, inverse, gain_vec, gradient):
    scaled = gradient * gain_vec
    gain_grad = jnp.sum(gradient * tokens * inverse, axis=0)
    token_grad = inverse * scaled - tokens * inverse**3 * jnp.mean(
        scaled * tokens, axis=1, keepdims=True
    )
    return (token_grad, gain_grad)


def mm(a, b, dims):
    return lax.dot_general(a, b, (dims, ((), ())), preferred_element_type=F32)


def shards(
    tokens_in, routes, cotangent, attn_gain, query_proj, key_proj, value_proj, output_proj,
    ffn_gain, router_proj, expert_gate, expert_up, expert_down,
):
    yh, x, z, c, t = place()
    blank = jnp.zeros((24, WIDE - PART), BF)
    extra = jnp.concatenate([router_proj, attn_gain[:, None], ffn_gain[:, None], blank[:, 10:]], axis=1)
    a_block = jnp.stack(
        [
            jnp.concatenate([query_proj, key_proj, extra], axis=1),
            jnp.concatenate([value_proj, output_proj, blank], axis=1),
        ]
    )
    e_block = jnp.stack([expert_gate, expert_up, expert_down]).transpose(2, 0, 1, 3)
    own_routes = lax.dynamic_slice(routes, (OWN * t, 0), (OWN, 4))
    chosen = jnp.any(own_routes[:, :, None] == jnp.arange(128)[None, None, :], axis=1).astype(F32)
    cosine, sine = (jnp.asarray(v) for v in rope_tables())
    w, experts, tok_all, cot_all, gates, normed_own, queries, keys, values, attended, residual = forward(
        a_block, e_block, tokens_in, cotangent, chosen, cosine, sine
    )
    weights = w.reshape(2, 2, D, WIDE)
    router = weights[0, 0, :, PART:]
    gain_attn = router[:, 8].astype(F32)
    gain_ffn = router[:, 9].astype(F32)
    grad_normed_ffn, mixture, grad_experts, grad_router = run_expert(
        experts.reshape(3, D, HALF), tok_all, cot_all, gates, router
    )
    ge = reduce_experts(grad_experts.reshape(3, 2, 4, 4, 2, 24, 768))
    ge = ge.astype(F32).transpose(1, 2, 0, 3)

    inputs = tokens_in.astype(F32)
    inverse_attn = lax.rsqrt(jnp.mean(inputs * inputs, axis=1, keepdims=True) + NORM_EPSILON)
    inverse_ffn = lax.rsqrt(jnp.mean(residual * residual, axis=1, keepdims=True) + NORM_EPSILON)
    cos_own = lax.dynamic_slice(cosine, (OWN * t, 0), (OWN, HD))
    sin_own = lax.dynamic_slice(sine, (OWN * t, 0), (OWN, HD))
    allowed = (OWN * t + jnp.arange(OWN))[:, None] >= jnp.arange(SEQ)[None, :]

    def unrotate(u):
        rolled = jnp.concatenate([u[..., HD // 2 :], u[..., : HD // 2]], axis=-1)
        return u * cos_own[:, None, :] - rolled * sin_own[:, None, :]

    grad_norm, grad_gain_ffn = norm_backward(residual, inverse_ffn, gain_ffn, grad_normed_ffn)
    grad_residual = cotangent.astype(F32) + grad_norm
    grad_branch = grad_residual.astype(BF)
    grad_q, grad_k, grad_v, grad_o = [], [], [], []
    for j in range(2):
        q, k, v = queries[j].reshape(OWN, 6, HD), keys[j], values[j]
        grad_att = mm(grad_branch, weights[j, 1, :, HD:PART], ((1,), (0,))).astype(BF).reshape(OWN, 6, HD)
        scores = jnp.einsum("qgd,sd->gqs", q, k, preferred_element_type=F32) * SCALE
        scores = jnp.where(allowed[None], scores, -1e30)
        exact = jax.nn.softmax(scores, axis=-1)
        probs = exact.astype(BF)
        grad_probs = jnp.einsum("qgd,sd->gqs", grad_att, v, preferred_element_type=F32)
        centred = jnp.sum(exact * grad_probs, axis=-1, keepdims=True)
        grad_scores = (exact * (grad_probs - centred)).astype(BF)
        grad_q.append(jnp.einsum("gqs,sd->qgd", grad_scores, k, preferred_element_type=F32) * SCALE)
        grad_k.append(jnp.einsum("gqs,qgd->sd", grad_scores, q, preferred_element_type=F32) * SCALE)
        grad_v.append(jnp.einsum("gqs,qgd->sd", probs, grad_att, preferred_element_type=F32))
        grad_o.append(mm(grad_branch, attended[j], ((0,), (0,))).astype(BF))
    grad_kv = jnp.concatenate([grad_k[0], grad_k[1], grad_v[0], grad_v[1]], axis=1)
    theirs = lax.dynamic_slice(grad_kv, (OWN * (1 - t), 0), (OWN, 4 * HD)).astype(BF)
    received = lax.ppermute(theirs, "tensor", [(0, 1), (1, 0)])
    grad_kv = lax.dynamic_slice(grad_kv, (OWN * t, 0), (OWN, 4 * HD)) + received.astype(F32)
    grad_normed = 0.0
    grad_a = []
    for j in range(2):
        gq = unrotate(grad_q[j]).astype(BF).reshape(OWN, HALF)
        gk = unrotate(grad_kv[:, HD * j : HD * (j + 1)].reshape(OWN, 1, HD)).astype(BF).reshape(OWN, HD)
        gv = grad_kv[:, HD * (2 + j) : HD * (3 + j)].astype(BF)
        lin = jnp.concatenate([gq, gk, gv], axis=1)
        w_in = jnp.concatenate([weights[j, 0, :, :PART], weights[j, 1, :, :HD]], axis=1)
        grad_normed = grad_normed + mm(lin, w_in, ((1,), (1,)))
        grad_a.append(jnp.concatenate([mm(normed_own, lin, ((0,), (0,))).astype(BF), grad_o[j]], axis=1))
    grad_input_norm, grad_gain_attn = norm_backward(inputs, inverse_attn, gain_attn, grad_normed)
    grad_input = (grad_residual + grad_input_norm).astype(BF)

    small = jnp.concatenate([grad_router[:, :8], grad_gain_attn[:, None], grad_gain_ffn[:, None]], axis=1)
    small = small.reshape(2, 4, 4, 2, 24, 10).transpose(1, 2, 0, 3, 4, 5).reshape(16, 960)
    small = jnp.pad(small, ((0, 0), (0, 64))).reshape(4, 4, 8, 128)
    ga, mix, small = reduce_attention(
        jnp.stack(grad_a).reshape(2, 2, 4, 4, 2, 24, 1792), mixture.reshape(4, 2, OWN, D), small
    )
    layer_output = (residual + mix).astype(BF)
    small = small.reshape(1024)[:960].reshape(2, 2, 2, 12, 10)
    small = lax.dynamic_slice(small, (yh, c, t, 0, 0), (1, 1, 1, 12, 10)).reshape(12, 10)
    return (
        layer_output,
        grad_input,
        small[:, 8],
        ga[:, :HALF],
        ga[:, HALF : HALF + HD],
        ga[:, HALF + HD : 1024],
        ga[:, 1024:],
        small[:, 9],
        small[:, :8],
        ge[0],
        ge[1],
        ge[2],
    )


def solution(mesh):
    return jax.shard_map(
        shards,
        mesh=mesh,
        in_specs=(
            P(("dp", "tensor"), None),
            P("dp", None),
            P(("dp", "tensor"), None),
            P("dp"),
            P("dp", "tensor"),
            P("dp", "tensor"),
            P("dp", "tensor"),
            P("dp", "tensor"),
            P("dp"),
            P("dp", None),
            P("dp", None, "tensor"),
            P("dp", None, "tensor"),
            P("dp", None, "tensor"),
        ),
        out_specs=(
            P(("dp", "tensor"), None),
            P(("dp", "tensor"), None),
            P(("dp", "tensor")),
            P("dp", "tensor"),
            P("dp", "tensor"),
            P("dp", "tensor"),
            P("dp", "tensor"),
            P(("dp", "tensor")),
            P(("dp", "tensor"), None),
            P("dp", None, "tensor"),
            P("dp", None, "tensor"),
            P("dp", None, "tensor"),
        ),
        check_vma=False,
    )
```

```python
import functools

import jax
import jax.numpy as jnp
import numpy as np
from jax import lax
from jax.experimental import pallas as pl
from jax.experimental.pallas import tpu as pltpu
from jax.sharding import PartitionSpec as P

HD = 128
E = 8
D = 1536
SEQ = 512
OWN = 256
HALF = 768
PART = 896
WIDE = 1024
NORM_EPSILON = 1e-06
ROPE_BASE = 1000000.0
SCALE = HD ** (-0.5)
MESH = pl.DeviceIdType.MESH
BF = jnp.bfloat16
F32 = jnp.float32
ANY = pl.BlockSpec(memory_space=pl.ANY)
VMEM = pl.BlockSpec(memory_space=pltpu.VMEM)
MIB = 1 << 20


def place():
    d = lax.axis_index("dp")
    t = lax.axis_index("tensor")
    c = lax.rem(d, 2)
    z = lax.rem(lax.div(d, 2), 4)
    x = lax.rem(lax.div(d, 8), 4)
    yh = lax.div(d, 32)
    return yh, x, z, c, t


def device(yh, x, z, c, t):
    return (((yh * 4 + x) * 4 + z) * 2 + c, t)


def up4(v, k):
    return lax.rem(v + k, 4)


def up2(v, k):
    return lax.rem(v + k, 2)


def rows_of(b, size=OWN):
    return pl.ds(pl.multiple_of(b * size, size), size)


def nn(a, b):
    return jnp.dot(a, b, preferred_element_type=F32)


def nt(a, b):
    return lax.dot_general(a, b, (((1,), (1,)), ((), ())), preferred_element_type=F32)


def tn(a, b):
    return lax.dot_general(a, b, (((0,), (0,)), ((), ())), preferred_element_type=F32)


class Links:
    def __init__(self, send_sems, local_sems):
        self.me = place()
        self.send_sems, self.local_sems = send_sems, local_sems
        self.sent, self.local, self.count = [], [], 0

    def at(self, dy=0, dx=0, dz=0, dc=0):
        yh, x, z, c, t = self.me
        y = up4(yh * 2 + t, dy)
        return device(lax.div(y, 2), up4(x, dx), up4(z, dz), up2(c, dc), lax.rem(y, 2))

    def flip(self, dyh=0, dt=0, dc=0):
        yh, x, z, c, t = self.me
        return device(up2(yh, dyh), x, z, up2(c, dc), up2(t, dt))

    def barrier(self, partners):
        sem = pltpu.get_barrier_semaphore()
        for partner in partners:
            pl.semaphore_signal(sem, inc=1, device_id=partner, device_id_type=MESH)
        pl.semaphore_wait(sem, len(partners))

    def send(self, src, dst, recv_sem, target):
        copy = pltpu.make_async_remote_copy(
            src_ref=src,
            dst_ref=dst,
            send_sem=self.send_sems.at[self.count],
            recv_sem=recv_sem,
            device_id=target,
            device_id_type=MESH,
        )
        copy.start()
        self.count += 1
        self.sent.append(copy)
        return copy

    def keep(self, src, dst):
        copy = pltpu.make_async_copy(src, dst, self.local_sems.at[len(self.local)])
        copy.start()
        self.local.append(copy)
        return copy

    def left(self, copy):
        copy.wait_send()
        self.sent = [other for other in self.sent if other is not copy]

    def finish(self):
        for copy in self.sent:
            copy.wait_send()


ALONG = [dict(dx=k) for k in (1, 2, 3)] + [dict(dz=k) for k in (1, 2, 3)]
NEAR = [dict(dx=k) for k in (1, 3)] + [dict(dz=k) for k in (1, 3)]
RING = [dict(dy=k) for k in (1, 2, 3)]
CROSS = [dict(dy=k, dc=1) for k in (1, 2, 3)]
TWIN = [dict(dc=1)]


def plane_gather(links, whole, piece, own, sems, arrived):
    _, x, z, _, _ = links.me
    got = {}

    def spot(fn, h, da, db, *i):
        xo, zo = (up4(x, da), up4(z, db)) if h == 0 else (up4(x, db), up4(z, da))
        return fn(h, xo, zo, *i)

    def target(h, second, k):
        return links.at(dx=k) if (h == 0) != second else links.at(dz=k)

    def sem(h, da, db, i=0):
        return sems.at[((h * 4 + da) * 4 + db) * 2 + i]

    def push(h, da, second):
        dst = spot(whole, h, da, 0)
        src = own(h) if da == 0 else dst
        for k in (1, 3):
            key = (h, da, 4 - k) if second else (h, 4 - k, 0)
            got[key] = links.send(src, dst, sem(*key), target(h, second, k))

    def take(h, da, db, second):
        got[(h, da, db)].wait_recv()
        i, k = (0, 1) if (db if second else da) == 3 else (1, 3)
        key = (h, da, 2, i) if second else (h, 2, 0, i)
        ref = spot(piece, h, da, db, i)
        got[key] = links.send(ref, ref, sem(*key), target(h, second, k))

    def far(h, da, db):
        for i in (0, 1):
            got[(h, da, db, i)].wait_recv()

    for h in (0, 1):
        push(h, 0, False)
    for h in (0, 1):
        push(h, 0, True)
    yield
    for da in (3, 1):
        for h in (0, 1):
            take(h, da, 0, False)
            push(h, da, True)
            arrived(spot(whole, h, da, 0), h, da, 0)
        yield
    for db in (3, 1):
        for h in (0, 1):
            take(h, 0, db, True)
            arrived(spot(whole, h, 0, db), h, 0, db)
    yield
    for h in (0, 1):
        far(h, 2, 0)
        push(h, 2, True)
        arrived(spot(whole, h, 2, 0), h, 2, 0)
    yield
    for da in (3, 1, 2):
        for db in (3, 1):
            for h in (0, 1):
                take(h, da, db, True)
                arrived(spot(whole, h, da, db), h, da, db)
        yield
    for da in (0, 3, 1, 2):
        for h in (0, 1):
            far(h, da, 2)
            arrived(spot(whole, h, da, 2), h, da, 2)
        yield


def ring_gather(links, src, block, sems, arrived):
    got = {}

    def part(ref, i):
        return ref.at[pl.ds(128 * i, 128), :]

    for i in (0, 1):
        for k in (1, 3):
            half = i if k == 1 else 1 - i
            j = 4 - k
            got[(j, half)] = links.send(
                part(src, half), part(block(0), half), sems.at[j * 2 + half], links.at(dy=k)
            )
    yield
    for j, half, k in ((3, 0, 1), (1, 1, 3)):
        got[(j, half)].wait_recv()
        ref = part(block(j), half)
        got[(2, half)] = links.send(ref, ref, sems.at[4 + half], links.at(dy=k))
    yield
    for j, half in ((3, 1), (1, 0)):
        got[(j, half)].wait_recv()
        arrived(block(j), j)
    yield
    for half in (0, 1):
        got[(2, half)].wait_recv()
    arrived(block(2), 2)
    yield


def advance(steps, count=1):
    for _ in range(count):
        next(steps, None)


def drain(steps):
    for _ in steps:
        pass


def roped(u, cosine, sine):
    return u * cosine + pltpu.roll(u, 64, 1) * sine


def unroped(u, cosine, sine):
    return u * cosine - pltpu.roll(u, 64, 1) * sine


def causal_bias(t):
    row = lax.broadcasted_iota(jnp.int32, (OWN, SEQ), 0) + OWN * t
    column = lax.broadcasted_iota(jnp.int32, (OWN, SEQ), 1)
    return jnp.where(row >= column, 0.0, -1e30).astype(F32)


def inverse_norm(v):
    return lax.rsqrt(jnp.mean(v * v, axis=1, keepdims=True) + NORM_EPSILON)


def gain_rows(w):
    tables = [w[0, 0, i, :, PART:].astype(F32).T for i in (0, 1)]
    both = jnp.concatenate(tables, axis=1)
    return both[8:9, :], both[9:10, :]


def forward_kernel(
    a, e, tok, cot, chosen, cosine, sine,
    w_out, e_all, tok_all, cot_all, gates_all, normed_out, q_out, k_out, v_out, att_out, residual_out, gains_out,
    w, a_pair, a_own, e_pair, e_own, pair, normed, tok_two, gates,
    send_sems, local_sems, a_sems, ring_sems, plane_sems, twin_sems, expert_sems, token_sems,
    cot_sems, cot_twin_sems, e_sems, x_sems, x_twin_sems, g_sems, g_twin_sems,
):
    links = Links(send_sems, local_sems)
    yh, x, z, c, t = links.me
    y = yh * 2 + t
    twin = links.at(dc=1)
    here = pl.ds(pl.multiple_of(192 * x + 48 * z, 48), 48)
    links.barrier([links.at(**p) for p in NEAR + RING + CROSS + TWIN])

    kept = [links.keep(a.at[c], a_pair.at[c])]
    a_copy = links.send(a.at[1 - c], a_pair.at[c], a_sems.at[0], twin)
    columns = pl.ds(pl.multiple_of(t * 384, 384), 384)
    slot = e_pair.at[:, yh, c, :, columns]
    kept[0].wait()
    a_copy.wait_recv()
    a_own[...] = jnp.concatenate([a_pair[0].astype(F32), a_pair[1].astype(F32)], axis=0).astype(BF)
    mine = w.at[t, c, yh, here, :]
    ring = {}
    for k in (1, 3, 2):
        ring[4 - k] = links.send(a_own, mine, ring_sems.at[4 - k], links.at(dy=k))
    w_kept = links.keep(a_own, mine)
    experts = []
    for dy in range(4):
        for dc in range(2):
            src = e.at[up4(y, dy) * 2 + up2(c, dc)]
            if dy + dc == 0:
                e_kept = links.keep(src, slot)
            else:
                index = ((4 - dy) % 4) * 2 + dc
                experts.append(links.send(src, slot, expert_sems.at[index], links.at(dy=dy, dc=dc)))
    kept = [links.keep(tok, pair.at[t]), links.keep(cot, cot_all.at[y * 2 + c])]
    token = links.send(tok, pair.at[t], token_sems.at[0], links.flip(dt=1))
    twins = []

    def cot_arrived(ref, j):
        twins.append(links.send(ref, ref, cot_twin_sems.at[j], twin))

    twins.append(links.send(cot, cot_all.at[y * 2 + c], cot_twin_sems.at[0], twin))
    cots = ring_gather(links, cot, lambda j: cot_all.at[up4(y, j) * 2 + c], cot_sems, cot_arrived)
    advance(cots)

    w_kept.wait()
    for j in (1, 3, 2):
        ring[j].wait_recv()
    w_twins = []

    def w_arrived(ref, h, da, db):
        w_twins.append(links.send(ref, ref, twin_sems.at[(h * 4 + da) * 4 + db], twin))

    def w_whole(h, xo, zo):
        return w.at[h, c, :, pl.ds(pl.multiple_of(192 * xo + 48 * zo, 48), 48), :]

    def w_piece(h, xo, zo, i):
        return w.at[h, c, i, pl.ds(pl.multiple_of(192 * xo + 48 * zo, 48), 48), :]

    weights = plane_gather(links, w_whole, w_piece, lambda h: w_whole(h, x, z), plane_sems, w_arrived)
    advance(weights)
    for h in (0, 1):
        w_arrived(w_whole(h, x, z), h, 0, 0)
    e_kept.wait()
    for copy in experts:
        copy.wait_recv()
    for n in range(3):
        for i in range(2):
            e_own[n, i] = jnp.concatenate(
                [e_pair[n, i, 0].astype(F32), e_pair[n, i, 1].astype(F32)], axis=0
            ).astype(BF)
    kept.append(links.keep(e_own, e_all.at[:, :, here, :]))

    def e_whole(h, xo, zo):
        return e_all.at[:, h, pl.ds(pl.multiple_of(192 * xo + 48 * zo, 48), 48), :]

    def e_piece(h, xo, zo, i):
        return e_all.at[:, h, pl.ds(pl.multiple_of(192 * xo + 48 * zo, 48), 48), pl.ds(384 * i, 384)]

    expert = plane_gather(
        links, e_whole, e_piece, lambda h: e_own.at[:, h], e_sems, lambda ref, h, da, db: None
    )
    advance(weights, 3)
    advance(cots)
    advance(weights, 4)
    advance(expert)
    drain(weights)
    advance(cots)
    token.wait_recv()
    for copy in kept[:2]:
        copy.wait()
    for copy in w_twins:
        copy.wait_recv()
    w_dump = links.keep(w, w_out)

    gain_one, gain_two = gain_rows(w)
    gains_out[0:1, :] = gain_one
    gains_out[1:2, :] = gain_two
    gains_out[2:8, :] = jnp.zeros((6, D), F32)
    for i in (0, 1):
        v = pair[i].astype(F32)
        normed[pl.ds(OWN * i, OWN), :] = (v * inverse_norm(v) * gain_one).astype(BF)
    own = rows_of(t)
    normed_out[...] = normed[own, :]
    bias = causal_bias(t)
    cos_own, sin_own = cosine[own, :], sine[own, :]
    residual_out[...] = pair[t].astype(F32)
    for j in (0, 1):
        q = nn(normed_out[:, :HALF], w[j, 0, 0, :, :HALF]) + nn(normed_out[:, HALF:], w[j, 0, 1, :, :HALF])
        k = nn(normed[:, :HALF], w[j, 0, 0, :, HALF:PART]) + nn(normed[:, HALF:], w[j, 0, 1, :, HALF:PART])
        v = nn(normed[:, :HALF], w[j, 1, 0, :, :HD]) + nn(normed[:, HALF:], w[j, 1, 1, :, :HD])
        v = v.astype(BF)
        k = roped(k, cosine[...], sine[...]).astype(BF)
        k_out[j] = k
        v_out[j] = v
        for g in range(6):
            lanes = slice(HD * g, HD * (g + 1))
            qh = roped(q[:, lanes], cos_own, sin_own).astype(BF)
            q_out[j, :, lanes] = qh
            scores = nt(qh, k) * SCALE + bias
            raised = jnp.exp(scores - jnp.max(scores, axis=1, keepdims=True))
            probs = (raised * (1.0 / jnp.sum(raised, axis=1, keepdims=True))).astype(BF)
            att_out[j, :, lanes] = nn(probs, v).astype(BF)
            if g == 2 or g == 5:
                advance(expert)
        for i in (0, 1):
            columns = pl.ds(HALF * i, HALF)
            residual_out[:, columns] += nt(att_out[j], w[j, 1, i, :, HD:PART])
        if j == 0:
            advance(cots)
    residual = residual_out[...]
    tok_two[...] = (residual * inverse_norm(residual) * gain_two).astype(BF)
    block = tok_all.at[y * 2 + c]
    kept.append(links.keep(tok_two, block))

    def x_arrived(ref, j):
        twins.append(links.send(ref, ref, x_twin_sems.at[j], twin))

    tokens = ring_gather(links, tok_two, lambda j: tok_all.at[up4(y, j) * 2 + c], x_sems, x_arrived)
    advance(tokens)
    twins.append(links.send(tok_two, block, x_twin_sems.at[0], twin))
    logits = nn(tok_two[:, :HALF], w[0, 0, 0, :, PART:]) + nn(tok_two[:, HALF:], w[0, 0, 1, :, PART:])
    masked = jnp.where(chosen[...] > 0.5, logits, -1e30)
    raised = jnp.where(chosen[...] > 0.5, jnp.exp(masked - jnp.max(masked, axis=1, keepdims=True)), 0.0)
    table = raised * (1.0 / jnp.sum(raised, axis=1, keepdims=True))
    gates[...] = table.T[:8, :]
    kept.append(links.keep(gates, gates_all.at[y * 2 + c]))
    gate = {}
    for k in (1, 3, 2):
        gate[4 - k] = links.send(gates, gates_all.at[y * 2 + c], g_sems.at[4 - k], links.at(dy=k))
    twins.append(links.send(gates, gates_all.at[y * 2 + c], g_twin_sems.at[0], twin))
    advance(expert, 2)
    advance(tokens)
    drain(expert)
    drain(tokens)
    drain(cots)
    for j in (1, 3, 2):
        gate[j].wait_recv()
        ref = gates_all.at[up4(y, j) * 2 + c]
        twins.append(links.send(ref, ref, g_twin_sems.at[j], twin))
    for copy in twins:
        copy.wait_recv()
    for copy in kept[2:]:
        copy.wait()
    w_dump.wait()
    links.finish()


def forward(a, e, tok, cot, chosen, cosine, sine):
    dma = [pltpu.SemaphoreType.DMA((n,)) for n in (192, 12, 1, 4, 64, 32, 8, 1, 8, 4, 64, 8, 4, 4, 4)]
    return pl.pallas_call(
        forward_kernel,
        out_shape=(
            jax.ShapeDtypeStruct((2, 2, 2, HALF, WIDE), BF),
            jax.ShapeDtypeStruct((3, 2, HALF, HALF), BF),
            jax.ShapeDtypeStruct((8, OWN, D), BF),
            jax.ShapeDtypeStruct((8, OWN, D), BF),
            jax.ShapeDtypeStruct((8, 8, OWN), F32),
            jax.ShapeDtypeStruct((OWN, D), BF),
            jax.ShapeDtypeStruct((2, OWN, HALF), BF),
            jax.ShapeDtypeStruct((2, SEQ, HD), BF),
            jax.ShapeDtypeStruct((2, SEQ, HD), BF),
            jax.ShapeDtypeStruct((2, OWN, HALF), BF),
            jax.ShapeDtypeStruct((OWN, D), F32),
            jax.ShapeDtypeStruct((8, D), F32),
        ),
        in_specs=[ANY, ANY, ANY, ANY, VMEM, VMEM, VMEM],
        out_specs=(ANY,) * 5 + (VMEM,) * 7,
        scratch_shapes=[
            pltpu.VMEM((2, 2, 2, HALF, WIDE), BF),
            pltpu.VMEM((2, 24, WIDE), BF),
            pltpu.VMEM((48, WIDE), BF),
            pltpu.VMEM((3, 2, 2, 24, HALF), BF),
            pltpu.VMEM((3, 2, 48, HALF), BF),
            pltpu.VMEM((2, OWN, D), BF),
            pltpu.VMEM((SEQ, D), BF),
            pltpu.VMEM((OWN, D), BF),
            pltpu.VMEM((8, OWN), F32),
        ]
        + dma,
        compiler_params=pltpu.CompilerParams(
            collective_id=1, has_side_effects=True, vmem_limit_bytes=48 * MIB
        ),
        name="forward",
    )(a, e, tok, cot, chosen, cosine, sine)


ORDER = (2, 1, 3, 0)


class RingSum:
    SCRATCH = [
        pltpu.VMEM((4, OWN, D), BF),
        pltpu.VMEM((2, OWN, D), BF),
        pltpu.VMEM((4, OWN, D), BF),
        pltpu.VMEM((2, OWN // 2, D), BF),
        pltpu.VMEM((2, OWN, D), BF),
        pltpu.SemaphoreType.DMA((4,)),
        pltpu.SemaphoreType.DMA((4,)),
    ]

    def __init__(self, links, own, theirs, twin, far, near, twin_sems, ring_sems):
        self.links, self.own, self.theirs, self.twin = links, own, theirs, twin
        self.far, self.near, self.twin_sems, self.ring_sems = far, near, twin_sems, ring_sems
        self.twins, self.sent = {}, {}

    def place(self, k, core):
        if not core:
            return self.own.at[k]
        step = ORDER.index(k)
        if step >= 2:
            self.links.left(self.twins[ORDER[step - 2]])
        return self.theirs.at[step % 2]

    def to_twin(self, k):
        self.twins[k] = self.links.send(
            self.theirs.at[ORDER.index(k) % 2], self.twin.at[k], self.twin_sems.at[k], self.links.at(dc=1)
        )

    def pass_on(self, k):
        links, own = self.links, self.own
        self.twins[k].wait_recv()
        own[k] = (own[k].astype(F32) + self.twin[k].astype(F32)).astype(BF)
        if k == 2:
            for i, to in ((0, 1), (1, 3)):
                self.sent[i] = links.send(
                    own.at[2, pl.ds(128 * i, 128)], self.far.at[i], self.ring_sems.at[i], links.at(dy=to)
                )
        elif k:
            i = 0 if k == 1 else 1
            half = pl.ds(128 * i, 128)
            self.sent[i].wait_recv()
            own[k, half, :] = (own[k, half, :].astype(F32) + self.far[i].astype(F32)).astype(BF)
            self.sent[3 - i] = links.send(own.at[k], self.near.at[1 - i], self.ring_sems.at[3 - i], links.at(dy=k))

    def total(self):
        for i in (0, 1):
            self.sent[2 + i].wait_recv()
        return self.own[0].astype(F32) + self.near[0].astype(F32) + self.near[1].astype(F32)


def expert_kernel(
    w, x_all, c_all, gates, router, gx_out, mix_out, dw_out, router_out, *rest
):
    xs, cs, hidden, d_gate, d_up, d_logit, staged = rest[:7]
    grads, mixes = rest[7:14], rest[14:21]
    send_sems, load_sems, dw_sems = rest[21:]
    links = Links(send_sems, None)
    yh, _, _, c, t = links.me
    y = yh * 2 + t
    loads = {}
    for k in (2, 1, 3, 0):
        for core in (1, 0):
            b = up4(y, k) * 2 + up2(c, core)
            for n, (src, dst) in enumerate(((x_all, xs), (c_all, cs))):
                copy = pltpu.make_async_copy(src.at[b], dst.at[rows_of(b), :], load_sems.at[(k * 2 + core) * 2 + n])
                copy.start()
                loads[(k, core, n)] = copy
    links.barrier([links.at(**p) for p in RING + TWIN])
    lane = lax.broadcasted_iota(jnp.int32, (OWN, 128), 1)
    mine = (lane == y * 2 + c).astype(F32)
    grad_sum, mix_sum = RingSum(links, *grads), RingSum(links, *mixes)

    def one_block(b, grad, mix):
        rows = rows_of(b)
        xb, cb = xs[rows, :], cs[rows, :]
        gate_in = nn(xb, w[0])
        up_in = nn(xb, w[1])
        back = nn(cb, w[2])
        table = jnp.concatenate([gates[b], jnp.zeros((120, OWN), F32)], axis=0).T
        gate = jnp.sum(table * mine, axis=1, keepdims=True)
        sig = 0.5 * jnp.tanh(0.5 * gate_in) + 0.5
        act = gate_in * sig
        hid = act * up_in
        grad_gate = jnp.sum(hid * back, axis=1, keepdims=True)
        grad_hidden = gate * back
        dl = (gate * grad_gate * (mine - table)).astype(BF)
        dg = (grad_hidden * up_in * (sig + act * (1.0 - sig))).astype(BF)
        du = (grad_hidden * act).astype(BF)
        hw = (gate * hid).astype(BF)
        hidden[rows, :] = hw
        d_gate[rows, :] = dg
        d_up[rows, :] = du
        d_logit[rows, :] = dl
        grad[...] = (nt(dg, w[0]) + nt(du, w[1]) + nt(dl, router[...])).astype(BF)
        mix[...] = nt(hw, w[2]).astype(BF)

    done = None
    for k in ORDER:
        for core in (1, 0):
            loads[(k, core, 0)].wait()
            loads[(k, core, 1)].wait()
            b = up4(y, k) * 2 + up2(c, core)
            one_block(b, grad_sum.place(k, core), mix_sum.place(k, core))
            if core:
                grad_sum.to_twin(k)
                mix_sum.to_twin(k)
                if done is not None:
                    grad_sum.pass_on(done)
        done = k
    grad_sum.pass_on(0)

    def strip(i, carry):
        columns = rows_of(i)
        xt = xs[:, columns]
        slot = lax.rem(i, 2)

        def stored(n, at):
            return pltpu.make_async_copy(staged.at[slot, n], dw_out.at[n, rows_of(at)], dw_sems.at[slot * 3 + n])

        @pl.when(i >= 2)
        def _():
            for n in range(3):
                stored(n, i - 2).wait()

        for n, (left, right) in enumerate(((xt, d_gate), (xt, d_up), (cs[:, columns], hidden))):
            staged[slot, n] = tn(left, right[...]).astype(BF)
        router_out[:, columns] = tn(d_logit[...], xt)[:8, :]
        for n in range(3):
            stored(n, i).start()
        return carry

    for part in range(3):
        mix_sum.pass_on(ORDER[part])
        lax.fori_loop(2 * part, 2 * part + 2, strip, 0)
    mix_sum.pass_on(0)
    gx_out[...] = grad_sum.total()
    mix_out[...] = mix_sum.total().astype(BF)
    for slot in range(2):
        for n in range(3):
            pltpu.make_async_copy(staged.at[slot, n], dw_out.at[n, rows_of(4 + slot)], dw_sems.at[slot * 3 + n]).wait()
    links.finish()


def run_expert(w, x_all, c_all, gates, router):
    return pl.pallas_call(
        expert_kernel,
        out_shape=(
            jax.ShapeDtypeStruct((OWN, D), F32),
            jax.ShapeDtypeStruct((OWN, D), BF),
            jax.ShapeDtypeStruct((3, D, HALF), BF),
            jax.ShapeDtypeStruct((8, D), F32),
        ),
        in_specs=[VMEM, ANY, ANY, VMEM, VMEM],
        out_specs=(VMEM, VMEM, ANY, VMEM),
        scratch_shapes=[
            pltpu.VMEM((8 * OWN, D), BF),
            pltpu.VMEM((8 * OWN, D), BF),
            pltpu.VMEM((8 * OWN, HALF), BF),
            pltpu.VMEM((8 * OWN, HALF), BF),
            pltpu.VMEM((8 * OWN, HALF), BF),
            pltpu.VMEM((8 * OWN, 128), BF),
            pltpu.VMEM((2, 3, OWN, HALF), BF),
        ]
        + RingSum.SCRATCH
        + RingSum.SCRATCH
        + [pltpu.SemaphoreType.DMA((n,)) for n in (24, 16, 6)],
        compiler_params=pltpu.CompilerParams(
            collective_id=5, has_side_effects=True, vmem_limit_bytes=60 * MIB
        ),
        name="expert",
    )(w, x_all, c_all, gates, router)


def plane_reduce(links, h, ops, sems):
    def target(k, stage):
        return links.at(dx=k) if (h == 0) == (stage == 1) else links.at(dz=k)

    for stage in (0, 1):
        base = 4 * stage
        far, near = {}, {}
        for i, k in ((0, 1), (1, 3)):
            far[i] = links.send(ops.far(stage, i), ops.far_land(stage, i), sems.at[base + i], target(k, stage))
        yield
        for i, k in ((0, 1), (1, 3)):
            ops.ready(stage, k)
            far[i].wait_recv()
            ops.add_far(stage, i, k)
            near[i] = links.send(
                ops.near(stage, k), ops.near_land(stage, 1 - i), sems.at[base + 3 - i], target(k, stage)
            )
        yield
        ops.ready(stage, 0)
        for i in (0, 1):
            near[i].wait_recv()
        ops.total(stage)
    yield


def loop(counts, fn):
    a, b = counts

    def body(i, carry):
        fn(lax.div(i, b), lax.rem(i, b))
        return carry

    lax.fori_loop(0, a * b, body, 0)


SLOT = {1: 0, 3: 1, 0: 2}


class ExpertOps:
    SCRATCH = [
        pltpu.VMEM((2, 3, 3, 4, 48, HALF), BF),
        pltpu.VMEM((2, 2, 3, 4, 48, 384), BF),
        pltpu.VMEM((2, 2, 3, 4, 48, HALF), BF),
        pltpu.VMEM((2, 4, 3, 48, HALF), BF),
        pltpu.VMEM((2, 2, 3, 48, 384), BF),
        pltpu.VMEM((2, 2, 3, 48, HALF), BF),
        pltpu.VMEM((2, 2, 3, 24, HALF), BF),
    ]

    def __init__(self, links, h, g, acc, far1, near1, mid, far2, near2, last):
        self.h, self.g, self.acc, self.far1, self.near1 = h, g, acc, far1, near1
        self.mid, self.far2, self.near2, self.last = mid, far2, near2, last
        _, self.x, self.z, _, _ = links.me
        self.loads = {k: links.keep(self.block(k), acc.at[h, SLOT[k]]) for k in (1, 3, 0)}

    def block(self, k, *columns):
        if self.h == 0:
            return self.g.at[(slice(None), 0, slice(None), up4(self.z, k), slice(None)) + columns]
        return self.g.at[(slice(None), 1, up4(self.x, k), slice(None), slice(None)) + columns]

    def ready(self, stage, k):
        if stage == 0:
            self.loads[k].wait()

    def far(self, stage, i):
        columns = pl.ds(384 * i, 384)
        return self.mid.at[self.h, 2, :, :, columns] if stage else self.block(2, columns)

    def far_land(self, stage, i):
        return (self.far2 if stage else self.far1).at[self.h, i]

    def near(self, stage, k):
        return self.mid.at[self.h, k] if stage else self.acc.at[self.h, SLOT[k]]

    def near_land(self, stage, i):
        return (self.near2 if stage else self.near1).at[self.h, i]

    def add_far(self, stage, i, k):
        h, columns = self.h, slice(384 * i, 384 * (i + 1))

        def first(m, a):
            s = SLOT[k]
            self.acc[h, s, m, a, :, columns] = (
                self.acc[h, s, m, a, :, columns].astype(F32) + self.far1[h, i, m, a].astype(F32)
            ).astype(BF)

        def second(m, _):
            self.mid[h, k, m, :, columns] = (
                self.mid[h, k, m, :, columns].astype(F32) + self.far2[h, i, m].astype(F32)
            ).astype(BF)

        loop((3, 1) if stage else (3, 4), second if stage else first)

    def total(self, stage):
        h = self.h
        here = self.x if h == 0 else self.z

        def first(k, m):
            a = up4(here, k)
            self.mid[h, k, m] = (
                self.acc[h, 2, m, a].astype(F32)
                + self.near1[h, 0, m, a].astype(F32)
                + self.near1[h, 1, m, a].astype(F32)
            ).astype(BF)

        def second(m, _):
            value = (
                self.mid[h, 0, m].astype(F32)
                + self.near2[h, 0, m].astype(F32)
                + self.near2[h, 1, m].astype(F32)
            )
            self.last[h, 0, m] = value[:24, :].astype(BF)
            self.last[h, 1, m] = value[24:, :].astype(BF)

        loop((3, 1) if stage else (4, 3), second if stage else first)


class AttentionOps:
    SCRATCH = [
        pltpu.VMEM((2, 2, 2, 4, 4, 48, PART), BF),
        pltpu.VMEM((2, 4, 2, 4, 48, PART), BF),
        pltpu.VMEM((2, 2, 4, 48, PART), BF),
        pltpu.VMEM((2, 2, 2, 4, 48, PART), BF),
        pltpu.VMEM((2, 4, 2, 48, PART), BF),
        pltpu.VMEM((2, 2, 48, PART), BF),
        pltpu.VMEM((2, 2, 2, 48, PART), BF),
        pltpu.VMEM((2, 2, 48, PART), BF),
    ]

    def __init__(self, links, h, twin_sems, g, twin, far1, near1, mid, far2, near2, last):
        self.h, self.g, self.twin, self.far1, self.near1 = h, g, twin, far1, near1
        self.mid, self.far2, self.near2, self.last = mid, far2, near2, last
        _, self.x, self.z, self.c, _ = links.me
        self.twins = {}
        for k in (2, 1, 3, 0):
            self.twins[k] = links.send(
                self.block(1 - self.c, k), twin.at[h, k], twin_sems.at[h * 4 + k], links.at(dc=1)
            )

    def place(self, k):
        return up4(self.z if self.h == 0 else self.x, k)

    def block(self, core, k):
        if self.h == 0:
            return self.g.at[0, core, :, :, self.place(k)]
        return self.g.at[1, core, :, self.place(k)]

    def get(self, k, i, a):
        return self.g[0, self.c, i, a, self.place(k)] if self.h == 0 else self.g[1, self.c, i, self.place(k), a]

    def put(self, k, i, a, value):
        if self.h == 0:
            self.g[0, self.c, i, a, self.place(k)] = value.astype(BF)
        else:
            self.g[1, self.c, i, self.place(k), a] = value.astype(BF)

    def add_twin(self, k):
        self.twins[k].wait_recv()

        def add(i, a):
            self.put(k, i, a, self.get(k, i, a).astype(F32) + self.twin[self.h, k, i, a].astype(F32))

        loop((2, 4), add)

    def ready(self, stage, k):
        if stage == 0:
            self.add_twin(k)

    def far(self, stage, i):
        if stage:
            return self.mid.at[self.h, 2, i]
        if i == 0:
            self.add_twin(2)
        if self.h == 0:
            return self.g.at[0, self.c, i, :, self.place(2)]
        return self.g.at[1, self.c, i, self.place(2)]

    def far_land(self, stage, i):
        return (self.far2 if stage else self.far1).at[self.h, i]

    def near(self, stage, k):
        return self.mid.at[self.h, k] if stage else self.block(self.c, k)

    def near_land(self, stage, i):
        return (self.near2 if stage else self.near1).at[self.h, i]

    def add_far(self, stage, i, k):
        h = self.h
        if stage:
            self.mid[h, k, i] = (self.mid[h, k, i].astype(F32) + self.far2[h, i].astype(F32)).astype(BF)
            return

        def add(a, _):
            self.put(k, i, a, self.get(k, i, a).astype(F32) + self.far1[h, i, a].astype(F32))

        loop((4, 1), add)

    def total(self, stage):
        h = self.h
        here = self.x if h == 0 else self.z

        def first(k, i):
            a = up4(here, k)
            self.mid[h, k, i] = (
                self.get(0, i, a).astype(F32)
                + self.near1[h, 0, i, a].astype(F32)
                + self.near1[h, 1, i, a].astype(F32)
            ).astype(BF)

        def second(i, _):
            self.last[h, i] = (
                self.mid[h, 0, i].astype(F32)
                + self.near2[h, 0, i].astype(F32)
                + self.near2[h, 1, i].astype(F32)
            ).astype(BF)

        loop((2, 1) if stage else (4, 2), second if stage else first)


def backward_kernel(
    g, w, gx, cot, tok, residual, normed, q, k, v, att, cosine, sine, gains, router,
    ge, grad_input, ga, small_out, *rest
):
    expert_refs, attention_refs = rest[:7], rest[7:15]
    (
        wo, wqkv, flow, grad_residual, grad_branch, lin, kv_own, kv_send, kv_recv,
        ring, swap_out, swap_in, small, s_twin, s_land, s_back,
    ) = rest[15:31]
    (
        send_sems, local_sems, expert_sems, attention_sems, twin_sems, back_sems, kv_sems,
        ring_sems, swap_sems, small_sems,
    ) = rest[31:]
    links = Links(send_sems, local_sems)
    yh, x, z, c, t = links.me
    twin = links.at(dc=1)
    load_flow = links.keep(gx, flow)

    def load_out(j):
        return links.keep(w.at[j, 1, :, :, pl.ds(HD, HALF)], wo)

    def load_in(j):
        return [
            links.keep(w.at[j, 0, :, :, pl.ds(0, PART)], wqkv.at[:, :, pl.ds(0, PART)]),
            links.keep(w.at[j, 1, :, :, pl.ds(0, HD)], wqkv.at[:, :, pl.ds(PART, HD)]),
        ]

    out_load = load_out(0)
    links.barrier([links.at(**p) for p in ALONG + RING + CROSS + TWIN])
    reduce_experts = [
        plane_reduce(links, h, ExpertOps(links, h, g, *expert_refs), expert_sems.at[pl.ds(8 * h, 8)])
        for h in (0, 1)
    ]

    def experts(count=1):
        for _ in range(count):
            for steps in reduce_experts:
                next(steps, None)

    experts()
    in_loads = load_in(0)

    load_flow.wait()
    scaled = flow[...] * gains[1:2, :]
    value = residual[...]
    inverse = inverse_norm(value)
    mean = jnp.mean(scaled * value, axis=1, keepdims=True)
    grad = cot[...].astype(F32) + inverse * scaled - value * (inverse * inverse * inverse * mean)
    gain_two = jnp.sum(flow[...] * (value * inverse), axis=0, keepdims=True)
    grad_residual[...] = grad
    grad_branch[...] = grad.astype(BF)
    own = rows_of(t)
    bias = causal_bias(t)
    cos_own, sin_own = cosine[...], sine[...]

    def weight_rows(left, right, store):
        for i in (0, 1):
            for half in (0, 1):
                first = HALF * i + 384 * half
                rows = tn(left[:, first : first + 384], right)
                store(i, half, rows.reshape(2, 4, 48, rows.shape[1]).astype(BF))

    da = attention_refs[0]
    exchanges = []
    for j in (0, 1):
        out_load.wait()
        grad_att = (nn(grad_branch[:, :HALF], wo[0]) + nn(grad_branch[:, HALF:], wo[1])).astype(BF)
        if j == 0:
            out_load = load_out(1)
        kj, vj = k[j], v[j]
        gk = jnp.zeros((SEQ, HD), F32)
        gv = jnp.zeros((SEQ, HD), F32)
        for h in range(6):
            lanes = slice(HD * h, HD * (h + 1))
            qh, gh = q[j, :, lanes], grad_att[:, lanes]
            scores = nt(qh, kj) * SCALE + bias
            raised = jnp.exp(scores - jnp.max(scores, axis=1, keepdims=True))
            exact = raised * (1.0 / jnp.sum(raised, axis=1, keepdims=True))
            grad_probs = nt(gh, vj)
            centred = jnp.sum(exact * grad_probs, axis=1, keepdims=True)
            grad_scores = (exact * (grad_probs - centred)).astype(BF)
            lin[j, :, lanes] = unroped(nn(grad_scores, kj) * SCALE, cos_own, sin_own).astype(BF)
            gk = gk + tn(grad_scores, qh)
            gv = gv + tn(exact.astype(BF), gh)
        both = jnp.concatenate([gk * SCALE, gv], axis=1)
        low, high = both[:OWN, :], both[OWN:, :]
        kv_own[j] = jnp.where(t == 0, low, high)
        kv_send[j] = jnp.where(t == 0, high, low).astype(BF)
        exchanges.append(links.send(kv_send.at[j], kv_recv.at[j], kv_sems.at[j], links.flip(dt=1)))

        def store_out(i, half, value, j=j):
            da[j, 1, i, 2 * half : 2 * half + 2, :, :, HD:] = value

        weight_rows(grad_branch, att[j], store_out)
        experts()

    reduce_attention = []

    def attention(count=1):
        for _ in range(count):
            for steps in reduce_attention:
                next(steps, None)

    for j in (0, 1):
        exchanges[j].wait_recv()
        total = kv_own[j] + kv_recv[j].astype(F32)
        lin[j, :, HALF:PART] = unroped(total[:, :HD], cos_own, sin_own).astype(BF)
        lin[j, :, PART:] = total[:, HD:].astype(BF)

        def store_in(i, half, value, j=j):
            da[j, 0, i, 2 * half : 2 * half + 2] = value[..., :PART]
            da[j, 1, i, 2 * half : 2 * half + 2, :, :, :HD] = value[..., PART:]

        weight_rows(normed, lin[j], store_in)
        ops = AttentionOps(links, j, twin_sems, *attention_refs)
        for copy in in_loads:
            copy.wait()
        for i in (0, 1):
            columns = slice(HALF * i, HALF * (i + 1))
            part = nt(lin[j], wqkv[i])
            flow[:, columns] = part if j == 0 else flow[:, columns] + part
        if j == 0:
            in_loads = load_in(1)
        experts()
        reduce_attention.append(
            plane_reduce(links, j, ops, attention_sems.at[pl.ds(8 * j, 8)])
        )
        next(reduce_attention[j])
    experts(3)

    last, slot, back = expert_refs[6], (yh * 2 + t) * 2 + c, []
    for dyh in range(2):
        for dt in range(2):
            for dc in range(2):
                columns = pl.ds(pl.multiple_of(up2(t, dt) * 384, 384), 384)
                src = last.at[up2(yh, dyh), up2(c, dc), :, :, columns]
                if dyh + dt + dc == 0:
                    stay = links.keep(src, ge.at[slot])
                else:
                    index = (dyh * 2 + dt) * 2 + dc
                    back.append(
                        links.send(src, ge.at[slot], back_sems.at[index], links.flip(dyh=dyh, dt=dt, dc=dc))
                    )

    gradient = flow[...]
    scaled = gradient * gains[0:1, :]
    value = tok[...].astype(F32)
    inverse = inverse_norm(value)
    mean = jnp.mean(scaled * value, axis=1, keepdims=True)
    grad_input[...] = (
        grad_residual[...] + inverse * scaled - value * (inverse * inverse * inverse * mean)
    ).astype(BF)
    gain_one = jnp.sum(gradient * (value * inverse), axis=0, keepdims=True)
    rows = jnp.concatenate([router[...], gain_one, gain_two, jnp.zeros((6, D), F32)], axis=0)
    small[0] = rows[:, :HALF]
    small[1] = rows[:, HALF:]
    s_copy = links.send(small.at[1 - c], s_twin, small_sems.at[0], twin)
    attention()
    s_copy.wait_recv()
    small[c] = small[c] + s_twin[...]

    def everyone(axis, at):
        copies = {}
        for step in (1, 2, 3):
            j = 4 - step
            copies[j] = links.send(
                small.at[c], s_land.at[at, j - 1], small_sems.at[3 * at + j], links.at(**{axis: step})
            )
        return copies

    def settle(copies, at):
        for copy in copies.values():
            copy.wait_recv()
            links.left(copy)
        small[c] = small[c] + s_land[at, 0] + s_land[at, 1] + s_land[at, 2]

    copies = everyone("dz", 0)
    settle(copies, 0)
    copies = everyone("dx", 1)
    attention()
    settle(copies, 1)
    copies = everyone("dy", 2)
    settle(copies, 2)
    s_copy = links.send(small.at[c], s_back, small_sems.at[10], twin)
    attention()
    attention()

    last = attention_refs[7]
    around = []
    for dyh, dt in ((1, 1), (1, 0), (0, 1)):
        index = dyh * 2 + dt - 1
        around.append(
            links.send(
                last.at[up2(t, dt), up2(yh, dyh)], ring.at[index], ring_sems.at[index], links.flip(dyh=dyh, dt=dt)
            )
        )
    s_copy.wait_recv()
    small_out[c] = small[c]
    small_out[1 - c] = s_back[...]
    for copy in around:
        copy.wait_recv()
    total = last[t, yh].astype(F32)
    for i in range(3):
        total = total + ring[i].astype(F32)
    swap_out[...] = jnp.where(c == 0, total[24:, :], total[:24, :])
    swap = links.send(swap_out, swap_in, swap_sems.at[0], twin)
    ga[c] = jnp.where(c == 0, total[:24, :], total[24:, :])
    for copy in back:
        copy.wait_recv()
    stay.wait()
    swap.wait_recv()
    ga[1 - c] = swap_in[...]
    links.finish()


def backward(g, w, gx, cot, tok, residual, normed, q, k, v, att, cosine, sine, gains, router):
    return pl.pallas_call(
        backward_kernel,
        out_shape=(
            jax.ShapeDtypeStruct((8, 3, 24, 384), BF),
            jax.ShapeDtypeStruct((OWN, D), BF),
            jax.ShapeDtypeStruct((2, 24, PART), F32),
            jax.ShapeDtypeStruct((2, 16, HALF), F32),
        ),
        in_specs=[ANY] * 3 + [VMEM] * 12,
        out_specs=(ANY, VMEM, VMEM, VMEM),
        scratch_shapes=ExpertOps.SCRATCH
        + AttentionOps.SCRATCH
        + [
            pltpu.VMEM((2, HALF, HALF), BF),
            pltpu.VMEM((2, HALF, WIDE), BF),
            pltpu.VMEM((OWN, D), F32),
            pltpu.VMEM((OWN, D), F32),
            pltpu.VMEM((OWN, D), BF),
            pltpu.VMEM((2, OWN, WIDE), BF),
            pltpu.VMEM((2, OWN, 2 * HD), F32),
            pltpu.VMEM((2, OWN, 2 * HD), BF),
            pltpu.VMEM((2, OWN, 2 * HD), BF),
            pltpu.VMEM((3, 48, PART), BF),
            pltpu.VMEM((24, PART), F32),
            pltpu.VMEM((24, PART), F32),
            pltpu.VMEM((2, 16, HALF), F32),
            pltpu.VMEM((16, HALF), F32),
            pltpu.VMEM((3, 3, 16, HALF), F32),
            pltpu.VMEM((16, HALF), F32),
        ]
        + [pltpu.SemaphoreType.DMA((n,)) for n in (80, 16, 16, 16, 8, 8, 2, 3, 1, 11)],
        compiler_params=pltpu.CompilerParams(
            collective_id=6, has_side_effects=True, vmem_limit_bytes=60 * MIB
        ),
        name="backward",
    )(g, w, gx, cot, tok, residual, normed, q, k, v, att, cosine, sine, gains, router)


def rope_tables():
    half_size = HD // 2
    exponent = -(np.float32(2.0) * np.arange(half_size, dtype=np.float32)) / np.float32(HD)
    frequency = np.power(np.float32(ROPE_BASE), exponent, dtype=np.float32)
    angles = np.arange(SEQ, dtype=np.float32)[:, None] * frequency[None, :]
    cosine, sine = np.cos(angles), np.sin(angles)
    return np.concatenate([cosine, cosine], axis=1), np.concatenate([-sine, sine], axis=1)


def shards(
    tokens_in, routes, cotangent, attn_gain, query_proj, key_proj, value_proj, output_proj,
    ffn_gain, router_proj, expert_gate, expert_up, expert_down,
):
    d, t = lax.axis_index("dp"), lax.axis_index("tensor")
    blank = jnp.zeros((24, WIDE - PART), BF)
    extra = jnp.concatenate([router_proj, attn_gain[:, None], ffn_gain[:, None], blank[:, 10:]], axis=1)
    a_block = jnp.stack(
        [
            jnp.concatenate([query_proj, key_proj, extra], axis=1),
            jnp.concatenate([value_proj, output_proj, blank], axis=1),
        ]
    )
    e_block = jnp.stack([expert_gate, expert_up, expert_down]).transpose(2, 0, 1, 3)
    own_routes = lax.dynamic_slice(routes, (OWN * t, 0), (OWN, 4))
    chosen = jnp.any(own_routes[:, :, None] == jnp.arange(128)[None, None, :], axis=1).astype(F32)
    cosine, sine = (jnp.asarray(v) for v in rope_tables())
    w, experts, tok_all, cot_all, gates, normed, queries, keys, values, attended, residual, gains = forward(
        a_block, e_block, tokens_in, cotangent, chosen, cosine, sine
    )
    router = w[0, 0, :, :, PART:].reshape(D, WIDE - PART)
    flow, mixture, grad_experts, grad_router = run_expert(
        experts.reshape(3, D, HALF), tok_all, cot_all, gates, router
    )
    ge, grad_input, ga, small = backward(
        grad_experts.reshape(3, 2, 4, 4, 48, HALF), w, flow, cotangent, tokens_in, residual, normed,
        queries, keys, values, attended,
        lax.dynamic_slice(cosine, (OWN * t, 0), (OWN, HD)), lax.dynamic_slice(sine, (OWN * t, 0), (OWN, HD)),
        gains, grad_router,
    )
    layer_output = (residual + mixture.astype(F32)).astype(BF)
    ge = ge.astype(F32).transpose(1, 2, 0, 3)
    small = jnp.concatenate([small[0], small[1]], axis=1)
    small = lax.dynamic_slice(small, (0, 24 * d + 12 * t), (16, 12))
    return (
        layer_output,
        grad_input,
        small[8],
        ga[0, :, :HALF],
        ga[0, :, HALF:],
        ga[1, :, :HD],
        ga[1, :, HD:],
        small[9],
        small[:8].T,
        ge[0],
        ge[1],
        ge[2],
    )


def solution(mesh):
    return jax.shard_map(
        shards,
        mesh=mesh,
        in_specs=(
            P(("dp", "tensor"), None),
            P("dp", None),
            P(("dp", "tensor"), None),
            P("dp"),
            P("dp", "tensor"),
            P("dp", "tensor"),
            P("dp", "tensor"),
            P("dp", "tensor"),
            P("dp"),
            P("dp", None),
            P("dp", None, "tensor"),
            P("dp", None, "tensor"),
            P("dp", None, "tensor"),
        ),
        out_specs=(
            P(("dp", "tensor"), None),
            P(("dp", "tensor"), None),
            P(("dp", "tensor")),
            P("dp", "tensor"),
            P("dp", "tensor"),
            P("dp", "tensor"),
            P("dp", "tensor"),
            P(("dp", "tensor")),
            P(("dp", "tensor"), None),
            P("dp", None, "tensor"),
            P("dp", None, "tensor"),
            P("dp", None, "tensor"),
        ),
        check_vma=False,
    )
```

```python
import functools

import jax
import jax.numpy as jnp
import numpy as np
from jax import lax
from jax.experimental import pallas as pl
from jax.experimental.pallas import tpu as pltpu
from jax.sharding import PartitionSpec as P

HD = 128
E = 8
D = 1536
SEQ = 512
OWN = 256
HALF = 768
PART = 896
WIDE = 1024
NORM_EPSILON = 1e-06
ROPE_BASE = 1000000.0
SCALE = HD ** (-0.5)
MESH = pl.DeviceIdType.MESH
BF = jnp.bfloat16
F32 = jnp.float32
ANY = pl.BlockSpec(memory_space=pl.ANY)
VMEM = pl.BlockSpec(memory_space=pltpu.VMEM)
MIB = 1 << 20


def place():
    d = lax.axis_index("dp")
    t = lax.axis_index("tensor")
    c = lax.rem(d, 2)
    z = lax.rem(lax.div(d, 2), 4)
    x = lax.rem(lax.div(d, 8), 4)
    yh = lax.div(d, 32)
    return yh, x, z, c, t


def device(yh, x, z, c, t):
    return (((yh * 4 + x) * 4 + z) * 2 + c, t)


def up4(v, k):
    return lax.rem(v + k, 4)


def up2(v, k):
    return lax.rem(v + k, 2)


def rows_of(b, size=OWN):
    return pl.ds(pl.multiple_of(b * size, size), size)


def nn(a, b):
    return jnp.dot(a, b, preferred_element_type=F32)


def nt(a, b):
    return lax.dot_general(a, b, (((1,), (1,)), ((), ())), preferred_element_type=F32)


def tn(a, b):
    return lax.dot_general(a, b, (((0,), (0,)), ((), ())), preferred_element_type=F32)


class Links:
    def __init__(self, send_sems, local_sems):
        self.me = place()
        self.send_sems, self.local_sems = send_sems, local_sems
        self.sent, self.local, self.count = [], [], 0

    def at(self, dy=0, dx=0, dz=0, dc=0):
        yh, x, z, c, t = self.me
        y = up4(yh * 2 + t, dy)
        return device(lax.div(y, 2), up4(x, dx), up4(z, dz), up2(c, dc), lax.rem(y, 2))

    def flip(self, dyh=0, dt=0, dc=0):
        yh, x, z, c, t = self.me
        return device(up2(yh, dyh), x, z, up2(c, dc), up2(t, dt))

    def barrier(self, partners):
        sem = pltpu.get_barrier_semaphore()
        for partner in partners:
            pl.semaphore_signal(sem, inc=1, device_id=partner, device_id_type=MESH)
        pl.semaphore_wait(sem, len(partners))

    def send(self, src, dst, recv_sem, target):
        copy = pltpu.make_async_remote_copy(
            src_ref=src,
            dst_ref=dst,
            send_sem=self.send_sems.at[self.count],
            recv_sem=recv_sem,
            device_id=target,
            device_id_type=MESH,
        )
        copy.start()
        self.count += 1
        self.sent.append(copy)
        return copy

    def keep(self, src, dst):
        copy = pltpu.make_async_copy(src, dst, self.local_sems.at[len(self.local)])
        copy.start()
        self.local.append(copy)
        return copy

    def left(self, copy):
        copy.wait_send()
        self.sent = [other for other in self.sent if other is not copy]

    def finish(self):
        for copy in self.sent:
            copy.wait_send()


ALONG = [dict(dx=k) for k in (1, 2, 3)] + [dict(dz=k) for k in (1, 2, 3)]
NEAR = [dict(dx=k) for k in (1, 3)] + [dict(dz=k) for k in (1, 3)]
RING = [dict(dy=k) for k in (1, 2, 3)]
CROSS = [dict(dy=k, dc=1) for k in (1, 2, 3)]
TWIN = [dict(dc=1)]


def plane_gather(links, h, own, one, column, sems, arrived):
    got = {}

    def target(second, k):
        return links.at(dx=k) if (h == 0) != second else links.at(dz=k)

    def push(second, src, dst):
        base = 4 if second else 0
        for n, k in ((0, 1), (1, 3)):
            got[(second, 4 - k)] = links.send(src, dst, sems.at[base + 1 - n], target(second, k))

    def take(second, d, view):
        got[(second, d)].wait_recv()
        i, k = (0, 1) if d == 3 else (1, 3)
        ref = view(d, i)
        got[(second, 2, i)] = links.send(ref, ref, sems.at[(4 if second else 0) + 2 + i], target(second, k))

    push(False, own, one(0))
    yield
    for d in (3, 1):
        take(False, d, one)
    yield
    for i in (0, 1):
        got[(False, 2, i)].wait_recv()
    push(True, column(0), column(0))
    arrived(column(0), 0)
    yield
    for d in (3, 1):
        take(True, d, column)
        arrived(column(d), d)
    yield
    for i in (0, 1):
        got[(True, 2, i)].wait_recv()
    arrived(column(2), 2)
    yield


def plane_views(links, base):
    _, x, z, _, _ = links.me

    def views(h):
        here = (x, z) if h == 0 else (z, x)

        def pick(first, second, *i):
            return base(h, first, second, *i) if h == 0 else base(h, second, first, *i)

        def one(d, *i):
            return pick(up4(here[0], d), here[1], *i)

        def column(d, *i):
            return pick(slice(None), up4(here[1], d), *i)

        return one, column

    return views


def ring_gather(links, src, block, sems, arrived):
    got = {}

    def part(ref, i):
        return ref.at[pl.ds(128 * i, 128), :]

    for i in (0, 1):
        for k in (1, 3):
            half = i if k == 1 else 1 - i
            j = 4 - k
            got[(j, half)] = links.send(
                part(src, half), part(block(0), half), sems.at[j * 2 + half], links.at(dy=k)
            )
    yield
    for j, half, k in ((3, 0, 1), (1, 1, 3)):
        got[(j, half)].wait_recv()
        ref = part(block(j), half)
        got[(2, half)] = links.send(ref, ref, sems.at[4 + half], links.at(dy=k))
    yield
    for j, half in ((3, 1), (1, 0)):
        got[(j, half)].wait_recv()
        arrived(block(j), j)
    yield
    for half in (0, 1):
        got[(2, half)].wait_recv()
    arrived(block(2), 2)
    yield


def advance(*groups, count=1):
    for _ in range(count):
        for steps in groups:
            next(steps, None)


def drain(*groups):
    for steps in groups:
        for _ in steps:
            pass


def roped(u, cosine, sine):
    return u * cosine + pltpu.roll(u, 64, 1) * sine


def unroped(u, cosine, sine):
    return u * cosine - pltpu.roll(u, 64, 1) * sine


def causal_bias(t):
    row = lax.broadcasted_iota(jnp.int32, (OWN, SEQ), 0) + OWN * t
    column = lax.broadcasted_iota(jnp.int32, (OWN, SEQ), 1)
    return jnp.where(row >= column, 0.0, -1e30).astype(F32)


def inverse_norm(v):
    return lax.rsqrt(jnp.mean(v * v, axis=1, keepdims=True) + NORM_EPSILON)


def flat(w, j, half, i, lanes):
    block = w[j, half, i, :, :, :, lanes]
    return block.reshape(HALF, block.shape[-1])


def gain_rows(w):
    tables = [flat(w, 0, 0, i, slice(512, 640)).astype(F32).T for i in (0, 1)]
    both = jnp.concatenate(tables, axis=1)
    return both[8:9, :], both[9:10, :]


def forward_kernel(
    a_in, a_out, e, tok, cot, chosen_all, cosine_all, sine_all,
    w_in_out, w_out_out, router_out, e_all, tok_all, cot_all, gates_all, normed_out, q_out, k_out, v_out, att_out, residual_out, gains_out,
    w, wo, a_pair, o_pair, a_own, o_own, e_pair, e_own, pair, normed, tok_two, gates, chosen, cosine, sine,
    send_sems, local_sems, a_sems, ring_sems, plane_sems, twin_sems, o_plane_sems, o_twin_sems, expert_sems, token_sems,
    cot_sems, cot_twin_sems, e_sems, x_sems, x_twin_sems, g_sems, g_twin_sems,
):
    links = Links(send_sems, local_sems)
    yh, x, z, c, t = links.me
    y = yh * 2 + t
    twin = links.at(dc=1)
    links.barrier([links.at(**p) for p in NEAR + RING + CROSS + TWIN])

    groups = ((a_in, a_pair, a_own, w), (a_out, o_pair, o_own, wo))
    kept = [links.keep(src.at[c], two.at[c]) for src, two, _, _ in groups]
    copies = [
        links.send(src.at[1 - c], two.at[c], a_sems.at[n], twin) for n, (src, two, _, _) in enumerate(groups)
    ]
    tables = [links.keep(chosen_all, chosen), links.keep(cosine_all, cosine), links.keep(sine_all, sine)]
    ring, w_kept = {}, []
    for n, (_, two, block, full) in enumerate(groups):
        kept[n].wait()
        copies[n].wait_recv()
        block[...] = jnp.concatenate([two[0].astype(F32), two[1].astype(F32)], axis=0).astype(BF)
        mine = full.at[t, c, yh, x, z]
        for k in (1, 3, 2):
            ring[(n, 4 - k)] = links.send(block, mine, ring_sems.at[n * 4 + 4 - k], links.at(dy=k))
        w_kept.append(links.keep(block, mine))
    columns = pl.ds(pl.multiple_of(t * 384, 384), 384)
    slot = e_pair.at[:, yh, c, :, columns]
    experts = []
    for dy in range(4):
        for dc in range(2):
            src = e.at[up4(y, dy) * 2 + up2(c, dc)]
            if dy + dc == 0:
                e_kept = links.keep(src, slot)
            else:
                index = ((4 - dy) % 4) * 2 + dc
                experts.append(links.send(src, slot, expert_sems.at[index], links.at(dy=dy, dc=dc)))
    kept += [links.keep(tok, pair.at[t]), links.keep(cot, cot_all.at[y * 2 + c])]
    token = links.send(tok, pair.at[t], token_sems.at[0], links.flip(dt=1))
    twins = []

    def cot_arrived(ref, j):
        twins.append(links.send(ref, ref, cot_twin_sems.at[j], twin))

    twins.append(links.send(cot, cot_all.at[y * 2 + c], cot_twin_sems.at[0], twin))
    cots = ring_gather(links, cot, lambda j: cot_all.at[up4(y, j) * 2 + c], cot_sems, cot_arrived)
    advance(cots)

    w_twins = ([], [])

    def spread(n):
        full, twin_n = groups[n][3], (twin_sems, o_twin_sems)[n]

        def base(h, xo, zo, i=slice(None)):
            return full.at[h, c, i, xo, zo]

        views = plane_views(links, base)
        w_kept[n].wait()
        for j in (1, 3, 2):
            ring[(n, j)].wait_recv()
        steps = []
        for h in (0, 1):

            def arrived(ref, d, h=h):
                w_twins[n].append(links.send(ref, ref, twin_n.at[h * 4 + d], twin))

            one, column = views(h)
            sems = (plane_sems, o_plane_sems)[n].at[pl.ds(8 * h, 8)]
            steps.append(plane_gather(links, h, one(0), one, column, sems, arrived))
        advance(*steps)
        return steps

    weights = spread(0)
    out_weights = spread(1)
    e_kept.wait()
    for copy in experts:
        copy.wait_recv()
    for n in range(3):
        for i in range(2):
            e_own[n, i] = jnp.concatenate(
                [e_pair[n, i, 0].astype(F32), e_pair[n, i, 1].astype(F32)], axis=0
            ).astype(BF)
    e_placed = links.keep(e_own, e_all.at[:, :, x, z])

    def e_base(h, xo, zo, i=None):
        if i is None:
            return e_all.at[:, h, xo, zo]
        return e_all.at[:, h, xo, zo, :, pl.ds(384 * i, 384)]

    e_views = plane_views(links, e_base)
    expert = [
        plane_gather(links, h, e_own.at[:, h], *e_views(h), e_sems.at[pl.ds(8 * h, 8)], lambda ref, d: None)
        for h in (0, 1)
    ]
    advance(*weights)
    advance(*out_weights)
    advance(*weights)
    advance(*out_weights)
    e_placed.wait()
    advance(*expert)
    advance(*weights)
    advance(*weights)
    advance(*out_weights)
    token.wait_recv()
    for copy in kept[2:4] + tables:
        copy.wait()
    for copy in w_twins[0]:
        copy.wait_recv()
    w_dumps = [
        links.keep(w.at[:, :, :, :, :, :, pl.ds(0, 512)], w_in_out),
        links.keep(w.at[0, 0, :, :, :, :, pl.ds(512, 128)], router_out),
    ]

    gain_one, gain_two = gain_rows(w)
    gains_out[0:1, :] = gain_one
    gains_out[1:2, :] = gain_two
    gains_out[2:8, :] = jnp.zeros((6, D), F32)
    for i in (0, 1):
        v = pair[i].astype(F32)
        normed[pl.ds(OWN * i, OWN), :] = (v * inverse_norm(v) * gain_one).astype(BF)
    own = rows_of(t)
    normed_out[...] = normed[own, :]
    bias = causal_bias(t)
    cos_own, sin_own = cosine[own, :], sine[own, :]
    residual_out[...] = pair[t].astype(F32)

    def project(source, j, half, lanes):
        return nn(source[:, :HALF], flat(w, j, half, 0, lanes)) + nn(source[:, HALF:], flat(w, j, half, 1, lanes))

    for j in (0, 1):
        k = project(normed, j, 1, slice(256, 384))
        v = project(normed, j, 1, slice(384, 512)).astype(BF)
        q = jnp.concatenate(
            [project(normed_out, j, 0, slice(0, 512)), project(normed_out, j, 1, slice(0, 256))], axis=1
        )
        k = roped(k, cosine[...], sine[...]).astype(BF)
        k_out[j] = k
        v_out[j] = v
        for g in range(6):
            lanes = slice(HD * g, HD * (g + 1))
            qh = roped(q[:, lanes], cos_own, sin_own).astype(BF)
            q_out[j, :, lanes] = qh
            scores = nt(qh, k) * SCALE + bias
            raised = jnp.exp(scores - jnp.max(scores, axis=1, keepdims=True))
            probs = (raised * (1.0 / jnp.sum(raised, axis=1, keepdims=True))).astype(BF)
            att_out[j, :, lanes] = nn(probs, v).astype(BF)
            if (j, g) in ((0, 1), (0, 4)):
                advance(*expert)
            if (j, g) in ((0, 4), (1, 4)):
                advance(cots)
    drain(*out_weights)
    for copy in w_twins[1]:
        copy.wait_recv()
    w_dumps.append(links.keep(wo, w_out_out))
    for i in (0, 1):
        columns = pl.ds(HALF * i, HALF)
        part = residual_out[:, columns]
        for j in (0, 1):
            for half in (0, 1):
                part = part + nt(att_out[j, :, 384 * half : 384 * (half + 1)], flat(wo, j, half, i, slice(0, 384)))
        residual_out[:, columns] = part
    residual = residual_out[...]
    tok_two[...] = (residual * inverse_norm(residual) * gain_two).astype(BF)
    block = tok_all.at[y * 2 + c]
    kept.append(links.keep(tok_two, block))

    def x_arrived(ref, j):
        twins.append(links.send(ref, ref, x_twin_sems.at[j], twin))

    tokens = ring_gather(links, tok_two, lambda j: tok_all.at[up4(y, j) * 2 + c], x_sems, x_arrived)
    advance(tokens)
    twins.append(links.send(tok_two, block, x_twin_sems.at[0], twin))
    lanes = slice(512, 640)
    logits = nn(tok_two[:, :HALF], flat(w, 0, 0, 0, lanes)) + nn(tok_two[:, HALF:], flat(w, 0, 0, 1, lanes))
    masked = jnp.where(chosen[...] > 0.5, logits, -1e30)
    raised = jnp.where(chosen[...] > 0.5, jnp.exp(masked - jnp.max(masked, axis=1, keepdims=True)), 0.0)
    table = raised * (1.0 / jnp.sum(raised, axis=1, keepdims=True))
    gates[...] = table.T[:8, :]
    kept.append(links.keep(gates, gates_all.at[y * 2 + c]))
    gate = {}
    for k in (1, 3, 2):
        gate[4 - k] = links.send(gates, gates_all.at[y * 2 + c], g_sems.at[4 - k], links.at(dy=k))
    twins.append(links.send(gates, gates_all.at[y * 2 + c], g_twin_sems.at[0], twin))
    advance(*expert)
    advance(tokens)
    advance(tokens)
    drain(*expert)
    drain(tokens)
    drain(cots)
    for j in (1, 3, 2):
        gate[j].wait_recv()
        ref = gates_all.at[up4(y, j) * 2 + c]
        twins.append(links.send(ref, ref, g_twin_sems.at[j], twin))
    for copy in twins:
        copy.wait_recv()
    for copy in kept[4:] + w_dumps:
        copy.wait()
    links.finish()


def forward(a_in, a_out, e, tok, cot, chosen, cosine, sine):
    dma = [
        pltpu.SemaphoreType.DMA((n,)) for n in (160, 20, 2, 8, 16, 8, 16, 8, 8, 1, 8, 4, 16, 8, 4, 4, 4)
    ]
    return pl.pallas_call(
        forward_kernel,
        out_shape=(
            jax.ShapeDtypeStruct((2, 2, 2, 4, 4, 48, 512), BF),
            jax.ShapeDtypeStruct((2, 2, 2, 4, 4, 48, 384), BF),
            jax.ShapeDtypeStruct((2, 4, 4, 48, 128), BF),
            jax.ShapeDtypeStruct((3, 2, 4, 4, 48, HALF), BF),
            jax.ShapeDtypeStruct((8, OWN, D), BF),
            jax.ShapeDtypeStruct((8, OWN, D), BF),
            jax.ShapeDtypeStruct((8, 8, OWN), F32),
            jax.ShapeDtypeStruct((OWN, D), BF),
            jax.ShapeDtypeStruct((2, OWN, HALF), BF),
            jax.ShapeDtypeStruct((2, SEQ, HD), BF),
            jax.ShapeDtypeStruct((2, SEQ, HD), BF),
            jax.ShapeDtypeStruct((2, OWN, HALF), BF),
            jax.ShapeDtypeStruct((OWN, D), F32),
            jax.ShapeDtypeStruct((8, D), F32),
        ),
        in_specs=[ANY] * 8,
        out_specs=(ANY,) * 7 + (VMEM,) * 7,
        scratch_shapes=[
            pltpu.VMEM((2, 2, 2, 4, 4, 48, 640), BF),
            pltpu.VMEM((2, 2, 2, 4, 4, 48, 384), BF),
            pltpu.VMEM((2, 24, 640), BF),
            pltpu.VMEM((2, 24, 384), BF),
            pltpu.VMEM((48, 640), BF),
            pltpu.VMEM((48, 384), BF),
            pltpu.VMEM((3, 2, 2, 24, HALF), BF),
            pltpu.VMEM((3, 2, 48, HALF), BF),
            pltpu.VMEM((2, OWN, D), BF),
            pltpu.VMEM((SEQ, D), BF),
            pltpu.VMEM((OWN, D), BF),
            pltpu.VMEM((8, OWN), F32),
            pltpu.VMEM((OWN, 128), F32),
            pltpu.VMEM((SEQ, HD), F32),
            pltpu.VMEM((SEQ, HD), F32),
        ]
        + dma,
        compiler_params=pltpu.CompilerParams(
            collective_id=1, has_side_effects=True, vmem_limit_bytes=60 * MIB
        ),
        name="forward",
    )(a_in, a_out, e, tok, cot, chosen, cosine, sine)


ORDER = (2, 1, 3, 0)


class RingSum:
    SCRATCH = [
        pltpu.VMEM((4, OWN, D), BF),
        pltpu.VMEM((2, OWN, D), BF),
        pltpu.VMEM((4, OWN, D), BF),
        pltpu.VMEM((2, OWN // 2, D), BF),
        pltpu.VMEM((2, OWN, D), BF),
        pltpu.SemaphoreType.DMA((4,)),
        pltpu.SemaphoreType.DMA((4,)),
    ]

    def __init__(self, links, own, theirs, twin, far, near, twin_sems, ring_sems):
        self.links, self.own, self.theirs, self.twin = links, own, theirs, twin
        self.far, self.near, self.twin_sems, self.ring_sems = far, near, twin_sems, ring_sems
        self.twins, self.sent = {}, {}

    def place(self, k, core):
        if not core:
            return self.own.at[k]
        step = ORDER.index(k)
        if step >= 2:
            self.links.left(self.twins[ORDER[step - 2]])
        return self.theirs.at[step % 2]

    def to_twin(self, k):
        self.twins[k] = self.links.send(
            self.theirs.at[ORDER.index(k) % 2], self.twin.at[k], self.twin_sems.at[k], self.links.at(dc=1)
        )

    def add_twin(self, k):
        self.twins[k].wait_recv()
        self.own[k] = (self.own[k].astype(F32) + self.twin[k].astype(F32)).astype(BF)

    def pass_on(self, k):
        links, own = self.links, self.own
        self.add_twin(k)
        if k == 2:
            for i, to in ((0, 1), (1, 3)):
                self.sent[i] = links.send(
                    own.at[2, pl.ds(128 * i, 128)], self.far.at[i], self.ring_sems.at[i], links.at(dy=to)
                )
        elif k:
            i = 0 if k == 1 else 1
            half = pl.ds(128 * i, 128)
            self.sent[i].wait_recv()
            own[k, half, :] = (own[k, half, :].astype(F32) + self.far[i].astype(F32)).astype(BF)
            self.sent[3 - i] = links.send(own.at[k], self.near.at[1 - i], self.ring_sems.at[3 - i], links.at(dy=k))

    def total(self):
        for i in (0, 1):
            self.sent[2 + i].wait_recv()
        return self.own[0].astype(F32) + self.near[0].astype(F32) + self.near[1].astype(F32)


def expert_kernel(
    w_all, x_all, c_all, gates_all, router_all, gx_out, mix_out, dw_out, router_out, *rest
):
    w, gates, router, xs, cs, hidden, d_gate, d_up, d_logit, staged = rest[:10]
    grads, mixes = rest[10:17], rest[17:21]
    send_sems, load_sems, dw_sems, local_sems = rest[21:]
    links = Links(send_sems, local_sems)
    yh, _, _, c, t = links.me
    y = yh * 2 + t
    tables = [links.keep(w_all, w), links.keep(gates_all, gates), links.keep(router_all, router)]
    loads = {}
    for k in (2, 1, 3, 0):
        for core in (1, 0):
            b = up4(y, k) * 2 + up2(c, core)
            for n, (src, dst) in enumerate(((x_all, xs), (c_all, cs))):
                copy = pltpu.make_async_copy(src.at[b], dst.at[rows_of(b), :], load_sems.at[(k * 2 + core) * 2 + n])
                copy.start()
                loads[(k, core, n)] = copy
    links.barrier([links.at(**p) for p in RING + TWIN])
    lane = lax.broadcasted_iota(jnp.int32, (OWN, 128), 1)
    mine = (lane == y * 2 + c).astype(F32)
    grad_sum, mix_sum = RingSum(links, *grads), RingSum(links, *mixes[:3], None, None, mixes[3], None)

    def one_block(b, grad, mix):
        rows = rows_of(b)
        xb, cb = xs[rows, :], cs[rows, :]
        table = jnp.concatenate([gates[b], jnp.zeros((120, OWN), F32)], axis=0).T
        gate = jnp.sum(table * mine, axis=1, keepdims=True)
        grad_gate = jnp.zeros((OWN, 1), F32)
        for n in range(3):
            columns = slice(256 * n, 256 * (n + 1))
            gate_in = nn(xb, w[0, :, columns])
            up_in = nn(xb, w[1, :, columns])
            back = nn(cb, w[2, :, columns])
            sig = 0.5 * jnp.tanh(0.5 * gate_in) + 0.5
            act = gate_in * sig
            hid = act * up_in
            grad_gate = grad_gate + jnp.sum(hid * back, axis=1, keepdims=True)
            grad_hidden = gate * back
            hidden[rows, columns] = (gate * hid).astype(BF)
            d_gate[rows, columns] = (grad_hidden * up_in * (sig + act * (1.0 - sig))).astype(BF)
            d_up[rows, columns] = (grad_hidden * act).astype(BF)
        dl = (gate * grad_gate * (mine - table)).astype(BF)
        d_logit[rows, :] = dl
        dg, du, hw = d_gate[rows, :], d_up[rows, :], hidden[rows, :]
        for n in range(6):
            columns = slice(256 * n, 256 * (n + 1))
            grad[:, columns] = (
                nt(dg, w[0, columns, :]) + nt(du, w[1, columns, :]) + nt(dl, router[columns, :])
            ).astype(BF)
            mix[:, columns] = nt(hw, w[2, columns, :]).astype(BF)

    for copy in tables:
        copy.wait()
    mixed = []

    def mix_done(k):
        mix_sum.add_twin(k)
        return links.keep(mix_sum.own.at[k], mix_out.at[k])

    done = None
    for k in ORDER:
        for core in (1, 0):
            loads[(k, core, 0)].wait()
            loads[(k, core, 1)].wait()
            b = up4(y, k) * 2 + up2(c, core)
            one_block(b, grad_sum.place(k, core), mix_sum.place(k, core))
            if core:
                grad_sum.to_twin(k)
                mix_sum.to_twin(k)
                if done is not None:
                    grad_sum.pass_on(done)
                    mixed.append(mix_done(done))
        done = k
    grad_sum.pass_on(0)
    mixed.append(mix_done(0))

    def strip(i, carry):
        columns = rows_of(i)
        xt = xs[:, columns]
        slot = lax.rem(i, 2)

        def stored(n, at):
            return pltpu.make_async_copy(staged.at[slot, n], dw_out.at[n, rows_of(at)], dw_sems.at[slot * 3 + n])

        @pl.when(i >= 2)
        def _():
            for n in range(3):
                stored(n, i - 2).wait()

        for n, (left, right) in enumerate(((xt, d_gate), (xt, d_up), (cs[:, columns], hidden))):
            staged[slot, n] = tn(left, right[...]).astype(BF)
        router_out[:, columns] = tn(d_logit[...], xt)[:8, :]
        for n in range(3):
            stored(n, i).start()
        return carry

    lax.fori_loop(0, 6, strip, 0)
    gx_out[...] = grad_sum.total()
    for copy in mixed:
        copy.wait()
    for slot in range(2):
        for n in range(3):
            pltpu.make_async_copy(staged.at[slot, n], dw_out.at[n, rows_of(4 + slot)], dw_sems.at[slot * 3 + n]).wait()
    links.finish()


def run_expert(w, x_all, c_all, gates, router):
    return pl.pallas_call(
        expert_kernel,
        out_shape=(
            jax.ShapeDtypeStruct((OWN, D), F32),
            jax.ShapeDtypeStruct((4, OWN, D), BF),
            jax.ShapeDtypeStruct((3, D, HALF), BF),
            jax.ShapeDtypeStruct((8, D), F32),
        ),
        in_specs=[ANY] * 5,
        out_specs=(VMEM, ANY, ANY, VMEM),
        scratch_shapes=[
            pltpu.VMEM((3, D, HALF), BF),
            pltpu.VMEM((8, 8, OWN), F32),
            pltpu.VMEM((D, WIDE - PART), BF),
            pltpu.VMEM((8 * OWN, D), BF),
            pltpu.VMEM((8 * OWN, D), BF),
            pltpu.VMEM((8 * OWN, HALF), BF),
            pltpu.VMEM((8 * OWN, HALF), BF),
            pltpu.VMEM((8 * OWN, HALF), BF),
            pltpu.VMEM((8 * OWN, 128), BF),
            pltpu.VMEM((2, 3, OWN, HALF), BF),
        ]
        + RingSum.SCRATCH
        + RingSum.SCRATCH[:3]
        + RingSum.SCRATCH[5:6]
        + [pltpu.SemaphoreType.DMA((n,)) for n in (24, 16, 6, 7)],
        compiler_params=pltpu.CompilerParams(
            collective_id=5, has_side_effects=True, vmem_limit_bytes=60 * MIB
        ),
        name="expert",
    )(w, x_all, c_all, gates, router)


def plane_reduce(links, h, ops, sems):
    def target(k, stage):
        return links.at(dx=k) if (h == 0) == (stage == 1) else links.at(dz=k)

    for stage in (0, 1):
        base = 4 * stage
        far, near = {}, {}
        for i, k in ((0, 1), (1, 3)):
            far[i] = links.send(ops.far(stage, i), ops.far_land(stage, i), sems.at[base + i], target(k, stage))
        yield
        for i, k in ((0, 1), (1, 3)):
            ops.ready(stage, k)
            far[i].wait_recv()
            ops.add_far(stage, i, k)
            near[i] = links.send(
                ops.near(stage, k), ops.near_land(stage, 1 - i), sems.at[base + 3 - i], target(k, stage)
            )
        yield
        ops.ready(stage, 0)
        for i in (0, 1):
            near[i].wait_recv()
        ops.total(stage)
    yield


def loop(counts, fn):
    a, b = counts

    def body(i, carry):
        fn(lax.div(i, b), lax.rem(i, b))
        return carry

    lax.fori_loop(0, a * b, body, 0)


SLOT = {1: 0, 3: 1, 0: 2}


class ExpertOps:
    SCRATCH = [
        pltpu.VMEM((2, 3, 3, 4, 48, HALF), BF),
        pltpu.VMEM((2, 2, 3, 4, 48, 384), BF),
        pltpu.VMEM((2, 2, 3, 4, 48, HALF), BF),
        pltpu.VMEM((2, 4, 3, 48, HALF), BF),
        pltpu.VMEM((2, 2, 3, 48, 384), BF),
        pltpu.VMEM((2, 2, 3, 48, HALF), BF),
        pltpu.VMEM((2, 2, 3, 24, HALF), BF),
    ]

    def __init__(self, links, h, g, acc, far1, near1, mid, far2, near2, last):
        self.h, self.g, self.acc, self.far1, self.near1 = h, g, acc, far1, near1
        self.mid, self.far2, self.near2, self.last = mid, far2, near2, last
        _, self.x, self.z, _, _ = links.me
        self.loads = {k: links.keep(self.block(k), acc.at[h, SLOT[k]]) for k in (1, 3, 0)}

    def block(self, k, *columns):
        if self.h == 0:
            return self.g.at[(slice(None), 0, slice(None), up4(self.z, k), slice(None)) + columns]
        return self.g.at[(slice(None), 1, up4(self.x, k), slice(None), slice(None)) + columns]

    def ready(self, stage, k):
        if stage == 0:
            self.loads[k].wait()

    def far(self, stage, i):
        columns = pl.ds(384 * i, 384)
        return self.mid.at[self.h, 2, :, :, columns] if stage else self.block(2, columns)

    def far_land(self, stage, i):
        return (self.far2 if stage else self.far1).at[self.h, i]

    def near(self, stage, k):
        return self.mid.at[self.h, k] if stage else self.acc.at[self.h, SLOT[k]]

    def near_land(self, stage, i):
        return (self.near2 if stage else self.near1).at[self.h, i]

    def add_far(self, stage, i, k):
        h, columns = self.h, slice(384 * i, 384 * (i + 1))

        def first(m, a):
            s = SLOT[k]
            self.acc[h, s, m, a, :, columns] = (
                self.acc[h, s, m, a, :, columns].astype(F32) + self.far1[h, i, m, a].astype(F32)
            ).astype(BF)

        def second(m, _):
            self.mid[h, k, m, :, columns] = (
                self.mid[h, k, m, :, columns].astype(F32) + self.far2[h, i, m].astype(F32)
            ).astype(BF)

        loop((3, 1) if stage else (3, 4), second if stage else first)

    def total(self, stage):
        h = self.h
        here = self.x if h == 0 else self.z

        def first(k, m):
            a = up4(here, k)
            self.mid[h, k, m] = (
                self.acc[h, 2, m, a].astype(F32)
                + self.near1[h, 0, m, a].astype(F32)
                + self.near1[h, 1, m, a].astype(F32)
            ).astype(BF)

        def second(m, _):
            value = (
                self.mid[h, 0, m].astype(F32)
                + self.near2[h, 0, m].astype(F32)
                + self.near2[h, 1, m].astype(F32)
            )
            self.last[h, 0, m] = value[:24, :].astype(BF)
            self.last[h, 1, m] = value[24:, :].astype(BF)

        loop((3, 1) if stage else (4, 3), second if stage else first)


def attention_scratch(width):
    return [
        pltpu.VMEM((2, 2, 2, 4, 4, 48, width), BF),
        pltpu.VMEM((2, 4, 2, 4, 48, width), BF),
        pltpu.VMEM((2, 2, 4, 48, width), BF),
        pltpu.VMEM((2, 2, 2, 4, 48, width), BF),
        pltpu.VMEM((2, 4, 2, 48, width), BF),
        pltpu.VMEM((2, 2, 48, width), BF),
        pltpu.VMEM((2, 2, 2, 48, width), BF),
        pltpu.VMEM((2, 2, 48, width), BF),
    ]


class AttentionOps:
    def __init__(self, links, h, twin_sems, g, twin, far1, near1, mid, far2, near2, last):
        self.h, self.g, self.twin, self.far1, self.near1 = h, g, twin, far1, near1
        self.mid, self.far2, self.near2, self.last = mid, far2, near2, last
        _, self.x, self.z, self.c, _ = links.me
        self.twins = {}
        for k in (2, 1, 3, 0):
            self.twins[k] = links.send(
                self.block(1 - self.c, k), twin.at[h, k], twin_sems.at[h * 4 + k], links.at(dc=1)
            )

    def place(self, k):
        return up4(self.z if self.h == 0 else self.x, k)

    def block(self, core, k):
        if self.h == 0:
            return self.g.at[0, core, :, :, self.place(k)]
        return self.g.at[1, core, :, self.place(k)]

    def get(self, k, i, a):
        return self.g[0, self.c, i, a, self.place(k)] if self.h == 0 else self.g[1, self.c, i, self.place(k), a]

    def put(self, k, i, a, value):
        if self.h == 0:
            self.g[0, self.c, i, a, self.place(k)] = value.astype(BF)
        else:
            self.g[1, self.c, i, self.place(k), a] = value.astype(BF)

    def add_twin(self, k):
        self.twins[k].wait_recv()

        def add(i, a):
            self.put(k, i, a, self.get(k, i, a).astype(F32) + self.twin[self.h, k, i, a].astype(F32))

        loop((2, 4), add)

    def ready(self, stage, k):
        if stage == 0:
            self.add_twin(k)

    def far(self, stage, i):
        if stage:
            return self.mid.at[self.h, 2, i]
        if i == 0:
            self.add_twin(2)
        if self.h == 0:
            return self.g.at[0, self.c, i, :, self.place(2)]
        return self.g.at[1, self.c, i, self.place(2)]

    def far_land(self, stage, i):
        return (self.far2 if stage else self.far1).at[self.h, i]

    def near(self, stage, k):
        return self.mid.at[self.h, k] if stage else self.block(self.c, k)

    def near_land(self, stage, i):
        return (self.near2 if stage else self.near1).at[self.h, i]

    def add_far(self, stage, i, k):
        h = self.h
        if stage:
            self.mid[h, k, i] = (self.mid[h, k, i].astype(F32) + self.far2[h, i].astype(F32)).astype(BF)
            return

        def add(a, _):
            self.put(k, i, a, self.get(k, i, a).astype(F32) + self.far1[h, i, a].astype(F32))

        loop((4, 1), add)

    def total(self, stage):
        h = self.h
        here = self.x if h == 0 else self.z

        def first(k, i):
            a = up4(here, k)
            self.mid[h, k, i] = (
                self.get(0, i, a).astype(F32)
                + self.near1[h, 0, i, a].astype(F32)
                + self.near1[h, 1, i, a].astype(F32)
            ).astype(BF)

        def second(i, _):
            self.last[h, i] = (
                self.mid[h, 0, i].astype(F32)
                + self.near2[h, 0, i].astype(F32)
                + self.near2[h, 1, i].astype(F32)
            ).astype(BF)

        loop((2, 1) if stage else (4, 2), second if stage else first)


def backward_kernel(
    g, w_in, w_out, mix, gx,
    cot_in, tok_in, residual_in, normed_in, q_in, k_in, v_in, att_in, cosine_in, sine_in, gains_in, router_in,
    ge, grad_input, layer_output, ga_in, ga_out, small_out, *rest
):
    expert_refs, in_refs, out_refs = rest[:7], rest[7:15], rest[15:23]
    inputs = rest[23:34]
    cot, residual, normed, q, k, v, att, cosine, sine, gains, router = inputs
    (
        wqkv, flow, grad_residual, grad_branch, lin, kv_own, kv_send, kv_recv,
        ring_in, ring_out, swap_in_out, swap_in_in, swap_out_out, swap_out_in,
        small, s_twin, s_land, s_back, mix_far, mix_near,
    ) = rest[34:54]
    (
        send_sems, local_sems, expert_sems, in_sems, out_sems, in_twin_sems, out_twin_sems, back_sems, kv_sems,
        ring_sems, swap_sems, small_sems, mix_sems,
    ) = rest[54:]
    links = Links(send_sems, local_sems)
    yh, x, z, c, t = links.me
    twin = links.at(dc=1)
    loads = [
        links.keep(src, dst)
        for src, dst in zip(
            (gx, cot_in, residual_in, gains_in, normed_in, q_in, k_in, v_in, att_in, cosine_in, sine_in, router_in),
            (flow, cot, residual, gains, normed, q, k, v, att, cosine, sine, router),
        )
    ]
    out_load = links.keep(w_out.at[0], wqkv.at[:, :, :, pl.ds(0, 384)])
    links.barrier([links.at(**p) for p in ALONG + RING + CROSS + TWIN])
    reduce_experts = [
        plane_reduce(links, h, ExpertOps(links, h, g, *expert_refs), expert_sems.at[pl.ds(8 * h, 8)])
        for h in (0, 1)
    ]

    def step(group, count=1):
        for _ in range(count):
            for steps in group:
                next(steps, None)

    step(reduce_experts)
    mix_sent = {}
    for i, to in ((0, 1), (1, 3)):
        mix_sent[i] = links.send(
            mix.at[2, pl.ds(128 * i, 128)], mix_far.at[i], mix_sems.at[i], links.at(dy=to)
        )
        keep = 1 - i
        mix_sent[2 + i] = links.send(
            mix.at[to, pl.ds(128 * keep, 128)], mix_near.at[i, pl.ds(128 * keep, 128)], mix_sems.at[2 + i],
            links.at(dy=to),
        )

    for copy in loads[:4]:
        copy.wait()
    scaled = flow[...] * gains[1:2, :]
    value = residual[...]
    inverse = inverse_norm(value)
    mean = jnp.mean(scaled * value, axis=1, keepdims=True)
    grad = cot[...].astype(F32) + inverse * scaled - value * (inverse * inverse * inverse * mean)
    gain_two = jnp.sum(flow[...] * (value * inverse), axis=0, keepdims=True)
    grad_residual[...] = grad
    grad_branch[...] = grad.astype(BF)
    mix_load = [links.keep(mix.at[to, pl.ds(at, 128)], cot.at[pl.ds(at, 128)]) for to, at in ((1, 0), (3, 128))]
    for copy in loads[4:]:
        copy.wait()
    bias = causal_bias(t)
    cos_own, sin_own = cosine[...], sine[...]

    def weight_rows(left, right, store):
        for i in (0, 1):
            for half in (0, 1):
                first = HALF * i + 384 * half
                rows = tn(left[:, first : first + 384], right)
                store(i, slice(2 * half, 2 * half + 2), rows.reshape(2, 4, 48, rows.shape[1]).astype(BF))

    def start(refs, twin_sems, sems, group):
        j = len(group)
        ops = AttentionOps(links, j, twin_sems, *refs)
        group.append(plane_reduce(links, j, ops, sems.at[pl.ds(8 * j, 8)]))

    reduce_out, reduce_in = [], []
    for j in (0, 1):

        def store_out(i, at, value, j=j):
            for half in (0, 1):
                out_refs[0][j, half, i, at] = value[..., 384 * half : 384 * (half + 1)]

        weight_rows(grad_branch, att[j], store_out)
        start(out_refs, out_twin_sems, out_sems, reduce_out)
    step(reduce_out)
    tok_load = [links.keep(tok_in.at[:, pl.ds(HALF * i, HALF)], att.at[i]) for i in (0, 1)]

    exchanges = []
    for j in (0, 1):
        out_load.wait()
        grad_att = jnp.concatenate(
            [
                nn(grad_branch[:, :HALF], wqkv[half, 0, :, :384])
                + nn(grad_branch[:, HALF:], wqkv[half, 1, :, :384])
                for half in (0, 1)
            ],
            axis=1,
        ).astype(BF)
        if j == 0:
            out_load = links.keep(w_out.at[1], wqkv.at[:, :, :, pl.ds(0, 384)])
        else:
            in_load = links.keep(w_in.at[0], wqkv)
        kj, vj = k[j], v[j]
        gk = jnp.zeros((SEQ, HD), F32)
        gv = jnp.zeros((SEQ, HD), F32)
        for h in range(6):
            lanes = slice(HD * h, HD * (h + 1))
            qh, gh = q[j, :, lanes], grad_att[:, lanes]
            scores = nt(qh, kj) * SCALE + bias
            raised = jnp.exp(scores - jnp.max(scores, axis=1, keepdims=True))
            exact = raised * (1.0 / jnp.sum(raised, axis=1, keepdims=True))
            grad_probs = nt(gh, vj)
            centred = jnp.sum(exact * grad_probs, axis=1, keepdims=True)
            grad_scores = (exact * (grad_probs - centred)).astype(BF)
            lin[j, :, lanes] = unroped(nn(grad_scores, kj) * SCALE, cos_own, sin_own).astype(BF)
            gk = gk + tn(grad_scores, qh)
            gv = gv + tn(exact.astype(BF), gh)
            if (j, h) in ((0, 2), (1, 1), (1, 4)):
                step(reduce_out)
            if (j, h) == (0, 2):
                step(reduce_experts)
        both = jnp.concatenate([gk * SCALE, gv], axis=1)
        low, high = both[:OWN, :], both[OWN:, :]
        kv_own[j] = jnp.where(t == 0, low, high)
        kv_send[j] = jnp.where(t == 0, high, low).astype(BF)
        exchanges.append(links.send(kv_send.at[j], kv_recv.at[j], kv_sems.at[j], links.flip(dt=1)))
        if j == 0:
            for copy in mix_load:
                copy.wait()
            for i, to in ((0, 1), (1, 3)):
                mix_sent[i].wait_recv()
                half = pl.ds(128 * i, 128)
                cot[half, :] = (cot[half, :].astype(F32) + mix_far[i].astype(F32)).astype(BF)
                mix_sent[4 + i] = links.send(
                    cot.at[half], mix_near.at[i, half], mix_sems.at[4 + i], links.at(dy=to)
                )

    for j in (0, 1):
        exchanges[j].wait_recv()
        total = kv_own[j] + kv_recv[j].astype(F32)
        lin[j, :, HALF:PART] = unroped(total[:, :HD], cos_own, sin_own).astype(BF)
        lin[j, :, PART:] = total[:, HD:].astype(BF)

        def store_in(i, at, value, j=j):
            for half in (0, 1):
                in_refs[0][j, half, i, at] = value[..., 512 * half : 512 * (half + 1)]

        weight_rows(normed, lin[j], store_in)
        start(in_refs, in_twin_sems, in_sems, reduce_in)
        in_load.wait()
        for i in (0, 1):
            columns = slice(HALF * i, HALF * (i + 1))
            part = nt(lin[j, :, :512], wqkv[0, i]) + nt(lin[j, :, 512:], wqkv[1, i])
            flow[:, columns] = part if j == 0 else flow[:, columns] + part
        if j == 0:
            in_load = links.keep(w_in.at[1], wqkv)
        next(reduce_in[j])
    mix_last = links.keep(mix.at[0], normed)
    for copy in tok_load:
        copy.wait()

    gradient = flow[...]
    scaled = gradient * gains[0:1, :]
    value = jnp.concatenate([att[0], att[1]], axis=1).astype(F32)
    inverse = inverse_norm(value)
    mean = jnp.mean(scaled * value, axis=1, keepdims=True)
    grad_branch[...] = (
        grad_residual[...] + inverse * scaled - value * (inverse * inverse * inverse * mean)
    ).astype(BF)
    results = [links.keep(grad_branch, grad_input)]
    gain_one = jnp.sum(gradient * (value * inverse), axis=0, keepdims=True)
    rows = jnp.concatenate([router[...], gain_one, gain_two, jnp.zeros((6, D), F32)], axis=0)
    small[0] = rows[:, :HALF]
    small[1] = rows[:, HALF:]
    s_copy = links.send(small.at[1 - c], s_twin, small_sems.at[0], twin)
    step(reduce_experts)
    step(reduce_out)
    step(reduce_in)
    s_copy.wait_recv()
    small[c] = small[c] + s_twin[...]

    def everyone(axis, at):
        copies = {}
        for k in (1, 2, 3):
            j = 4 - k
            copies[j] = links.send(
                small.at[c], s_land.at[at, j - 1], small_sems.at[3 * at + j], links.at(**{axis: k})
            )
        return copies

    def settle(copies, at):
        for copy in copies.values():
            copy.wait_recv()
            links.left(copy)
        small[c] = small[c] + s_land[at, 0] + s_land[at, 1] + s_land[at, 2]

    def around(refs, ring, base):
        copies = []
        for dyh, dt in ((1, 1), (1, 0), (0, 1)):
            index = dyh * 2 + dt - 1
            copies.append(
                links.send(
                    refs[7].at[up2(t, dt), up2(yh, dyh)], ring.at[index], ring_sems.at[base + index],
                    links.flip(dyh=dyh, dt=dt),
                )
            )
        return copies

    def collect(copies, refs, ring, out, theirs, mine, at):
        for copy in copies:
            copy.wait_recv()
        total = refs[7][t, yh].astype(F32)
        for i in range(3):
            total = total + ring[i].astype(F32)
        theirs[...] = jnp.where(c == 0, total[24:, :], total[:24, :])
        swap = links.send(theirs, mine, swap_sems.at[at], twin)
        out[c] = jnp.where(c == 0, total[:24, :], total[24:, :])
        return swap

    copies = everyone("dz", 0)
    out_around = around(out_refs, ring_out, 0)
    step(reduce_experts)
    for n in (2, 3, 4, 5):
        mix_sent[n].wait_recv()
    mix_last.wait()
    normed[...] = (
        residual[...] + normed[...].astype(F32) + mix_near[0].astype(F32) + mix_near[1].astype(F32)
    ).astype(BF)
    results.append(links.keep(normed, layer_output))
    settle(copies, 0)
    copies = everyone("dx", 1)
    out_swap = collect(out_around, out_refs, ring_out, ga_out, swap_out_out, swap_out_in, 0)
    step(reduce_in)
    step(reduce_experts)

    last, slot, back = expert_refs[6], (yh * 2 + t) * 2 + c, []
    for dyh in range(2):
        for dt in range(2):
            for dc in range(2):
                columns = pl.ds(pl.multiple_of(up2(t, dt) * 384, 384), 384)
                src = last.at[up2(yh, dyh), up2(c, dc), :, :, columns]
                if dyh + dt + dc == 0:
                    stay = links.keep(src, ge.at[slot])
                else:
                    index = (dyh * 2 + dt) * 2 + dc
                    back.append(
                        links.send(src, ge.at[slot], back_sems.at[index], links.flip(dyh=dyh, dt=dt, dc=dc))
                    )

    settle(copies, 1)
    copies = everyone("dy", 2)
    step(reduce_in)
    settle(copies, 2)
    s_copy = links.send(small.at[c], s_back, small_sems.at[10], twin)
    step(reduce_in)
    in_around = around(in_refs, ring_in, 3)
    s_copy.wait_recv()
    small_out[c] = small[c]
    small_out[1 - c] = s_back[...]
    in_swap = collect(in_around, in_refs, ring_in, ga_in, swap_in_out, swap_in_in, 1)
    for copy in back:
        copy.wait_recv()
    for copy in results + [stay]:
        copy.wait()
    out_swap.wait_recv()
    ga_out[1 - c] = swap_out_in[...]
    in_swap.wait_recv()
    ga_in[1 - c] = swap_in_in[...]
    links.finish()


def backward(*args):
    staged = args[5:6] + args[7:]
    return pl.pallas_call(
        backward_kernel,
        out_shape=(
            jax.ShapeDtypeStruct((8, 3, 24, 384), BF),
            jax.ShapeDtypeStruct((OWN, D), BF),
            jax.ShapeDtypeStruct((OWN, D), BF),
            jax.ShapeDtypeStruct((2, 24, 512), F32),
            jax.ShapeDtypeStruct((2, 24, 384), F32),
            jax.ShapeDtypeStruct((2, 16, HALF), F32),
        ),
        in_specs=[ANY] * len(args),
        out_specs=(ANY,) * 3 + (VMEM,) * 3,
        scratch_shapes=ExpertOps.SCRATCH
        + attention_scratch(512)
        + attention_scratch(384)
        + [pltpu.VMEM(v.shape, v.dtype) for v in staged]
        + [
            pltpu.VMEM((2, 2, HALF, 512), BF),
            pltpu.VMEM((OWN, D), F32),
            pltpu.VMEM((OWN, D), F32),
            pltpu.VMEM((OWN, D), BF),
            pltpu.VMEM((2, OWN, WIDE), BF),
            pltpu.VMEM((2, OWN, 2 * HD), F32),
            pltpu.VMEM((2, OWN, 2 * HD), BF),
            pltpu.VMEM((2, OWN, 2 * HD), BF),
            pltpu.VMEM((3, 48, 512), BF),
            pltpu.VMEM((3, 48, 384), BF),
            pltpu.VMEM((24, 512), F32),
            pltpu.VMEM((24, 512), F32),
            pltpu.VMEM((24, 384), F32),
            pltpu.VMEM((24, 384), F32),
            pltpu.VMEM((2, 16, HALF), F32),
            pltpu.VMEM((16, HALF), F32),
            pltpu.VMEM((3, 3, 16, HALF), F32),
            pltpu.VMEM((16, HALF), F32),
            pltpu.VMEM((2, OWN // 2, D), BF),
            pltpu.VMEM((2, OWN, D), BF),
        ]
        + [pltpu.SemaphoreType.DMA((n,)) for n in (112, 40, 16, 16, 16, 8, 8, 8, 2, 6, 2, 11, 6)],
        compiler_params=pltpu.CompilerParams(
            collective_id=6, has_side_effects=True, vmem_limit_bytes=60 * MIB
        ),
        name="backward",
    )(*args)


def rope_tables():
    half_size = HD // 2
    exponent = -(np.float32(2.0) * np.arange(half_size, dtype=np.float32)) / np.float32(HD)
    frequency = np.power(np.float32(ROPE_BASE), exponent, dtype=np.float32)
    angles = np.arange(SEQ, dtype=np.float32)[:, None] * frequency[None, :]
    cosine, sine = np.cos(angles), np.sin(angles)
    return np.concatenate([cosine, cosine], axis=1), np.concatenate([-sine, sine], axis=1)


def shards(
    tokens_in, routes, cotangent, attn_gain, query_proj, key_proj, value_proj, output_proj,
    ffn_gain, router_proj, expert_gate, expert_up, expert_down,
):
    d, t = lax.axis_index("dp"), lax.axis_index("tensor")
    blank = jnp.zeros((24, 128), BF)
    extra = jnp.concatenate([router_proj, attn_gain[:, None], ffn_gain[:, None], blank[:, 10:]], axis=1)
    a_in = jnp.stack(
        [
            jnp.concatenate([query_proj[:, :512], extra], axis=1),
            jnp.concatenate([query_proj[:, 512:], key_proj, value_proj, blank], axis=1),
        ]
    )
    a_out = jnp.stack([output_proj[:, :384], output_proj[:, 384:]])
    e_block = jnp.stack([expert_gate, expert_up, expert_down]).transpose(2, 0, 1, 3)
    own_routes = lax.dynamic_slice(routes, (OWN * t, 0), (OWN, 4))
    chosen = jnp.any(own_routes[:, :, None] == jnp.arange(128)[None, None, :], axis=1).astype(F32)
    cosine, sine = (jnp.asarray(v) for v in rope_tables())
    (
        w_in, w_out, router, experts, tok_all, cot_all, gates, normed, queries, keys, values, attended, residual, gains
    ) = forward(a_in, a_out, e_block, tokens_in, cotangent, chosen, cosine, sine)
    flow, mixture, grad_experts, grad_router = run_expert(
        experts.reshape(3, D, HALF), tok_all, cot_all, gates, router.reshape(D, 128)
    )
    ge, grad_input, layer_output, ga_in, ga_out, small = backward(
        grad_experts.reshape(3, 2, 4, 4, 48, HALF), w_in.reshape(2, 2, 2, HALF, 512), w_out.reshape(2, 2, 2, HALF, 384), mixture, flow, cotangent, tokens_in, residual,
        normed, queries, keys, values, attended,
        lax.dynamic_slice(cosine, (OWN * t, 0), (OWN, HD)), lax.dynamic_slice(sine, (OWN * t, 0), (OWN, HD)),
        gains, grad_router,
    )
    ge = ge.astype(F32).transpose(1, 2, 0, 3)
    small = jnp.concatenate([small[0], small[1]], axis=1)
    small = lax.dynamic_slice(small, (0, 24 * d + 12 * t), (16, 12))
    return (
        layer_output,
        grad_input,
        small[8],
        jnp.concatenate([ga_in[0], ga_in[1, :, :256]], axis=1),
        ga_in[1, :, 256:384],
        ga_in[1, :, 384:],
        jnp.concatenate([ga_out[0], ga_out[1]], axis=1),
        small[9],
        small[:8].T,
        ge[0],
        ge[1],
        ge[2],
    )


def solution(mesh):
    return jax.shard_map(
        shards,
        mesh=mesh,
        in_specs=(
            P(("dp", "tensor"), None),
            P("dp", None),
            P(("dp", "tensor"), None),
            P("dp"),
            P("dp", "tensor"),
            P("dp", "tensor"),
            P("dp", "tensor"),
            P("dp", "tensor"),
            P("dp"),
            P("dp", None),
            P("dp", None, "tensor"),
            P("dp", None, "tensor"),
            P("dp", None, "tensor"),
        ),
        out_specs=(
            P(("dp", "tensor"), None),
            P(("dp", "tensor"), None),
            P(("dp", "tensor")),
            P("dp", "tensor"),
            P("dp", "tensor"),
            P("dp", "tensor"),
            P("dp", "tensor"),
            P(("dp", "tensor")),
            P(("dp", "tensor"), None),
            P("dp", None, "tensor"),
            P("dp", None, "tensor"),
            P("dp", None, "tensor"),
        ),
        check_vma=False,
    )
```

```python
import functools

import jax
import jax.numpy as jnp
import numpy as np
from jax import lax
from jax.experimental import pallas as pl
from jax.experimental.pallas import tpu as pltpu
from jax.sharding import PartitionSpec as P

HD = 128
E = 8
D = 1536
SEQ = 512
OWN = 256
HALF = 768
PART = 896
WIDE = 1024
NORM_EPSILON = 1e-06
ROPE_BASE = 1000000.0
SCALE = HD ** (-0.5)
MESH = pl.DeviceIdType.MESH
BF = jnp.bfloat16
F32 = jnp.float32
ANY = pl.BlockSpec(memory_space=pl.ANY)
VMEM = pl.BlockSpec(memory_space=pltpu.VMEM)
MIB = 1 << 20


def place():
    d = lax.axis_index("dp")
    t = lax.axis_index("tensor")
    c = lax.rem(d, 2)
    z = lax.rem(lax.div(d, 2), 4)
    x = lax.rem(lax.div(d, 8), 4)
    yh = lax.div(d, 32)
    return yh, x, z, c, t


def device(yh, x, z, c, t):
    return (((yh * 4 + x) * 4 + z) * 2 + c, t)


def up4(v, k):
    return lax.rem(v + k, 4)


def up2(v, k):
    return lax.rem(v + k, 2)


def rows_of(b, size=OWN):
    return pl.ds(pl.multiple_of(b * size, size), size)


def nn(a, b):
    return jnp.dot(a, b, preferred_element_type=F32)


def nt(a, b):
    return lax.dot_general(a, b, (((1,), (1,)), ((), ())), preferred_element_type=F32)


def tn(a, b):
    return lax.dot_general(a, b, (((0,), (0,)), ((), ())), preferred_element_type=F32)


class Links:
    def __init__(self, send_sems, local_sems):
        self.me = place()
        self.send_sems, self.local_sems = send_sems, local_sems
        self.sent, self.local, self.count = [], [], 0

    def at(self, dy=0, dx=0, dz=0, dc=0):
        yh, x, z, c, t = self.me
        y = up4(yh * 2 + t, dy)
        return device(lax.div(y, 2), up4(x, dx), up4(z, dz), up2(c, dc), lax.rem(y, 2))

    def flip(self, dyh=0, dt=0, dc=0):
        yh, x, z, c, t = self.me
        return device(up2(yh, dyh), x, z, up2(c, dc), up2(t, dt))

    def barrier(self, partners):
        sem = pltpu.get_barrier_semaphore()
        for partner in partners:
            pl.semaphore_signal(sem, inc=1, device_id=partner, device_id_type=MESH)
        pl.semaphore_wait(sem, len(partners))

    def send(self, src, dst, recv_sem, target):
        copy = pltpu.make_async_remote_copy(
            src_ref=src,
            dst_ref=dst,
            send_sem=self.send_sems.at[self.count],
            recv_sem=recv_sem,
            device_id=target,
            device_id_type=MESH,
        )
        copy.start()
        self.count += 1
        self.sent.append(copy)
        return copy

    def keep(self, src, dst):
        copy = pltpu.make_async_copy(src, dst, self.local_sems.at[len(self.local)])
        copy.start()
        self.local.append(copy)
        return copy

    def left(self, copy):
        copy.wait_send()
        self.sent = [other for other in self.sent if other is not copy]

    def finish(self):
        for copy in self.sent:
            copy.wait_send()


ALONG = [dict(dx=k) for k in (1, 2, 3)] + [dict(dz=k) for k in (1, 2, 3)]
NEAR = [dict(dx=k) for k in (1, 3)] + [dict(dz=k) for k in (1, 3)]
RING = [dict(dy=k) for k in (1, 2, 3)]
CROSS = [dict(dy=k, dc=1) for k in (1, 2, 3)]
TWIN = [dict(dc=1)]


def plane_gather(links, h, own, one, column, sems, arrived):
    got = {}

    def target(second, k):
        return links.at(dx=k) if (h == 0) != second else links.at(dz=k)

    def push(second, src, dst):
        base = 4 if second else 0
        for n, k in ((0, 1), (1, 3)):
            got[(second, 4 - k)] = links.send(src, dst, sems.at[base + 1 - n], target(second, k))

    def take(second, d, view):
        got[(second, d)].wait_recv()
        i, k = (0, 1) if d == 3 else (1, 3)
        ref = view(d, i)
        got[(second, 2, i)] = links.send(ref, ref, sems.at[(4 if second else 0) + 2 + i], target(second, k))

    push(False, own, one(0))
    yield
    for d in (3, 1):
        take(False, d, one)
    yield
    for i in (0, 1):
        got[(False, 2, i)].wait_recv()
    push(True, column(0), column(0))
    arrived(column(0), 0)
    yield
    for d in (3, 1):
        take(True, d, column)
        arrived(column(d), d)
    yield
    for i in (0, 1):
        got[(True, 2, i)].wait_recv()
    arrived(column(2), 2)
    yield


def plane_views(links, base):
    _, x, z, _, _ = links.me

    def views(h):
        here = (x, z) if h == 0 else (z, x)

        def pick(first, second, *i):
            return base(h, first, second, *i) if h == 0 else base(h, second, first, *i)

        def one(d, *i):
            return pick(up4(here[0], d), here[1], *i)

        def column(d, *i):
            return pick(slice(None), up4(here[1], d), *i)

        return one, column

    return views


def ring_gather(links, src, block, sems, arrived):
    got = {}

    def part(ref, i):
        return ref.at[pl.ds(128 * i, 128), :]

    for i in (0, 1):
        for k in (1, 3):
            half = i if k == 1 else 1 - i
            j = 4 - k
            got[(j, half)] = links.send(
                part(src, half), part(block(0), half), sems.at[j * 2 + half], links.at(dy=k)
            )
    yield
    for j, half, k in ((3, 0, 1), (1, 1, 3)):
        got[(j, half)].wait_recv()
        ref = part(block(j), half)
        got[(2, half)] = links.send(ref, ref, sems.at[4 + half], links.at(dy=k))
    yield
    for j, half in ((3, 1), (1, 0)):
        got[(j, half)].wait_recv()
        arrived(block(j), j)
    yield
    for half in (0, 1):
        got[(2, half)].wait_recv()
    arrived(block(2), 2)
    yield


def advance(*groups, count=1):
    for _ in range(count):
        for steps in groups:
            next(steps, None)


def drain(*groups):
    for steps in groups:
        for _ in steps:
            pass


def roped(u, cosine, sine):
    return u * cosine + pltpu.roll(u, 64, 1) * sine


def unroped(u, cosine, sine):
    return u * cosine - pltpu.roll(u, 64, 1) * sine


def causal_bias(t):
    row = lax.broadcasted_iota(jnp.int32, (OWN, SEQ), 0) + OWN * t
    column = lax.broadcasted_iota(jnp.int32, (OWN, SEQ), 1)
    return jnp.where(row >= column, 0.0, -1e30).astype(F32)


def inverse_norm(v):
    return lax.rsqrt(jnp.mean(v * v, axis=1, keepdims=True) + NORM_EPSILON)


def flat(w, j, half, i, lanes):
    block = w[j, half, i, :, :, :, lanes]
    return block.reshape(HALF, block.shape[-1])


def gain_rows(w):
    tables = [flat(w, 0, 0, i, slice(512, 640)).astype(F32).T for i in (0, 1)]
    both = jnp.concatenate(tables, axis=1)
    return both[8:9, :], both[9:10, :]


def forward_kernel(
    a_in, a_out, e, tok, cot, chosen_all, cosine_all, sine_all,
    w_in_out, w_out_out, router_out, e_all, tok_all, cot_all, gates_all, normed_out, q_out, k_out, v_out, att_out, residual_out, gains_out,
    w, wo, a_pair, o_pair, a_own, o_own, e_pair, e_own, pair, normed, tok_two, gates, chosen, cosine, sine,
    send_sems, local_sems, a_sems, ring_sems, plane_sems, twin_sems, o_plane_sems, o_twin_sems, expert_sems, token_sems,
    cot_sems, cot_twin_sems, e_sems, x_sems, x_twin_sems, g_sems, g_twin_sems,
):
    links = Links(send_sems, local_sems)
    yh, x, z, c, t = links.me
    y = yh * 2 + t
    twin = links.at(dc=1)
    links.barrier([links.at(**p) for p in NEAR + RING + CROSS + TWIN])

    groups = ((a_in, a_pair, a_own, w), (a_out, o_pair, o_own, wo))
    kept = [links.keep(src.at[c], two.at[c]) for src, two, _, _ in groups]
    copies = [
        links.send(src.at[1 - c], two.at[c], a_sems.at[n], twin) for n, (src, two, _, _) in enumerate(groups)
    ]
    tables = [links.keep(chosen_all, chosen), links.keep(cosine_all, cosine), links.keep(sine_all, sine)]
    ring, w_kept = {}, []
    for n, (_, two, block, full) in enumerate(groups):
        kept[n].wait()
        copies[n].wait_recv()
        block[...] = jnp.concatenate([two[0].astype(F32), two[1].astype(F32)], axis=0).astype(BF)
        mine = full.at[t, c, yh, x, z]
        for k in (1, 3, 2):
            ring[(n, 4 - k)] = links.send(block, mine, ring_sems.at[n * 4 + 4 - k], links.at(dy=k))
        w_kept.append(links.keep(block, mine))
    columns = pl.ds(pl.multiple_of(t * 384, 384), 384)
    slot = e_pair.at[:, yh, c, :, columns]
    experts = []
    for dy in range(4):
        for dc in range(2):
            src = e.at[up4(y, dy) * 2 + up2(c, dc)]
            if dy + dc == 0:
                e_kept = links.keep(src, slot)
            else:
                index = ((4 - dy) % 4) * 2 + dc
                experts.append(links.send(src, slot, expert_sems.at[index], links.at(dy=dy, dc=dc)))
    kept += [links.keep(tok, pair.at[t]), links.keep(cot, cot_all.at[y * 2 + c])]
    token = links.send(tok, pair.at[t], token_sems.at[0], links.flip(dt=1))
    twins = []

    def cot_arrived(ref, j):
        twins.append(links.send(ref, ref, cot_twin_sems.at[j], twin))

    twins.append(links.send(cot, cot_all.at[y * 2 + c], cot_twin_sems.at[0], twin))
    cots = ring_gather(links, cot, lambda j: cot_all.at[up4(y, j) * 2 + c], cot_sems, cot_arrived)
    advance(cots)

    w_twins = ([], [])

    def spread(n):
        full, twin_n = groups[n][3], (twin_sems, o_twin_sems)[n]

        def base(h, xo, zo, i=slice(None)):
            return full.at[h, c, i, xo, zo]

        views = plane_views(links, base)
        w_kept[n].wait()
        for j in (1, 3, 2):
            ring[(n, j)].wait_recv()
        steps = []
        for h in (0, 1):

            def arrived(ref, d, h=h):
                w_twins[n].append(links.send(ref, ref, twin_n.at[h * 4 + d], twin))

            one, column = views(h)
            sems = (plane_sems, o_plane_sems)[n].at[pl.ds(8 * h, 8)]
            steps.append(plane_gather(links, h, one(0), one, column, sems, arrived))
        advance(*steps)
        return steps

    weights = spread(0)
    out_weights = spread(1)
    e_kept.wait()
    for copy in experts:
        copy.wait_recv()
    for n in range(3):
        for i in range(2):
            e_own[n, i] = jnp.concatenate(
                [e_pair[n, i, 0].astype(F32), e_pair[n, i, 1].astype(F32)], axis=0
            ).astype(BF)
    e_placed = links.keep(e_own, e_all.at[:, :, x, z])

    def e_base(h, xo, zo, i=None):
        if i is None:
            return e_all.at[:, h, xo, zo]
        return e_all.at[:, h, xo, zo, :, pl.ds(384 * i, 384)]

    e_views = plane_views(links, e_base)
    expert = [
        plane_gather(links, h, e_own.at[:, h], *e_views(h), e_sems.at[pl.ds(8 * h, 8)], lambda ref, d: None)
        for h in (0, 1)
    ]
    advance(*weights)
    advance(*out_weights)
    advance(*weights)
    advance(*out_weights)
    e_placed.wait()
    advance(*expert)
    advance(*weights)
    advance(*weights)
    advance(*out_weights)
    token.wait_recv()
    for copy in kept[2:4] + tables:
        copy.wait()
    for copy in w_twins[0]:
        copy.wait_recv()
    w_dumps = [
        links.keep(w.at[:, :, :, :, :, :, pl.ds(0, 512)], w_in_out),
        links.keep(w.at[0, 0, :, :, :, :, pl.ds(512, 128)], router_out),
    ]

    gain_one, gain_two = gain_rows(w)
    gains_out[0:1, :] = gain_one
    gains_out[1:2, :] = gain_two
    gains_out[2:8, :] = jnp.zeros((6, D), F32)
    for i in (0, 1):
        v = pair[i].astype(F32)
        normed[pl.ds(OWN * i, OWN), :] = (v * inverse_norm(v) * gain_one).astype(BF)
    own = rows_of(t)
    normed_out[...] = normed[own, :]
    bias = causal_bias(t)
    cos_own, sin_own = cosine[own, :], sine[own, :]
    residual_out[...] = pair[t].astype(F32)

    def project(source, j, half, lanes):
        return nn(source[:, :HALF], flat(w, j, half, 0, lanes)) + nn(source[:, HALF:], flat(w, j, half, 1, lanes))

    for j in (0, 1):
        k = project(normed, j, 1, slice(256, 384))
        v = project(normed, j, 1, slice(384, 512)).astype(BF)
        q = jnp.concatenate(
            [project(normed_out, j, 0, slice(0, 512)), project(normed_out, j, 1, slice(0, 256))], axis=1
        )
        k = roped(k, cosine[...], sine[...]).astype(BF)
        k_out[j] = k
        v_out[j] = v
        for g in range(6):
            lanes = slice(HD * g, HD * (g + 1))
            qh = roped(q[:, lanes], cos_own, sin_own).astype(BF)
            q_out[j, :, lanes] = qh
            scores = nt(qh, k) * SCALE + bias
            raised = jnp.exp(scores - jnp.max(scores, axis=1, keepdims=True))
            probs = (raised * (1.0 / jnp.sum(raised, axis=1, keepdims=True))).astype(BF)
            att_out[j, :, lanes] = nn(probs, v).astype(BF)
            if (j, g) in ((0, 1), (0, 4)):
                advance(*expert)
            if (j, g) in ((0, 4), (1, 4)):
                advance(cots)
    drain(*out_weights)
    for copy in w_twins[1]:
        copy.wait_recv()
    w_dumps.append(links.keep(wo, w_out_out))
    for i in (0, 1):
        columns = pl.ds(HALF * i, HALF)
        part = residual_out[:, columns]
        for j in (0, 1):
            for half in (0, 1):
                part = part + nt(att_out[j, :, 384 * half : 384 * (half + 1)], flat(wo, j, half, i, slice(0, 384)))
        residual_out[:, columns] = part
    residual = residual_out[...]
    tok_two[...] = (residual * inverse_norm(residual) * gain_two).astype(BF)
    block = tok_all.at[y * 2 + c]
    kept.append(links.keep(tok_two, block))

    def x_arrived(ref, j):
        twins.append(links.send(ref, ref, x_twin_sems.at[j], twin))

    tokens = ring_gather(links, tok_two, lambda j: tok_all.at[up4(y, j) * 2 + c], x_sems, x_arrived)
    advance(tokens)
    twins.append(links.send(tok_two, block, x_twin_sems.at[0], twin))
    lanes = slice(512, 640)
    logits = nn(tok_two[:, :HALF], flat(w, 0, 0, 0, lanes)) + nn(tok_two[:, HALF:], flat(w, 0, 0, 1, lanes))
    masked = jnp.where(chosen[...] > 0.5, logits, -1e30)
    raised = jnp.where(chosen[...] > 0.5, jnp.exp(masked - jnp.max(masked, axis=1, keepdims=True)), 0.0)
    table = raised * (1.0 / jnp.sum(raised, axis=1, keepdims=True))
    gates[...] = table.T[:8, :]
    kept.append(links.keep(gates, gates_all.at[y * 2 + c]))
    gate = {}
    for k in (1, 3, 2):
        gate[4 - k] = links.send(gates, gates_all.at[y * 2 + c], g_sems.at[4 - k], links.at(dy=k))
    twins.append(links.send(gates, gates_all.at[y * 2 + c], g_twin_sems.at[0], twin))
    advance(*expert)
    advance(tokens)
    advance(tokens)
    drain(*expert)
    drain(tokens)
    drain(cots)
    for j in (1, 3, 2):
        gate[j].wait_recv()
        ref = gates_all.at[up4(y, j) * 2 + c]
        twins.append(links.send(ref, ref, g_twin_sems.at[j], twin))
    for copy in twins:
        copy.wait_recv()
    for copy in kept[4:] + w_dumps:
        copy.wait()
    links.finish()


def forward(a_in, a_out, e, tok, cot, chosen, cosine, sine):
    dma = [
        pltpu.SemaphoreType.DMA((n,)) for n in (160, 20, 2, 8, 16, 8, 16, 8, 8, 1, 8, 4, 16, 8, 4, 4, 4)
    ]
    return pl.pallas_call(
        forward_kernel,
        out_shape=(
            jax.ShapeDtypeStruct((2, 2, 2, 4, 4, 48, 512), BF),
            jax.ShapeDtypeStruct((2, 2, 2, 4, 4, 48, 384), BF),
            jax.ShapeDtypeStruct((2, 4, 4, 48, 128), BF),
            jax.ShapeDtypeStruct((3, 2, 4, 4, 48, HALF), BF),
            jax.ShapeDtypeStruct((8, OWN, D), BF),
            jax.ShapeDtypeStruct((8, OWN, D), BF),
            jax.ShapeDtypeStruct((8, 8, OWN), F32),
            jax.ShapeDtypeStruct((OWN, D), BF),
            jax.ShapeDtypeStruct((2, OWN, HALF), BF),
            jax.ShapeDtypeStruct((2, SEQ, HD), BF),
            jax.ShapeDtypeStruct((2, SEQ, HD), BF),
            jax.ShapeDtypeStruct((2, OWN, HALF), BF),
            jax.ShapeDtypeStruct((OWN, D), F32),
            jax.ShapeDtypeStruct((8, D), F32),
        ),
        in_specs=[ANY] * 8,
        out_specs=(ANY,) * 7 + (VMEM,) * 7,
        scratch_shapes=[
            pltpu.VMEM((2, 2, 2, 4, 4, 48, 640), BF),
            pltpu.VMEM((2, 2, 2, 4, 4, 48, 384), BF),
            pltpu.VMEM((2, 24, 640), BF),
            pltpu.VMEM((2, 24, 384), BF),
            pltpu.VMEM((48, 640), BF),
            pltpu.VMEM((48, 384), BF),
            pltpu.VMEM((3, 2, 2, 24, HALF), BF),
            pltpu.VMEM((3, 2, 48, HALF), BF),
            pltpu.VMEM((2, OWN, D), BF),
            pltpu.VMEM((SEQ, D), BF),
            pltpu.VMEM((OWN, D), BF),
            pltpu.VMEM((8, OWN), F32),
            pltpu.VMEM((OWN, 128), F32),
            pltpu.VMEM((SEQ, HD), F32),
            pltpu.VMEM((SEQ, HD), F32),
        ]
        + dma,
        compiler_params=pltpu.CompilerParams(
            collective_id=1, has_side_effects=True, vmem_limit_bytes=60 * MIB
        ),
        name="forward",
    )(a_in, a_out, e, tok, cot, chosen, cosine, sine)


ORDER = (2, 1, 3, 0)


class RingSum:
    SCRATCH = [
        pltpu.VMEM((4, OWN, D), BF),
        pltpu.VMEM((2, OWN, D), BF),
        pltpu.VMEM((4, OWN, D), BF),
        pltpu.VMEM((2, OWN // 2, D), BF),
        pltpu.VMEM((2, OWN, D), BF),
        pltpu.SemaphoreType.DMA((4,)),
        pltpu.SemaphoreType.DMA((4,)),
    ]

    def __init__(self, links, own, theirs, twin, far, near, twin_sems, ring_sems):
        self.links, self.own, self.theirs, self.twin = links, own, theirs, twin
        self.far, self.near, self.twin_sems, self.ring_sems = far, near, twin_sems, ring_sems
        self.twins, self.sent = {}, {}

    def place(self, k, core):
        if not core:
            return self.own.at[k]
        step = ORDER.index(k)
        if step >= 2:
            self.links.left(self.twins[ORDER[step - 2]])
        return self.theirs.at[step % 2]

    def to_twin(self, k):
        self.twins[k] = self.links.send(
            self.theirs.at[ORDER.index(k) % 2], self.twin.at[k], self.twin_sems.at[k], self.links.at(dc=1)
        )

    def add_twin(self, k):
        self.twins[k].wait_recv()
        self.own[k] = (self.own[k].astype(F32) + self.twin[k].astype(F32)).astype(BF)

    def pass_on(self, k):
        links, own = self.links, self.own
        self.add_twin(k)
        if k == 2:
            for i, to in ((0, 1), (1, 3)):
                self.sent[i] = links.send(
                    own.at[2, pl.ds(128 * i, 128)], self.far.at[i], self.ring_sems.at[i], links.at(dy=to)
                )
        elif k:
            i = 0 if k == 1 else 1
            half = pl.ds(128 * i, 128)
            self.sent[i].wait_recv()
            own[k, half, :] = (own[k, half, :].astype(F32) + self.far[i].astype(F32)).astype(BF)
            self.sent[3 - i] = links.send(own.at[k], self.near.at[1 - i], self.ring_sems.at[3 - i], links.at(dy=k))

    def total(self):
        for i in (0, 1):
            self.sent[2 + i].wait_recv()
        return self.own[0].astype(F32) + self.near[0].astype(F32) + self.near[1].astype(F32)


def expert_kernel(
    w_all, x_all, c_all, gates_all, router_all, gx_out, mix_out, dw_out, router_out, *rest
):
    w, gates, router, xs, cs, hidden, d_gate, d_up, d_logit, staged = rest[:10]
    grads, mixes = rest[10:17], rest[17:21]
    send_sems, load_sems, dw_sems, local_sems = rest[21:]
    links = Links(send_sems, local_sems)
    yh, _, _, c, t = links.me
    y = yh * 2 + t
    tables = [links.keep(w_all, w), links.keep(gates_all, gates), links.keep(router_all, router)]
    loads = {}
    for k in (2, 1, 3, 0):
        for core in (1, 0):
            b = up4(y, k) * 2 + up2(c, core)
            for n, (src, dst) in enumerate(((x_all, xs), (c_all, cs))):
                copy = pltpu.make_async_copy(src.at[b], dst.at[rows_of(b), :], load_sems.at[(k * 2 + core) * 2 + n])
                copy.start()
                loads[(k, core, n)] = copy
    links.barrier([links.at(**p) for p in RING + TWIN])
    lane = lax.broadcasted_iota(jnp.int32, (OWN, 128), 1)
    mine = (lane == y * 2 + c).astype(F32)
    grad_sum, mix_sum = RingSum(links, *grads), RingSum(links, *mixes[:3], None, None, mixes[3], None)

    def one_block(b, grad, mix):
        rows = rows_of(b)
        xb, cb = xs[rows, :], cs[rows, :]
        table = jnp.concatenate([gates[b], jnp.zeros((120, OWN), F32)], axis=0).T
        gate = jnp.sum(table * mine, axis=1, keepdims=True)
        grad_gate = jnp.zeros((OWN, 1), F32)
        for n in range(3):
            columns = slice(256 * n, 256 * (n + 1))
            gate_in = nn(xb, w[0, :, columns])
            up_in = nn(xb, w[1, :, columns])
            back = nn(cb, w[2, :, columns])
            sig = 0.5 * jnp.tanh(0.5 * gate_in) + 0.5
            act = gate_in * sig
            hid = act * up_in
            grad_gate = grad_gate + jnp.sum(hid * back, axis=1, keepdims=True)
            grad_hidden = gate * back
            hidden[rows, columns] = (gate * hid).astype(BF)
            d_gate[rows, columns] = (grad_hidden * up_in * (sig + act * (1.0 - sig))).astype(BF)
            d_up[rows, columns] = (grad_hidden * act).astype(BF)
        dl = (gate * grad_gate * (mine - table)).astype(BF)
        d_logit[rows, :] = dl
        dg, du, hw = d_gate[rows, :], d_up[rows, :], hidden[rows, :]
        for n in range(6):
            columns = slice(256 * n, 256 * (n + 1))
            grad[:, columns] = (
                nt(dg, w[0, columns, :]) + nt(du, w[1, columns, :]) + nt(dl, router[columns, :])
            ).astype(BF)
            mix[:, columns] = nt(hw, w[2, columns, :]).astype(BF)

    for copy in tables:
        copy.wait()
    mixed = []

    def mix_done(k):
        mix_sum.add_twin(k)
        return links.keep(mix_sum.own.at[k], mix_out.at[k])

    done = None
    for k in ORDER:
        for core in (1, 0):
            loads[(k, core, 0)].wait()
            loads[(k, core, 1)].wait()
            b = up4(y, k) * 2 + up2(c, core)
            one_block(b, grad_sum.place(k, core), mix_sum.place(k, core))
            if core:
                grad_sum.to_twin(k)
                mix_sum.to_twin(k)
                if done is not None:
                    grad_sum.pass_on(done)
                    mixed.append(mix_done(done))
        done = k
    grad_sum.pass_on(0)
    mixed.append(mix_done(0))

    def strip(i, carry):
        columns = rows_of(i)
        xt = xs[:, columns]
        slot = lax.rem(i, 2)

        def stored(n, at):
            return pltpu.make_async_copy(staged.at[slot, n], dw_out.at[n, rows_of(at)], dw_sems.at[slot * 3 + n])

        @pl.when(i >= 2)
        def _():
            for n in range(3):
                stored(n, i - 2).wait()

        for n, (left, right) in enumerate(((xt, d_gate), (xt, d_up), (cs[:, columns], hidden))):
            staged[slot, n] = tn(left, right[...]).astype(BF)
        router_out[:, columns] = tn(d_logit[...], xt)[:8, :]
        for n in range(3):
            stored(n, i).start()
        return carry

    lax.fori_loop(0, 6, strip, 0)
    gx_out[...] = grad_sum.total()
    for copy in mixed:
        copy.wait()
    for slot in range(2):
        for n in range(3):
            pltpu.make_async_copy(staged.at[slot, n], dw_out.at[n, rows_of(4 + slot)], dw_sems.at[slot * 3 + n]).wait()
    links.finish()


def run_expert(w, x_all, c_all, gates, router):
    return pl.pallas_call(
        expert_kernel,
        out_shape=(
            jax.ShapeDtypeStruct((OWN, D), F32),
            jax.ShapeDtypeStruct((4, OWN, D), BF),
            jax.ShapeDtypeStruct((3, D, HALF), BF),
            jax.ShapeDtypeStruct((8, D), F32),
        ),
        in_specs=[ANY] * 5,
        out_specs=(VMEM, ANY, ANY, VMEM),
        scratch_shapes=[
            pltpu.VMEM((3, D, HALF), BF),
            pltpu.VMEM((8, 8, OWN), F32),
            pltpu.VMEM((D, WIDE - PART), BF),
            pltpu.VMEM((8 * OWN, D), BF),
            pltpu.VMEM((8 * OWN, D), BF),
            pltpu.VMEM((8 * OWN, HALF), BF),
            pltpu.VMEM((8 * OWN, HALF), BF),
            pltpu.VMEM((8 * OWN, HALF), BF),
            pltpu.VMEM((8 * OWN, 128), BF),
            pltpu.VMEM((2, 3, OWN, HALF), BF),
        ]
        + RingSum.SCRATCH
        + RingSum.SCRATCH[:3]
        + RingSum.SCRATCH[5:6]
        + [pltpu.SemaphoreType.DMA((n,)) for n in (24, 16, 6, 7)],
        compiler_params=pltpu.CompilerParams(
            collective_id=5, has_side_effects=True, vmem_limit_bytes=60 * MIB
        ),
        name="expert",
    )(w, x_all, c_all, gates, router)


def plane_reduce(links, h, ops, sems):
    def target(k, stage):
        return links.at(dx=k) if (h == 0) == (stage == 1) else links.at(dz=k)

    for stage in (0, 1):
        base = 4 * stage
        far, near = {}, {}
        for i, k in ((0, 1), (1, 3)):
            far[i] = links.send(ops.far(stage, i), ops.far_land(stage, i), sems.at[base + i], target(k, stage))
        yield
        for i, k in ((0, 1), (1, 3)):
            ops.ready(stage, k)
            far[i].wait_recv()
            ops.add_far(stage, i, k)
            near[i] = links.send(
                ops.near(stage, k), ops.near_land(stage, 1 - i), sems.at[base + 3 - i], target(k, stage)
            )
        yield
        ops.ready(stage, 0)
        for i in (0, 1):
            near[i].wait_recv()
        ops.total(stage)
    yield


def loop(counts, fn):
    a, b = counts

    def body(i, carry):
        fn(lax.div(i, b), lax.rem(i, b))
        return carry

    lax.fori_loop(0, a * b, body, 0)


SLOT = {1: 0, 3: 1, 0: 2}


class ExpertOps:
    SCRATCH = [
        pltpu.VMEM((2, 3, 3, 4, 48, HALF), BF),
        pltpu.VMEM((2, 2, 3, 4, 48, 384), BF),
        pltpu.VMEM((2, 2, 3, 4, 48, HALF), BF),
        pltpu.VMEM((2, 4, 3, 48, HALF), BF),
        pltpu.VMEM((2, 2, 3, 48, 384), BF),
        pltpu.VMEM((2, 2, 3, 48, HALF), BF),
        pltpu.VMEM((2, 2, 3, 24, HALF), BF),
    ]

    def __init__(self, links, h, g, acc, far1, near1, mid, far2, near2, last):
        self.h, self.g, self.acc, self.far1, self.near1 = h, g, acc, far1, near1
        self.mid, self.far2, self.near2, self.last = mid, far2, near2, last
        _, self.x, self.z, _, _ = links.me
        self.loads = {k: links.keep(self.block(k), acc.at[h, SLOT[k]]) for k in (1, 3, 0)}

    def block(self, k, *columns):
        if self.h == 0:
            return self.g.at[(slice(None), 0, slice(None), up4(self.z, k), slice(None)) + columns]
        return self.g.at[(slice(None), 1, up4(self.x, k), slice(None), slice(None)) + columns]

    def ready(self, stage, k):
        if stage == 0:
            self.loads[k].wait()

    def far(self, stage, i):
        columns = pl.ds(384 * i, 384)
        return self.mid.at[self.h, 2, :, :, columns] if stage else self.block(2, columns)

    def far_land(self, stage, i):
        return (self.far2 if stage else self.far1).at[self.h, i]

    def near(self, stage, k):
        return self.mid.at[self.h, k] if stage else self.acc.at[self.h, SLOT[k]]

    def near_land(self, stage, i):
        return (self.near2 if stage else self.near1).at[self.h, i]

    def add_far(self, stage, i, k):
        h, columns = self.h, slice(384 * i, 384 * (i + 1))

        def first(m, a):
            s = SLOT[k]
            self.acc[h, s, m, a, :, columns] = (
                self.acc[h, s, m, a, :, columns].astype(F32) + self.far1[h, i, m, a].astype(F32)
            ).astype(BF)

        def second(m, _):
            self.mid[h, k, m, :, columns] = (
                self.mid[h, k, m, :, columns].astype(F32) + self.far2[h, i, m].astype(F32)
            ).astype(BF)

        loop((3, 1) if stage else (3, 4), second if stage else first)

    def total(self, stage):
        h = self.h
        here = self.x if h == 0 else self.z

        def first(k, m):
            a = up4(here, k)
            self.mid[h, k, m] = (
                self.acc[h, 2, m, a].astype(F32)
                + self.near1[h, 0, m, a].astype(F32)
                + self.near1[h, 1, m, a].astype(F32)
            ).astype(BF)

        def second(m, _):
            value = (
                self.mid[h, 0, m].astype(F32)
                + self.near2[h, 0, m].astype(F32)
                + self.near2[h, 1, m].astype(F32)
            )
            self.last[h, 0, m] = value[:24, :].astype(BF)
            self.last[h, 1, m] = value[24:, :].astype(BF)

        loop((3, 1) if stage else (4, 3), second if stage else first)


def attention_scratch(width):
    return [
        pltpu.VMEM((2, 2, 2, 4, 4, 48, width), BF),
        pltpu.VMEM((2, 4, 2, 4, 48, width), BF),
        pltpu.VMEM((2, 2, 4, 48, width), BF),
        pltpu.VMEM((2, 2, 2, 4, 48, width), BF),
        pltpu.VMEM((2, 4, 2, 48, width), BF),
        pltpu.VMEM((2, 2, 48, width), BF),
        pltpu.VMEM((2, 2, 2, 48, width), BF),
        pltpu.VMEM((2, 2, 48, width), BF),
    ]


class AttentionOps:
    def __init__(self, links, h, twin_sems, g, twin, far1, near1, mid, far2, near2, last):
        self.h, self.g, self.twin, self.far1, self.near1 = h, g, twin, far1, near1
        self.mid, self.far2, self.near2, self.last = mid, far2, near2, last
        _, self.x, self.z, self.c, _ = links.me
        self.twins = {}
        for k in (2, 1, 3, 0):
            self.twins[k] = links.send(
                self.block(1 - self.c, k), twin.at[h, k], twin_sems.at[h * 4 + k], links.at(dc=1)
            )

    def place(self, k):
        return up4(self.z if self.h == 0 else self.x, k)

    def block(self, core, k):
        if self.h == 0:
            return self.g.at[0, core, :, :, self.place(k)]
        return self.g.at[1, core, :, self.place(k)]

    def get(self, k, i, a):
        return self.g[0, self.c, i, a, self.place(k)] if self.h == 0 else self.g[1, self.c, i, self.place(k), a]

    def put(self, k, i, a, value):
        if self.h == 0:
            self.g[0, self.c, i, a, self.place(k)] = value.astype(BF)
        else:
            self.g[1, self.c, i, self.place(k), a] = value.astype(BF)

    def add_twin(self, k):
        self.twins[k].wait_recv()

        def add(i, a):
            self.put(k, i, a, self.get(k, i, a).astype(F32) + self.twin[self.h, k, i, a].astype(F32))

        loop((2, 4), add)

    def ready(self, stage, k):
        if stage == 0:
            self.add_twin(k)

    def far(self, stage, i):
        if stage:
            return self.mid.at[self.h, 2, i]
        if i == 0:
            self.add_twin(2)
        if self.h == 0:
            return self.g.at[0, self.c, i, :, self.place(2)]
        return self.g.at[1, self.c, i, self.place(2)]

    def far_land(self, stage, i):
        return (self.far2 if stage else self.far1).at[self.h, i]

    def near(self, stage, k):
        return self.mid.at[self.h, k] if stage else self.block(self.c, k)

    def near_land(self, stage, i):
        return (self.near2 if stage else self.near1).at[self.h, i]

    def add_far(self, stage, i, k):
        h = self.h
        if stage:
            self.mid[h, k, i] = (self.mid[h, k, i].astype(F32) + self.far2[h, i].astype(F32)).astype(BF)
            return

        def add(a, _):
            self.put(k, i, a, self.get(k, i, a).astype(F32) + self.far1[h, i, a].astype(F32))

        loop((4, 1), add)

    def total(self, stage):
        h = self.h
        here = self.x if h == 0 else self.z

        def first(k, i):
            a = up4(here, k)
            self.mid[h, k, i] = (
                self.get(0, i, a).astype(F32)
                + self.near1[h, 0, i, a].astype(F32)
                + self.near1[h, 1, i, a].astype(F32)
            ).astype(BF)

        def second(i, _):
            self.last[h, i] = (
                self.mid[h, 0, i].astype(F32)
                + self.near2[h, 0, i].astype(F32)
                + self.near2[h, 1, i].astype(F32)
            ).astype(BF)

        loop((2, 1) if stage else (4, 2), second if stage else first)


def backward_kernel(
    g, w_in, w_out, mix, gx,
    cot_in, tok_in, residual_in, normed_in, q_in, k_in, v_in, att_in, cosine_in, sine_in, gains_in, router_in,
    ge, grad_input, layer_output, grad_q, grad_k, grad_v, grad_o, small_out, *rest
):
    expert_refs, in_refs, out_refs = rest[:7], rest[7:15], rest[15:23]
    inputs = rest[23:34]
    cot, residual, normed, q, k, v, att, cosine, sine, gains, router = inputs
    (
        wqkv, flow, grad_residual, grad_branch, lin, kv_own, kv_send, kv_recv,
        ring_in, ring_out, swap_in_own, swap_in_out, swap_in_in, swap_out_own, swap_out_out, swap_out_in,
        small, s_twin, s_land, s_back, mix_far, mix_near,
    ) = rest[34:56]
    (
        send_sems, local_sems, expert_sems, in_sems, out_sems, in_twin_sems, out_twin_sems, back_sems, kv_sems,
        ring_sems, swap_sems, small_sems, mix_sems,
    ) = rest[56:]
    links = Links(send_sems, local_sems)
    yh, x, z, c, t = links.me
    twin = links.at(dc=1)
    loads = [
        links.keep(src, dst)
        for src, dst in zip(
            (gx, cot_in, residual_in, gains_in, normed_in, q_in, k_in, v_in, att_in, cosine_in, sine_in, router_in),
            (flow, cot, residual, gains, normed, q, k, v, att, cosine, sine, router),
        )
    ]
    out_load = links.keep(w_out.at[0], wqkv.at[:, :, :, pl.ds(0, 384)])
    links.barrier([links.at(**p) for p in ALONG + RING + CROSS + TWIN])
    reduce_experts = [
        plane_reduce(links, h, ExpertOps(links, h, g, *expert_refs), expert_sems.at[pl.ds(8 * h, 8)])
        for h in (0, 1)
    ]

    def step(group, count=1):
        for _ in range(count):
            for steps in group:
                next(steps, None)

    step(reduce_experts)
    mix_sent = {}
    for i, to in ((0, 1), (1, 3)):
        mix_sent[i] = links.send(
            mix.at[2, pl.ds(128 * i, 128)], mix_far.at[i], mix_sems.at[i], links.at(dy=to)
        )

    for copy in loads[:4]:
        copy.wait()
    scaled = flow[...] * gains[1:2, :]
    value = residual[...]
    inverse = inverse_norm(value)
    mean = jnp.mean(scaled * value, axis=1, keepdims=True)
    grad = cot[...].astype(F32) + inverse * scaled - value * (inverse * inverse * inverse * mean)
    gain_two = jnp.sum(flow[...] * (value * inverse), axis=0, keepdims=True)
    grad_residual[...] = grad
    grad_branch[...] = grad.astype(BF)
    mix_load = [links.keep(mix.at[to, pl.ds(at, 128)], cot.at[pl.ds(at, 128)]) for to, at in ((1, 0), (3, 128))]
    for copy in loads[4:]:
        copy.wait()
    bias = causal_bias(t)
    cos_own, sin_own = cosine[...], sine[...]

    def weight_rows(left, right, store):
        for i in (0, 1):
            for half in (0, 1):
                first = HALF * i + 384 * half
                rows = tn(left[:, first : first + 384], right)
                store(i, slice(2 * half, 2 * half + 2), rows.reshape(2, 4, 48, rows.shape[1]).astype(BF))

    def start(refs, twin_sems, sems, group):
        j = len(group)
        ops = AttentionOps(links, j, twin_sems, *refs)
        group.append(plane_reduce(links, j, ops, sems.at[pl.ds(8 * j, 8)]))

    reduce_out, reduce_in = [], []
    for j in (0, 1):

        def store_out(i, at, value, j=j):
            for half in (0, 1):
                out_refs[0][j, half, i, at] = value[..., 384 * half : 384 * (half + 1)]

        weight_rows(grad_branch, att[j], store_out)
        start(out_refs, out_twin_sems, out_sems, reduce_out)
    step(reduce_out)
    step(reduce_experts)
    tok_load = [links.keep(tok_in.at[:, pl.ds(HALF * i, HALF)], att.at[i]) for i in (0, 1)]

    exchanges = []
    for j in (0, 1):
        out_load.wait()
        grad_att = jnp.concatenate(
            [
                nn(grad_branch[:, :HALF], wqkv[half, 0, :, :384])
                + nn(grad_branch[:, HALF:], wqkv[half, 1, :, :384])
                for half in (0, 1)
            ],
            axis=1,
        ).astype(BF)
        if j == 0:
            out_load = links.keep(w_out.at[1], wqkv.at[:, :, :, pl.ds(0, 384)])
        else:
            in_load = links.keep(w_in.at[0], wqkv)
        kj, vj = k[j], v[j]
        gk = jnp.zeros((SEQ, HD), F32)
        gv = jnp.zeros((SEQ, HD), F32)
        for h in range(6):
            lanes = slice(HD * h, HD * (h + 1))
            qh, gh = q[j, :, lanes], grad_att[:, lanes]
            scores = nt(qh, kj) * SCALE + bias
            raised = jnp.exp(scores - jnp.max(scores, axis=1, keepdims=True))
            exact = raised * (1.0 / jnp.sum(raised, axis=1, keepdims=True))
            grad_probs = nt(gh, vj)
            centred = jnp.sum(exact * grad_probs, axis=1, keepdims=True)
            grad_scores = (exact * (grad_probs - centred)).astype(BF)
            lin[j, :, lanes] = unroped(nn(grad_scores, kj) * SCALE, cos_own, sin_own).astype(BF)
            gk = gk + tn(grad_scores, qh)
            gv = gv + tn(exact.astype(BF), gh)
            if (j, h) == (1, 0):
                step(reduce_out)
        both = jnp.concatenate([gk * SCALE, gv], axis=1)
        low, high = both[:OWN, :], both[OWN:, :]
        kv_own[j] = jnp.where(t == 0, low, high)
        kv_send[j] = jnp.where(t == 0, high, low).astype(BF)
        exchanges.append(links.send(kv_send.at[j], kv_recv.at[j], kv_sems.at[j], links.flip(dt=1)))
    for copy in mix_load:
        copy.wait()
    for i, to in ((0, 1), (1, 3)):
        mix_sent[i].wait_recv()
        half = pl.ds(128 * i, 128)
        keep = pl.ds(128 * (1 - i), 128)
        cot[half, :] = (cot[half, :].astype(F32) + mix_far[i].astype(F32)).astype(BF)
        mix_sent[2 + i] = links.send(mix.at[to, keep], mix_near.at[i, keep], mix_sems.at[2 + i], links.at(dy=to))
        mix_sent[4 + i] = links.send(cot.at[half], mix_near.at[i, half], mix_sems.at[4 + i], links.at(dy=to))

    step(reduce_experts)

    for j in (0, 1):
        exchanges[j].wait_recv()
        total = kv_own[j] + kv_recv[j].astype(F32)
        lin[j, :, HALF:PART] = unroped(total[:, :HD], cos_own, sin_own).astype(BF)
        lin[j, :, PART:] = total[:, HD:].astype(BF)

        def store_in(i, at, value, j=j):
            for half in (0, 1):
                in_refs[0][j, half, i, at] = value[..., 512 * half : 512 * (half + 1)]

        weight_rows(normed, lin[j], store_in)
        start(in_refs, in_twin_sems, in_sems, reduce_in)
        in_load.wait()
        for i in (0, 1):
            columns = slice(HALF * i, HALF * (i + 1))
            part = nt(lin[j, :, :512], wqkv[0, i]) + nt(lin[j, :, 512:], wqkv[1, i])
            flow[:, columns] = part if j == 0 else flow[:, columns] + part
        if j == 0:
            in_load = links.keep(w_in.at[1], wqkv)
        next(reduce_in[j])
    mix_last = links.keep(mix.at[0], normed)
    for copy in tok_load:
        copy.wait()

    gradient = flow[...]
    scaled = gradient * gains[0:1, :]
    value = jnp.concatenate([att[0], att[1]], axis=1).astype(F32)
    inverse = inverse_norm(value)
    mean = jnp.mean(scaled * value, axis=1, keepdims=True)
    grad_branch[...] = (
        grad_residual[...] + inverse * scaled - value * (inverse * inverse * inverse * mean)
    ).astype(BF)
    results = [links.keep(grad_branch, grad_input)]
    gain_one = jnp.sum(gradient * (value * inverse), axis=0, keepdims=True)
    rows = jnp.concatenate([router[...], gain_one, gain_two, jnp.zeros((6, D), F32)], axis=0)
    small[0] = rows[:, :HALF]
    small[1] = rows[:, HALF:]
    s_copy = links.send(small.at[1 - c], s_twin, small_sems.at[0], twin)
    def everyone(axis, at):
        copies = {}
        for k in (1, 2, 3):
            j = 4 - k
            copies[j] = links.send(
                small.at[c], s_land.at[at, j - 1], small_sems.at[3 * at + j], links.at(**{axis: k})
            )
        return copies

    def settle(copies, at):
        for copy in copies.values():
            copy.wait_recv()
            links.left(copy)
        small[c] = small[c] + s_land[at, 0] + s_land[at, 1] + s_land[at, 2]

    def around(refs, ring, base):
        copies = []
        for dyh, dt in ((1, 1), (1, 0), (0, 1)):
            index = dyh * 2 + dt - 1
            copies.append(
                links.send(
                    refs[7].at[up2(t, dt), up2(yh, dyh)], ring.at[index], ring_sems.at[base + index],
                    links.flip(dyh=dyh, dt=dt),
                )
            )
        return copies

    def collect(copies, refs, ring, own, theirs, mine, at):
        for copy in copies:
            copy.wait_recv()
        total = refs[7][t, yh].astype(F32)
        for i in range(3):
            total = total + ring[i].astype(F32)
        theirs[...] = jnp.where(c == 0, total[24:, :], total[:24, :])
        swap = links.send(theirs, mine, swap_sems.at[at], twin)
        own[...] = jnp.where(c == 0, total[:24, :], total[24:, :])
        return swap

    def halves(swap, own, mine):
        swap.wait_recv()
        return jnp.where(c == 0, own[...], mine[...]), jnp.where(c == 0, mine[...], own[...])

    step(reduce_out)
    s_copy.wait_recv()
    small[c] = small[c] + s_twin[...]
    copies = everyone("dz", 0)
    step(reduce_experts)
    step(reduce_in)
    step(reduce_out)
    settle(copies, 0)
    copies = everyone("dx", 1)
    step(reduce_experts)

    last, slot, back = expert_refs[6], (yh * 2 + t) * 2 + c, []
    for dyh in range(2):
        for dt in range(2):
            for dc in range(2):
                columns = pl.ds(pl.multiple_of(up2(t, dt) * 384, 384), 384)
                src = last.at[up2(yh, dyh), up2(c, dc), :, :, columns]
                if dyh + dt + dc == 0:
                    stay = links.keep(src, ge.at[slot])
                else:
                    index = (dyh * 2 + dt) * 2 + dc
                    back.append(
                        links.send(src, ge.at[slot], back_sems.at[index], links.flip(dyh=dyh, dt=dt, dc=dc))
                    )

    step(reduce_out)
    out_around = around(out_refs, ring_out, 0)
    settle(copies, 1)
    copies = everyone("dy", 2)
    step(reduce_in)
    for n in (2, 3, 4, 5):
        mix_sent[n].wait_recv()
    mix_last.wait()
    normed[...] = (
        residual[...] + normed[...].astype(F32) + mix_near[0].astype(F32) + mix_near[1].astype(F32)
    ).astype(BF)
    results.append(links.keep(normed, layer_output))
    step(reduce_in)
    out_swap = collect(out_around, out_refs, ring_out, swap_out_own, swap_out_out, swap_out_in, 0)
    settle(copies, 2)
    s_copy = links.send(small.at[c], s_back, small_sems.at[10], twin)
    step(reduce_in)
    in_around = around(in_refs, ring_in, 3)
    s_copy.wait_recv()
    small_out[c] = small[c]
    small_out[1 - c] = s_back[...]
    in_swap = collect(in_around, in_refs, ring_in, swap_in_own, swap_in_out, swap_in_in, 1)
    for copy in back:
        copy.wait_recv()
    for copy in results + [stay]:
        copy.wait()
    first, second = halves(out_swap, swap_out_own, swap_out_in)
    grad_o[:, :384] = first
    grad_o[:, 384:] = second
    first, second = halves(in_swap, swap_in_own, swap_in_in)
    grad_q[:, :512] = first
    grad_q[:, 512:] = second[:, :256]
    grad_k[...] = second[:, 256:384]
    grad_v[...] = second[:, 384:]
    links.finish()


def backward(*args):
    staged = args[5:6] + args[7:]
    return pl.pallas_call(
        backward_kernel,
        out_shape=(
            jax.ShapeDtypeStruct((8, 3, 24, 384), BF),
            jax.ShapeDtypeStruct((OWN, D), BF),
            jax.ShapeDtypeStruct((OWN, D), BF),
            jax.ShapeDtypeStruct((24, HALF), F32),
            jax.ShapeDtypeStruct((24, HD), F32),
            jax.ShapeDtypeStruct((24, HD), F32),
            jax.ShapeDtypeStruct((24, HALF), F32),
            jax.ShapeDtypeStruct((2, 16, HALF), F32),
        ),
        in_specs=[ANY] * len(args),
        out_specs=(ANY,) * 3 + (VMEM,) * 5,
        scratch_shapes=ExpertOps.SCRATCH
        + attention_scratch(512)
        + attention_scratch(384)
        + [pltpu.VMEM(v.shape, v.dtype) for v in staged]
        + [
            pltpu.VMEM((2, 2, HALF, 512), BF),
            pltpu.VMEM((OWN, D), F32),
            pltpu.VMEM((OWN, D), F32),
            pltpu.VMEM((OWN, D), BF),
            pltpu.VMEM((2, OWN, WIDE), BF),
            pltpu.VMEM((2, OWN, 2 * HD), F32),
            pltpu.VMEM((2, OWN, 2 * HD), BF),
            pltpu.VMEM((2, OWN, 2 * HD), BF),
            pltpu.VMEM((3, 48, 512), BF),
            pltpu.VMEM((3, 48, 384), BF),
            pltpu.VMEM((24, 512), F32),
            pltpu.VMEM((24, 512), F32),
            pltpu.VMEM((24, 512), F32),
            pltpu.VMEM((24, 384), F32),
            pltpu.VMEM((24, 384), F32),
            pltpu.VMEM((24, 384), F32),
            pltpu.VMEM((2, 16, HALF), F32),
            pltpu.VMEM((16, HALF), F32),
            pltpu.VMEM((3, 3, 16, HALF), F32),
            pltpu.VMEM((16, HALF), F32),
            pltpu.VMEM((2, OWN // 2, D), BF),
            pltpu.VMEM((2, OWN, D), BF),
        ]
        + [pltpu.SemaphoreType.DMA((n,)) for n in (112, 40, 16, 16, 16, 8, 8, 8, 2, 6, 2, 11, 6)],
        compiler_params=pltpu.CompilerParams(
            collective_id=6, has_side_effects=True, vmem_limit_bytes=60 * MIB
        ),
        name="backward",
    )(*args)


def rope_tables():
    half_size = HD // 2
    exponent = -(np.float32(2.0) * np.arange(half_size, dtype=np.float32)) / np.float32(HD)
    frequency = np.power(np.float32(ROPE_BASE), exponent, dtype=np.float32)
    angles = np.arange(SEQ, dtype=np.float32)[:, None] * frequency[None, :]
    cosine, sine = np.cos(angles), np.sin(angles)
    return np.concatenate([cosine, cosine], axis=1), np.concatenate([-sine, sine], axis=1)


def shards(
    tokens_in, routes, cotangent, attn_gain, query_proj, key_proj, value_proj, output_proj,
    ffn_gain, router_proj, expert_gate, expert_up, expert_down,
):
    d, t = lax.axis_index("dp"), lax.axis_index("tensor")
    blank = jnp.zeros((24, 128), BF)
    extra = jnp.concatenate([router_proj, attn_gain[:, None], ffn_gain[:, None], blank[:, 10:]], axis=1)
    a_in = jnp.stack(
        [
            jnp.concatenate([query_proj[:, :512], extra], axis=1),
            jnp.concatenate([query_proj[:, 512:], key_proj, value_proj, blank], axis=1),
        ]
    )
    a_out = jnp.stack([output_proj[:, :384], output_proj[:, 384:]])
    e_block = jnp.stack([expert_gate, expert_up, expert_down]).transpose(2, 0, 1, 3)
    own_routes = lax.dynamic_slice(routes, (OWN * t, 0), (OWN, 4))
    chosen = jnp.any(own_routes[:, :, None] == jnp.arange(128)[None, None, :], axis=1).astype(F32)
    cosine, sine = (jnp.asarray(v) for v in rope_tables())
    (
        w_in, w_out, router, experts, tok_all, cot_all, gates, normed, queries, keys, values, attended, residual, gains
    ) = forward(a_in, a_out, e_block, tokens_in, cotangent, chosen, cosine, sine)
    flow, mixture, grad_experts, grad_router = run_expert(
        experts.reshape(3, D, HALF), tok_all, cot_all, gates, router.reshape(D, 128)
    )
    ge, grad_input, layer_output, grad_q, grad_k, grad_v, grad_o, small = backward(
        grad_experts.reshape(3, 2, 4, 4, 48, HALF), w_in.reshape(2, 2, 2, HALF, 512), w_out.reshape(2, 2, 2, HALF, 384), mixture, flow, cotangent, tokens_in, residual,
        normed, queries, keys, values, attended,
        lax.dynamic_slice(cosine, (OWN * t, 0), (OWN, HD)), lax.dynamic_slice(sine, (OWN * t, 0), (OWN, HD)),
        gains, grad_router,
    )
    ge = ge.astype(F32).transpose(1, 2, 0, 3)
    small = jnp.concatenate([small[0], small[1]], axis=1)
    small = lax.dynamic_slice(small, (0, 24 * d + 12 * t), (16, 12))
    return (
        layer_output,
        grad_input,
        small[8],
        grad_q,
        grad_k,
        grad_v,
        grad_o,
        small[9],
        small[:8].T,
        ge[0],
        ge[1],
        ge[2],
    )


def solution(mesh):
    return jax.shard_map(
        shards,
        mesh=mesh,
        in_specs=(
            P(("dp", "tensor"), None),
            P("dp", None),
            P(("dp", "tensor"), None),
            P("dp"),
            P("dp", "tensor"),
            P("dp", "tensor"),
            P("dp", "tensor"),
            P("dp", "tensor"),
            P("dp"),
            P("dp", None),
            P("dp", None, "tensor"),
            P("dp", None, "tensor"),
            P("dp", None, "tensor"),
        ),
        out_specs=(
            P(("dp", "tensor"), None),
            P(("dp", "tensor"), None),
            P(("dp", "tensor")),
            P("dp", "tensor"),
            P("dp", "tensor"),
            P("dp", "tensor"),
            P("dp", "tensor"),
            P(("dp", "tensor")),
            P(("dp", "tensor"), None),
            P("dp", None, "tensor"),
            P("dp", None, "tensor"),
            P("dp", None, "tensor"),
        ),
        check_vma=False,
    )
```

```python
import functools

import jax
import jax.numpy as jnp
import numpy as np
from jax import lax
from jax.experimental import pallas as pl
from jax.experimental.pallas import tpu as pltpu
from jax.sharding import PartitionSpec as P

HD = 128
E = 8
D = 1536
SEQ = 512
OWN = 256
HALF = 768
PART = 896
WIDE = 1024
NORM_EPSILON = 1e-06
ROPE_BASE = 1000000.0
SCALE = HD ** (-0.5)
MESH = pl.DeviceIdType.MESH
BF = jnp.bfloat16
F32 = jnp.float32
ANY = pl.BlockSpec(memory_space=pl.ANY)
VMEM = pl.BlockSpec(memory_space=pltpu.VMEM)
MIB = 1 << 20


def place():
    d = lax.axis_index("dp")
    t = lax.axis_index("tensor")
    c = lax.rem(d, 2)
    z = lax.rem(lax.div(d, 2), 4)
    x = lax.rem(lax.div(d, 8), 4)
    yh = lax.div(d, 32)
    return yh, x, z, c, t


def device(yh, x, z, c, t):
    return (((yh * 4 + x) * 4 + z) * 2 + c, t)


def up4(v, k):
    return lax.rem(v + k, 4)


def up2(v, k):
    return lax.rem(v + k, 2)


def rows_of(b, size=OWN):
    return pl.ds(pl.multiple_of(b * size, size), size)


def nn(a, b):
    return jnp.dot(a, b, preferred_element_type=F32)


def nt(a, b):
    return lax.dot_general(a, b, (((1,), (1,)), ((), ())), preferred_element_type=F32)


def tn(a, b):
    return lax.dot_general(a, b, (((0,), (0,)), ((), ())), preferred_element_type=F32)


class Links:
    def __init__(self, send_sems, local_sems):
        self.me = place()
        self.send_sems, self.local_sems = send_sems, local_sems
        self.sent, self.local, self.count = [], [], 0

    def at(self, dy=0, dx=0, dz=0, dc=0):
        yh, x, z, c, t = self.me
        y = up4(yh * 2 + t, dy)
        return device(lax.div(y, 2), up4(x, dx), up4(z, dz), up2(c, dc), lax.rem(y, 2))

    def flip(self, dyh=0, dt=0, dc=0):
        yh, x, z, c, t = self.me
        return device(up2(yh, dyh), x, z, up2(c, dc), up2(t, dt))

    def barrier(self, partners):
        sem = pltpu.get_barrier_semaphore()
        for partner in partners:
            pl.semaphore_signal(sem, inc=1, device_id=partner, device_id_type=MESH)
        pl.semaphore_wait(sem, len(partners))

    def send(self, src, dst, recv_sem, target):
        copy = pltpu.make_async_remote_copy(
            src_ref=src,
            dst_ref=dst,
            send_sem=self.send_sems.at[self.count],
            recv_sem=recv_sem,
            device_id=target,
            device_id_type=MESH,
        )
        copy.start()
        self.count += 1
        self.sent.append(copy)
        return copy

    def keep(self, src, dst):
        copy = pltpu.make_async_copy(src, dst, self.local_sems.at[len(self.local)])
        copy.start()
        self.local.append(copy)
        return copy

    def left(self, copy):
        copy.wait_send()
        self.sent = [other for other in self.sent if other is not copy]

    def finish(self):
        for copy in self.sent:
            copy.wait_send()


ALONG = [dict(dx=k) for k in (1, 2, 3)] + [dict(dz=k) for k in (1, 2, 3)]
NEAR = [dict(dx=k) for k in (1, 3)] + [dict(dz=k) for k in (1, 3)]
RING = [dict(dy=k) for k in (1, 2, 3)]
CROSS = [dict(dy=k, dc=1) for k in (1, 2, 3)]
TWIN = [dict(dc=1)]


def plane_gather(links, h, own, one, column, sems, arrived):
    got = {}

    def target(second, k):
        return links.at(dx=k) if (h == 0) != second else links.at(dz=k)

    def push(second, src, dst):
        base = 4 if second else 0
        for n, k in ((0, 1), (1, 3)):
            got[(second, 4 - k)] = links.send(src, dst, sems.at[base + 1 - n], target(second, k))

    def take(second, d, view):
        got[(second, d)].wait_recv()
        i, k = (0, 1) if d == 3 else (1, 3)
        ref = view(d, i)
        got[(second, 2, i)] = links.send(ref, ref, sems.at[(4 if second else 0) + 2 + i], target(second, k))

    push(False, own, one(0))
    yield
    for d in (3, 1):
        take(False, d, one)
    yield
    for i in (0, 1):
        got[(False, 2, i)].wait_recv()
    push(True, column(0), column(0))
    arrived(column(0), 0)
    yield
    for d in (3, 1):
        take(True, d, column)
        arrived(column(d), d)
    yield
    for i in (0, 1):
        got[(True, 2, i)].wait_recv()
    arrived(column(2), 2)
    yield


def plane_views(links, base):
    _, x, z, _, _ = links.me

    def views(h):
        here = (x, z) if h == 0 else (z, x)

        def pick(first, second, *i):
            return base(h, first, second, *i) if h == 0 else base(h, second, first, *i)

        def one(d, *i):
            return pick(up4(here[0], d), here[1], *i)

        def column(d, *i):
            return pick(slice(None), up4(here[1], d), *i)

        return one, column

    return views


def ring_gather(links, src, block, sems, arrived):
    got = {}

    def part(ref, i):
        return ref.at[pl.ds(128 * i, 128), :]

    for i in (0, 1):
        for k in (1, 3):
            half = i if k == 1 else 1 - i
            j = 4 - k
            got[(j, half)] = links.send(
                part(src, half), part(block(0), half), sems.at[j * 2 + half], links.at(dy=k)
            )
    yield
    for j, half, k in ((3, 0, 1), (1, 1, 3)):
        got[(j, half)].wait_recv()
        ref = part(block(j), half)
        got[(2, half)] = links.send(ref, ref, sems.at[4 + half], links.at(dy=k))
    yield
    for j, half in ((3, 1), (1, 0)):
        got[(j, half)].wait_recv()
        arrived(block(j), j)
    yield
    for half in (0, 1):
        got[(2, half)].wait_recv()
    arrived(block(2), 2)
    yield


def advance(*groups, count=1):
    for _ in range(count):
        for steps in groups:
            next(steps, None)


def drain(*groups):
    for steps in groups:
        for _ in steps:
            pass


def roped(u, cosine, sine):
    return u * cosine + pltpu.roll(u, 64, 1) * sine


def unroped(u, cosine, sine):
    return u * cosine - pltpu.roll(u, 64, 1) * sine


def causal_bias(t):
    row = lax.broadcasted_iota(jnp.int32, (OWN, SEQ), 0) + OWN * t
    column = lax.broadcasted_iota(jnp.int32, (OWN, SEQ), 1)
    return jnp.where(row >= column, 0.0, -1e30).astype(F32)


def inverse_norm(v):
    return lax.rsqrt(jnp.mean(v * v, axis=1, keepdims=True) + NORM_EPSILON)


def flat(w, j, half, i, lanes):
    block = w[j, half, i, :, :, :, lanes]
    return block.reshape(HALF, block.shape[-1])


def gain_rows(w):
    tables = [flat(w, 0, 0, i, slice(512, 640)).astype(F32).T for i in (0, 1)]
    both = jnp.concatenate(tables, axis=1)
    return both[8:9, :], both[9:10, :]


def forward_kernel(
    q_in, k_in, v_in, o_in, extra, e, tok, cot, chosen_all, cosine_all, sine_all,
    w_in_out, w_out_out, router_out, e_all, tok_all, cot_all, gates_all, normed_out, q_out, k_out, v_out, att_out, residual_out, gains_out,
    w, wo, a_full, a_pair, o_pair, a_own, o_own, e_pair, e_own, pair, normed, tok_two, gates, chosen, cosine, sine,
    send_sems, local_sems, a_sems, ring_sems, plane_sems, twin_sems, o_plane_sems, o_twin_sems, expert_sems, token_sems,
    cot_sems, cot_twin_sems, e_sems, x_sems, x_twin_sems, g_sems, g_twin_sems,
):
    links = Links(send_sems, local_sems)
    yh, x, z, c, t = links.me
    y = yh * 2 + t
    twin = links.at(dc=1)
    packed = [
        links.keep(q_in, a_full.at[:, pl.ds(0, HALF)]),
        links.keep(k_in, a_full.at[:, pl.ds(HALF, HD)]),
        links.keep(v_in, a_full.at[:, pl.ds(PART, HD)]),
    ]
    links.barrier([links.at(**p) for p in NEAR + RING + CROSS + TWIN])

    groups = ((a_pair, a_own, w), (o_pair, o_own, wo))
    for copy in packed:
        copy.wait()

    def blocks(core):
        inner = pl.ds(pl.multiple_of(512 * core, 128), 512)
        outer = pl.ds(pl.multiple_of(384 * core, 128), 384)
        return (
            ((a_full.at[:, inner], a_pair.at[c, :, pl.ds(0, 512)]), (extra, a_pair.at[c, :, pl.ds(512, 128)])),
            ((o_in.at[:, outer], o_pair.at[c]),),
        )

    placed = [[links.keep(src, dst) for src, dst in group] for group in blocks(c)]
    copies = [
        [links.send(src, dst, a_sems.at[2 * n + i], twin) for i, (src, dst) in enumerate(group)]
        for n, group in enumerate(blocks(1 - c))
    ]
    kept = []
    tables = [links.keep(chosen_all, chosen), links.keep(cosine_all, cosine), links.keep(sine_all, sine)]
    ring, w_kept = {}, []
    for n, (two, block, full) in enumerate(groups):
        for copy in placed[n]:
            copy.wait()
        for copy in copies[n]:
            copy.wait_recv()
        block[...] = jnp.concatenate([two[0].astype(F32), two[1].astype(F32)], axis=0).astype(BF)
        mine = full.at[t, c, yh, x, z]
        for k in (1, 3, 2):
            ring[(n, 4 - k)] = links.send(block, mine, ring_sems.at[n * 4 + 4 - k], links.at(dy=k))
        w_kept.append(links.keep(block, mine))
    columns = pl.ds(pl.multiple_of(t * 384, 384), 384)
    slot = e_pair.at[:, yh, c, :, columns]
    experts = []
    for dy in range(4):
        for dc in range(2):
            src = e.at[up4(y, dy) * 2 + up2(c, dc)]
            if dy + dc == 0:
                e_kept = links.keep(src, slot)
            else:
                index = ((4 - dy) % 4) * 2 + dc
                experts.append(links.send(src, slot, expert_sems.at[index], links.at(dy=dy, dc=dc)))
    kept += [links.keep(tok, pair.at[t]), links.keep(cot, cot_all.at[y * 2 + c])]
    token = links.send(tok, pair.at[t], token_sems.at[0], links.flip(dt=1))
    twins = []

    def cot_arrived(ref, j):
        twins.append(links.send(ref, ref, cot_twin_sems.at[j], twin))

    twins.append(links.send(cot, cot_all.at[y * 2 + c], cot_twin_sems.at[0], twin))
    cots = ring_gather(links, cot, lambda j: cot_all.at[up4(y, j) * 2 + c], cot_sems, cot_arrived)
    advance(cots)

    w_twins = ([], [])

    def spread(n):
        full, twin_n = groups[n][2], (twin_sems, o_twin_sems)[n]

        def base(h, xo, zo, i=slice(None)):
            return full.at[h, c, i, xo, zo]

        views = plane_views(links, base)
        w_kept[n].wait()
        for j in (1, 3, 2):
            ring[(n, j)].wait_recv()
        steps = []
        for h in (0, 1):

            def arrived(ref, d, h=h):
                w_twins[n].append(links.send(ref, ref, twin_n.at[h * 4 + d], twin))

            one, column = views(h)
            sems = (plane_sems, o_plane_sems)[n].at[pl.ds(8 * h, 8)]
            steps.append(plane_gather(links, h, one(0), one, column, sems, arrived))
        advance(*steps)
        return steps

    weights = spread(0)
    out_weights = spread(1)
    e_kept.wait()
    for copy in experts:
        copy.wait_recv()
    for n in range(3):
        for i in range(2):
            e_own[n, i] = jnp.concatenate(
                [e_pair[n, i, 0].astype(F32), e_pair[n, i, 1].astype(F32)], axis=0
            ).astype(BF)
    e_placed = links.keep(e_own, e_all.at[:, :, x, z])

    def e_base(h, xo, zo, i=None):
        if i is None:
            return e_all.at[:, h, xo, zo]
        return e_all.at[:, h, xo, zo, :, pl.ds(384 * i, 384)]

    e_views = plane_views(links, e_base)
    expert = [
        plane_gather(links, h, e_own.at[:, h], *e_views(h), e_sems.at[pl.ds(8 * h, 8)], lambda ref, d: None)
        for h in (0, 1)
    ]
    advance(*weights)
    advance(*out_weights)
    advance(*weights)
    advance(*out_weights)
    e_placed.wait()
    advance(*expert)
    advance(*weights)
    advance(*weights)
    advance(*out_weights)
    token.wait_recv()
    for copy in kept[:2] + tables:
        copy.wait()
    for copy in w_twins[0]:
        copy.wait_recv()
    w_dumps = [
        links.keep(w.at[:, :, :, :, :, :, pl.ds(0, 512)], w_in_out),
        links.keep(w.at[0, 0, :, :, :, :, pl.ds(512, 128)], router_out),
    ]

    gain_one, gain_two = gain_rows(w)
    gains_out[0:1, :] = gain_one
    gains_out[1:2, :] = gain_two
    gains_out[2:8, :] = jnp.zeros((6, D), F32)
    for i in (0, 1):
        v = pair[i].astype(F32)
        normed[pl.ds(OWN * i, OWN), :] = (v * inverse_norm(v) * gain_one).astype(BF)
    own = rows_of(t)
    normed_out[...] = normed[own, :]
    bias = causal_bias(t)
    cos_own, sin_own = cosine[own, :], sine[own, :]
    residual_out[...] = pair[t].astype(F32)

    def project(source, j, half, lanes):
        return nn(source[:, :HALF], flat(w, j, half, 0, lanes)) + nn(source[:, HALF:], flat(w, j, half, 1, lanes))

    for j in (0, 1):
        k = project(normed, j, 1, slice(256, 384))
        v = project(normed, j, 1, slice(384, 512)).astype(BF)
        q = jnp.concatenate(
            [project(normed_out, j, 0, slice(0, 512)), project(normed_out, j, 1, slice(0, 256))], axis=1
        )
        k = roped(k, cosine[...], sine[...]).astype(BF)
        k_out[j] = k
        v_out[j] = v
        for g in range(6):
            lanes = slice(HD * g, HD * (g + 1))
            qh = roped(q[:, lanes], cos_own, sin_own).astype(BF)
            q_out[j, :, lanes] = qh
            scores = nt(qh, k) * SCALE + bias
            raised = jnp.exp(scores - jnp.max(scores, axis=1, keepdims=True))
            probs = (raised * (1.0 / jnp.sum(raised, axis=1, keepdims=True))).astype(BF)
            att_out[j, :, lanes] = nn(probs, v).astype(BF)
            if (j, g) in ((0, 1), (0, 4)):
                advance(*expert)
            if (j, g) == (0, 4):
                advance(cots)
    drain(*out_weights)
    advance(cots)
    for copy in w_twins[1]:
        copy.wait_recv()
    w_dumps.append(links.keep(wo, w_out_out))
    for i in (0, 1):
        columns = pl.ds(HALF * i, HALF)
        part = residual_out[:, columns]
        for j in (0, 1):
            for half in (0, 1):
                part = part + nt(att_out[j, :, 384 * half : 384 * (half + 1)], flat(wo, j, half, i, slice(0, 384)))
        residual_out[:, columns] = part
    residual = residual_out[...]
    tok_two[...] = (residual * inverse_norm(residual) * gain_two).astype(BF)
    block = tok_all.at[y * 2 + c]
    kept.append(links.keep(tok_two, block))

    def x_arrived(ref, j):
        twins.append(links.send(ref, ref, x_twin_sems.at[j], twin))

    tokens = ring_gather(links, tok_two, lambda j: tok_all.at[up4(y, j) * 2 + c], x_sems, x_arrived)
    advance(tokens)
    twins.append(links.send(tok_two, block, x_twin_sems.at[0], twin))
    lanes = slice(512, 640)
    logits = nn(tok_two[:, :HALF], flat(w, 0, 0, 0, lanes)) + nn(tok_two[:, HALF:], flat(w, 0, 0, 1, lanes))
    masked = jnp.where(chosen[...] > 0.5, logits, -1e30)
    raised = jnp.where(chosen[...] > 0.5, jnp.exp(masked - jnp.max(masked, axis=1, keepdims=True)), 0.0)
    table = raised * (1.0 / jnp.sum(raised, axis=1, keepdims=True))
    gates[...] = table.T[:8, :]
    kept.append(links.keep(gates, gates_all.at[y * 2 + c]))
    gate = {}
    for k in (1, 3, 2):
        gate[4 - k] = links.send(gates, gates_all.at[y * 2 + c], g_sems.at[4 - k], links.at(dy=k))
    twins.append(links.send(gates, gates_all.at[y * 2 + c], g_twin_sems.at[0], twin))
    advance(tokens)
    advance(*expert)
    advance(tokens)
    drain(*expert)
    drain(tokens)
    drain(cots)
    for j in (1, 3, 2):
        gate[j].wait_recv()
        ref = gates_all.at[up4(y, j) * 2 + c]
        twins.append(links.send(ref, ref, g_twin_sems.at[j], twin))
    for copy in twins:
        copy.wait_recv()
    for copy in kept[2:] + w_dumps:
        copy.wait()
    links.finish()


def forward(*args):
    dma = [
        pltpu.SemaphoreType.DMA((n,)) for n in (160, 24, 3, 8, 16, 8, 16, 8, 8, 1, 8, 4, 16, 8, 4, 4, 4)
    ]
    return pl.pallas_call(
        forward_kernel,
        out_shape=(
            jax.ShapeDtypeStruct((2, 2, 2, 4, 4, 48, 512), BF),
            jax.ShapeDtypeStruct((2, 2, 2, 4, 4, 48, 384), BF),
            jax.ShapeDtypeStruct((2, 4, 4, 48, 128), BF),
            jax.ShapeDtypeStruct((3, 2, 4, 4, 48, HALF), BF),
            jax.ShapeDtypeStruct((8, OWN, D), BF),
            jax.ShapeDtypeStruct((8, OWN, D), BF),
            jax.ShapeDtypeStruct((8, 8, OWN), F32),
            jax.ShapeDtypeStruct((OWN, D), BF),
            jax.ShapeDtypeStruct((2, OWN, HALF), BF),
            jax.ShapeDtypeStruct((2, SEQ, HD), BF),
            jax.ShapeDtypeStruct((2, SEQ, HD), BF),
            jax.ShapeDtypeStruct((2, OWN, HALF), BF),
            jax.ShapeDtypeStruct((OWN, D), F32),
            jax.ShapeDtypeStruct((8, D), F32),
        ),
        in_specs=[ANY] * 11,
        out_specs=(ANY,) * 7 + (VMEM,) * 7,
        scratch_shapes=[
            pltpu.VMEM((2, 2, 2, 4, 4, 48, 640), BF),
            pltpu.VMEM((2, 2, 2, 4, 4, 48, 384), BF),
            pltpu.VMEM((24, WIDE), BF),
            pltpu.VMEM((2, 24, 640), BF),
            pltpu.VMEM((2, 24, 384), BF),
            pltpu.VMEM((48, 640), BF),
            pltpu.VMEM((48, 384), BF),
            pltpu.VMEM((3, 2, 2, 24, HALF), BF),
            pltpu.VMEM((3, 2, 48, HALF), BF),
            pltpu.VMEM((2, OWN, D), BF),
            pltpu.VMEM((SEQ, D), BF),
            pltpu.VMEM((OWN, D), BF),
            pltpu.VMEM((8, OWN), F32),
            pltpu.VMEM((OWN, 128), F32),
            pltpu.VMEM((SEQ, HD), F32),
            pltpu.VMEM((SEQ, HD), F32),
        ]
        + dma,
        compiler_params=pltpu.CompilerParams(
            collective_id=1, has_side_effects=True, vmem_limit_bytes=60 * MIB
        ),
        name="forward",
    )(*args)


ORDER = (2, 1, 3, 0)


class RingSum:
    SCRATCH = [
        pltpu.VMEM((4, OWN, D), BF),
        pltpu.VMEM((2, OWN, D), BF),
        pltpu.VMEM((4, OWN, D), BF),
        pltpu.VMEM((2, OWN // 2, D), BF),
        pltpu.VMEM((2, OWN, D), BF),
        pltpu.SemaphoreType.DMA((4,)),
        pltpu.SemaphoreType.DMA((4,)),
    ]

    def __init__(self, links, own, theirs, twin, far, near, twin_sems, ring_sems):
        self.links, self.own, self.theirs, self.twin = links, own, theirs, twin
        self.far, self.near, self.twin_sems, self.ring_sems = far, near, twin_sems, ring_sems
        self.twins, self.sent = {}, {}

    def place(self, k, core):
        if not core:
            return self.own.at[k]
        step = ORDER.index(k)
        if step >= 2:
            self.links.left(self.twins[ORDER[step - 2]])
        return self.theirs.at[step % 2]

    def to_twin(self, k):
        self.twins[k] = self.links.send(
            self.theirs.at[ORDER.index(k) % 2], self.twin.at[k], self.twin_sems.at[k], self.links.at(dc=1)
        )

    def add_twin(self, k):
        self.twins[k].wait_recv()
        self.own[k] = (self.own[k].astype(F32) + self.twin[k].astype(F32)).astype(BF)

    def pass_on(self, k):
        links, own = self.links, self.own
        self.add_twin(k)
        if k == 2:
            for i, to in ((0, 1), (1, 3)):
                self.sent[i] = links.send(
                    own.at[2, pl.ds(128 * i, 128)], self.far.at[i], self.ring_sems.at[i], links.at(dy=to)
                )
        elif k:
            i = 0 if k == 1 else 1
            half = pl.ds(128 * i, 128)
            self.sent[i].wait_recv()
            own[k, half, :] = (own[k, half, :].astype(F32) + self.far[i].astype(F32)).astype(BF)
            self.sent[3 - i] = links.send(own.at[k], self.near.at[1 - i], self.ring_sems.at[3 - i], links.at(dy=k))

    def total(self):
        for i in (0, 1):
            self.sent[2 + i].wait_recv()
        return self.own[0].astype(F32) + self.near[0].astype(F32) + self.near[1].astype(F32)


def expert_kernel(
    w_all, x_all, c_all, gates_all, router_all, gx_out, mix_out, dw_out, router_out, *rest
):
    w, gates, router, xs, cs, hidden, d_gate, d_up, d_logit, staged = rest[:10]
    grads, mixes = rest[10:17], rest[17:21]
    send_sems, load_sems, dw_sems, local_sems = rest[21:]
    links = Links(send_sems, local_sems)
    yh, _, _, c, t = links.me
    y = yh * 2 + t
    tables = [links.keep(w_all, w), links.keep(gates_all, gates), links.keep(router_all, router)]
    loads = {}
    for k in (2, 1, 3, 0):
        for core in (1, 0):
            b = up4(y, k) * 2 + up2(c, core)
            for n, (src, dst) in enumerate(((x_all, xs), (c_all, cs))):
                copy = pltpu.make_async_copy(src.at[b], dst.at[rows_of(b), :], load_sems.at[(k * 2 + core) * 2 + n])
                copy.start()
                loads[(k, core, n)] = copy
    links.barrier([links.at(**p) for p in RING + TWIN])
    lane = lax.broadcasted_iota(jnp.int32, (OWN, 128), 1)
    mine = (lane == y * 2 + c).astype(F32)
    grad_sum, mix_sum = RingSum(links, *grads), RingSum(links, *mixes[:3], None, None, mixes[3], None)

    def one_block(b, grad, mix):
        rows = rows_of(b)
        xb, cb = xs[rows, :], cs[rows, :]
        table = jnp.concatenate([gates[b], jnp.zeros((120, OWN), F32)], axis=0).T
        gate = jnp.sum(table * mine, axis=1, keepdims=True)
        grad_gate = jnp.zeros((OWN, 1), F32)
        for n in range(3):
            columns = slice(256 * n, 256 * (n + 1))
            gate_in = nn(xb, w[0, :, columns])
            up_in = nn(xb, w[1, :, columns])
            back = nn(cb, w[2, :, columns])
            sig = 0.5 * jnp.tanh(0.5 * gate_in) + 0.5
            act = gate_in * sig
            hid = act * up_in
            grad_gate = grad_gate + jnp.sum(hid * back, axis=1, keepdims=True)
            grad_hidden = gate * back
            hidden[rows, columns] = (gate * hid).astype(BF)
            d_gate[rows, columns] = (grad_hidden * up_in * (sig + act * (1.0 - sig))).astype(BF)
            d_up[rows, columns] = (grad_hidden * act).astype(BF)
        dl = (gate * grad_gate * (mine - table)).astype(BF)
        d_logit[rows, :] = dl
        dg, du, hw = d_gate[rows, :], d_up[rows, :], hidden[rows, :]
        for n in range(6):
            columns = slice(256 * n, 256 * (n + 1))
            grad[:, columns] = (
                nt(dg, w[0, columns, :]) + nt(du, w[1, columns, :]) + nt(dl, router[columns, :])
            ).astype(BF)
            mix[:, columns] = nt(hw, w[2, columns, :]).astype(BF)

    for copy in tables:
        copy.wait()
    mixed = []

    def mix_done(k):
        mix_sum.add_twin(k)
        return links.keep(mix_sum.own.at[k], mix_out.at[k])

    done = None
    for k in ORDER:
        for core in (1, 0):
            loads[(k, core, 0)].wait()
            loads[(k, core, 1)].wait()
            b = up4(y, k) * 2 + up2(c, core)
            one_block(b, grad_sum.place(k, core), mix_sum.place(k, core))
            if core:
                grad_sum.to_twin(k)
                mix_sum.to_twin(k)
                if done is not None:
                    grad_sum.pass_on(done)
                    mixed.append(mix_done(done))
        done = k
    grad_sum.pass_on(0)
    mixed.append(mix_done(0))

    def strip(i, carry):
        columns = rows_of(i)
        xt = xs[:, columns]
        slot = lax.rem(i, 2)

        def stored(n, at):
            return pltpu.make_async_copy(staged.at[slot, n], dw_out.at[n, rows_of(at)], dw_sems.at[slot * 3 + n])

        @pl.when(i >= 2)
        def _():
            for n in range(3):
                stored(n, i - 2).wait()

        for n, (left, right) in enumerate(((xt, d_gate), (xt, d_up), (cs[:, columns], hidden))):
            staged[slot, n] = tn(left, right[...]).astype(BF)
        router_out[:, columns] = tn(d_logit[...], xt)[:8, :]
        for n in range(3):
            stored(n, i).start()
        return carry

    lax.fori_loop(0, 6, strip, 0)
    gx_out[...] = grad_sum.total()
    for copy in mixed:
        copy.wait()
    for slot in range(2):
        for n in range(3):
            pltpu.make_async_copy(staged.at[slot, n], dw_out.at[n, rows_of(4 + slot)], dw_sems.at[slot * 3 + n]).wait()
    links.finish()


def run_expert(w, x_all, c_all, gates, router):
    return pl.pallas_call(
        expert_kernel,
        out_shape=(
            jax.ShapeDtypeStruct((OWN, D), F32),
            jax.ShapeDtypeStruct((4, OWN, D), BF),
            jax.ShapeDtypeStruct((3, D, HALF), BF),
            jax.ShapeDtypeStruct((8, D), F32),
        ),
        in_specs=[ANY] * 5,
        out_specs=(VMEM, ANY, ANY, VMEM),
        scratch_shapes=[
            pltpu.VMEM((3, D, HALF), BF),
            pltpu.VMEM((8, 8, OWN), F32),
            pltpu.VMEM((D, WIDE - PART), BF),
            pltpu.VMEM((8 * OWN, D), BF),
            pltpu.VMEM((8 * OWN, D), BF),
            pltpu.VMEM((8 * OWN, HALF), BF),
            pltpu.VMEM((8 * OWN, HALF), BF),
            pltpu.VMEM((8 * OWN, HALF), BF),
            pltpu.VMEM((8 * OWN, 128), BF),
            pltpu.VMEM((2, 3, OWN, HALF), BF),
        ]
        + RingSum.SCRATCH
        + RingSum.SCRATCH[:3]
        + RingSum.SCRATCH[5:6]
        + [pltpu.SemaphoreType.DMA((n,)) for n in (24, 16, 6, 7)],
        compiler_params=pltpu.CompilerParams(
            collective_id=5, has_side_effects=True, vmem_limit_bytes=60 * MIB
        ),
        name="expert",
    )(w, x_all, c_all, gates, router)


def plane_reduce(links, h, ops, sems):
    def target(k, stage):
        return links.at(dx=k) if (h == 0) == (stage == 1) else links.at(dz=k)

    for stage in (0, 1):
        base = 4 * stage
        far, near = {}, {}
        for i, k in ((0, 1), (1, 3)):
            far[i] = links.send(ops.far(stage, i), ops.far_land(stage, i), sems.at[base + i], target(k, stage))
        yield
        for i, k in ((0, 1), (1, 3)):
            ops.ready(stage, k)
            far[i].wait_recv()
            ops.add_far(stage, i, k)
            near[i] = links.send(
                ops.near(stage, k), ops.near_land(stage, 1 - i), sems.at[base + 3 - i], target(k, stage)
            )
        yield
        ops.ready(stage, 0)
        for i in (0, 1):
            near[i].wait_recv()
        ops.total(stage)
    yield


def loop(counts, fn):
    a, b = counts

    def body(i, carry):
        fn(lax.div(i, b), lax.rem(i, b))
        return carry

    lax.fori_loop(0, a * b, body, 0)


SLOT = {1: 0, 3: 1, 0: 2}


class ExpertOps:
    SCRATCH = [
        pltpu.VMEM((2, 3, 3, 4, 48, HALF), BF),
        pltpu.VMEM((2, 2, 3, 4, 48, 384), BF),
        pltpu.VMEM((2, 2, 3, 4, 48, HALF), BF),
        pltpu.VMEM((2, 4, 3, 48, HALF), BF),
        pltpu.VMEM((2, 2, 3, 48, 384), BF),
        pltpu.VMEM((2, 2, 3, 48, HALF), BF),
        pltpu.VMEM((2, 2, 3, 24, HALF), BF),
    ]

    def __init__(self, links, h, g, acc, far1, near1, mid, far2, near2, last):
        self.h, self.g, self.acc, self.far1, self.near1 = h, g, acc, far1, near1
        self.mid, self.far2, self.near2, self.last = mid, far2, near2, last
        _, self.x, self.z, _, _ = links.me
        self.loads = {k: links.keep(self.block(k), acc.at[h, SLOT[k]]) for k in (1, 3, 0)}

    def block(self, k, *columns):
        if self.h == 0:
            return self.g.at[(slice(None), 0, slice(None), up4(self.z, k), slice(None)) + columns]
        return self.g.at[(slice(None), 1, up4(self.x, k), slice(None), slice(None)) + columns]

    def ready(self, stage, k):
        if stage == 0:
            self.loads[k].wait()

    def far(self, stage, i):
        columns = pl.ds(384 * i, 384)
        return self.mid.at[self.h, 2, :, :, columns] if stage else self.block(2, columns)

    def far_land(self, stage, i):
        return (self.far2 if stage else self.far1).at[self.h, i]

    def near(self, stage, k):
        return self.mid.at[self.h, k] if stage else self.acc.at[self.h, SLOT[k]]

    def near_land(self, stage, i):
        return (self.near2 if stage else self.near1).at[self.h, i]

    def add_far(self, stage, i, k):
        h, columns = self.h, slice(384 * i, 384 * (i + 1))

        def first(m, a):
            s = SLOT[k]
            self.acc[h, s, m, a, :, columns] = (
                self.acc[h, s, m, a, :, columns].astype(F32) + self.far1[h, i, m, a].astype(F32)
            ).astype(BF)

        def second(m, _):
            self.mid[h, k, m, :, columns] = (
                self.mid[h, k, m, :, columns].astype(F32) + self.far2[h, i, m].astype(F32)
            ).astype(BF)

        loop((3, 1) if stage else (3, 4), second if stage else first)

    def total(self, stage):
        h = self.h
        here = self.x if h == 0 else self.z

        def first(k, m):
            a = up4(here, k)
            self.mid[h, k, m] = (
                self.acc[h, 2, m, a].astype(F32)
                + self.near1[h, 0, m, a].astype(F32)
                + self.near1[h, 1, m, a].astype(F32)
            ).astype(BF)

        def second(m, _):
            value = (
                self.mid[h, 0, m].astype(F32)
                + self.near2[h, 0, m].astype(F32)
                + self.near2[h, 1, m].astype(F32)
            )
            self.last[h, 0, m] = value[:24, :].astype(BF)
            self.last[h, 1, m] = value[24:, :].astype(BF)

        loop((3, 1) if stage else (4, 3), second if stage else first)


def attention_scratch(width):
    return [
        pltpu.VMEM((2, 2, 2, 4, 4, 48, width), BF),
        pltpu.VMEM((2, 4, 2, 4, 48, width), BF),
        pltpu.VMEM((2, 2, 4, 48, width), BF),
        pltpu.VMEM((2, 2, 2, 4, 48, width), BF),
        pltpu.VMEM((2, 4, 2, 48, width), BF),
        pltpu.VMEM((2, 2, 48, width), BF),
        pltpu.VMEM((2, 2, 2, 48, width), BF),
        pltpu.VMEM((2, 2, 48, width), BF),
    ]


class AttentionOps:
    def __init__(self, links, h, twin_sems, g, twin, far1, near1, mid, far2, near2, last):
        self.h, self.g, self.twin, self.far1, self.near1 = h, g, twin, far1, near1
        self.mid, self.far2, self.near2, self.last = mid, far2, near2, last
        _, self.x, self.z, self.c, _ = links.me
        self.twins = {}
        for k in (2, 1, 3, 0):
            self.twins[k] = links.send(
                self.block(1 - self.c, k), twin.at[h, k], twin_sems.at[h * 4 + k], links.at(dc=1)
            )

    def place(self, k):
        return up4(self.z if self.h == 0 else self.x, k)

    def block(self, core, k):
        if self.h == 0:
            return self.g.at[0, core, :, :, self.place(k)]
        return self.g.at[1, core, :, self.place(k)]

    def get(self, k, i, a):
        return self.g[0, self.c, i, a, self.place(k)] if self.h == 0 else self.g[1, self.c, i, self.place(k), a]

    def put(self, k, i, a, value):
        if self.h == 0:
            self.g[0, self.c, i, a, self.place(k)] = value.astype(BF)
        else:
            self.g[1, self.c, i, self.place(k), a] = value.astype(BF)

    def add_twin(self, k):
        self.twins[k].wait_recv()

        def add(i, a):
            self.put(k, i, a, self.get(k, i, a).astype(F32) + self.twin[self.h, k, i, a].astype(F32))

        loop((2, 4), add)

    def ready(self, stage, k):
        if stage == 0:
            self.add_twin(k)

    def far(self, stage, i):
        if stage:
            return self.mid.at[self.h, 2, i]
        if i == 0:
            self.add_twin(2)
        if self.h == 0:
            return self.g.at[0, self.c, i, :, self.place(2)]
        return self.g.at[1, self.c, i, self.place(2)]

    def far_land(self, stage, i):
        return (self.far2 if stage else self.far1).at[self.h, i]

    def near(self, stage, k):
        return self.mid.at[self.h, k] if stage else self.block(self.c, k)

    def near_land(self, stage, i):
        return (self.near2 if stage else self.near1).at[self.h, i]

    def add_far(self, stage, i, k):
        h = self.h
        if stage:
            self.mid[h, k, i] = (self.mid[h, k, i].astype(F32) + self.far2[h, i].astype(F32)).astype(BF)
            return

        def add(a, _):
            self.put(k, i, a, self.get(k, i, a).astype(F32) + self.far1[h, i, a].astype(F32))

        loop((4, 1), add)

    def total(self, stage):
        h = self.h
        here = self.x if h == 0 else self.z

        def first(k, i):
            a = up4(here, k)
            self.mid[h, k, i] = (
                self.get(0, i, a).astype(F32)
                + self.near1[h, 0, i, a].astype(F32)
                + self.near1[h, 1, i, a].astype(F32)
            ).astype(BF)

        def second(i, _):
            self.last[h, i] = (
                self.mid[h, 0, i].astype(F32)
                + self.near2[h, 0, i].astype(F32)
                + self.near2[h, 1, i].astype(F32)
            ).astype(BF)

        loop((2, 1) if stage else (4, 2), second if stage else first)


def backward_kernel(
    g, w_in, w_out, mix, gx,
    cot_in, tok_in, residual_in, normed_in, q_in, k_in, v_in, att_in, cosine_in, sine_in, gains_in, router_in,
    ge, grad_input, layer_output, grad_q, grad_k, grad_v, grad_o, small_out, *rest
):
    expert_refs, in_refs, out_refs = rest[:7], rest[7:15], rest[15:23]
    inputs = rest[23:34]
    cot, residual, normed, q, k, v, att, cosine, sine, gains, router = inputs
    (
        wqkv, flow, grad_residual, grad_branch, lin, kv_own, kv_send, kv_recv,
        ring_in, ring_out, swap_in_own, swap_in_out, swap_in_in, swap_out_own, swap_out_out, swap_out_in,
        small, s_twin, s_land, s_back, mix_far, mix_near,
    ) = rest[34:56]
    (
        send_sems, local_sems, expert_sems, in_sems, out_sems, in_twin_sems, out_twin_sems, back_sems, kv_sems,
        ring_sems, swap_sems, small_sems, mix_sems,
    ) = rest[56:]
    links = Links(send_sems, local_sems)
    yh, x, z, c, t = links.me
    twin = links.at(dc=1)
    loads = [
        links.keep(src, dst)
        for src, dst in zip(
            (gx, cot_in, residual_in, gains_in, normed_in, q_in, k_in, v_in, att_in, cosine_in, sine_in, router_in),
            (flow, cot, residual, gains, normed, q, k, v, att, cosine, sine, router),
        )
    ]
    out_load = links.keep(w_out.at[0], wqkv.at[:, :, :, pl.ds(0, 384)])
    links.barrier([links.at(**p) for p in ALONG + RING + CROSS + TWIN])
    reduce_experts = [
        plane_reduce(links, h, ExpertOps(links, h, g, *expert_refs), expert_sems.at[pl.ds(8 * h, 8)])
        for h in (0, 1)
    ]

    def step(group, count=1):
        for _ in range(count):
            for steps in group:
                next(steps, None)

    step(reduce_experts)
    mix_sent = {}
    for i, to in ((0, 1), (1, 3)):
        mix_sent[i] = links.send(
            mix.at[2, pl.ds(128 * i, 128)], mix_far.at[i], mix_sems.at[i], links.at(dy=to)
        )

    for copy in loads[:4]:
        copy.wait()
    scaled = flow[...] * gains[1:2, :]
    value = residual[...]
    inverse = inverse_norm(value)
    mean = jnp.mean(scaled * value, axis=1, keepdims=True)
    grad = cot[...].astype(F32) + inverse * scaled - value * (inverse * inverse * inverse * mean)
    gain_two = jnp.sum(flow[...] * (value * inverse), axis=0, keepdims=True)
    grad_residual[...] = grad
    grad_branch[...] = grad.astype(BF)
    mix_load = [links.keep(mix.at[to, pl.ds(at, 128)], cot.at[pl.ds(at, 128)]) for to, at in ((1, 0), (3, 128))]
    for copy in loads[4:]:
        copy.wait()
    bias = causal_bias(t)
    cos_own, sin_own = cosine[...], sine[...]

    def weight_rows(left, right, store):
        for i in (0, 1):
            for half in (0, 1):
                first = HALF * i + 384 * half
                rows = tn(left[:, first : first + 384], right)
                store(i, slice(2 * half, 2 * half + 2), rows.reshape(2, 4, 48, rows.shape[1]).astype(BF))

    def start(refs, twin_sems, sems, group):
        j = len(group)
        ops = AttentionOps(links, j, twin_sems, *refs)
        group.append(plane_reduce(links, j, ops, sems.at[pl.ds(8 * j, 8)]))

    reduce_out, reduce_in = [], []
    for j in (0, 1):

        def store_out(i, at, value, j=j):
            for half in (0, 1):
                out_refs[0][j, half, i, at] = value[..., 384 * half : 384 * (half + 1)]

        weight_rows(grad_branch, att[j], store_out)
        start(out_refs, out_twin_sems, out_sems, reduce_out)
    step(reduce_out)
    step(reduce_experts)
    tok_load = [links.keep(tok_in.at[:, pl.ds(HALF * i, HALF)], att.at[i]) for i in (0, 1)]

    exchanges = []
    for j in (0, 1):
        out_load.wait()
        grad_att = jnp.concatenate(
            [
                nn(grad_branch[:, :HALF], wqkv[half, 0, :, :384])
                + nn(grad_branch[:, HALF:], wqkv[half, 1, :, :384])
                for half in (0, 1)
            ],
            axis=1,
        ).astype(BF)
        if j == 0:
            out_load = links.keep(w_out.at[1], wqkv.at[:, :, :, pl.ds(0, 384)])
        else:
            in_load = links.keep(w_in.at[0], wqkv)
        kj, vj = k[j], v[j]
        gk = jnp.zeros((SEQ, HD), F32)
        gv = jnp.zeros((SEQ, HD), F32)
        for h in range(6):
            lanes = slice(HD * h, HD * (h + 1))
            qh, gh = q[j, :, lanes], grad_att[:, lanes]
            scores = nt(qh, kj) * SCALE + bias
            raised = jnp.exp(scores - jnp.max(scores, axis=1, keepdims=True))
            exact = raised * (1.0 / jnp.sum(raised, axis=1, keepdims=True))
            grad_probs = nt(gh, vj)
            centred = jnp.sum(exact * grad_probs, axis=1, keepdims=True)
            grad_scores = (exact * (grad_probs - centred)).astype(BF)
            lin[j, :, lanes] = unroped(nn(grad_scores, kj) * SCALE, cos_own, sin_own).astype(BF)
            gk = gk + tn(grad_scores, qh)
            gv = gv + tn(exact.astype(BF), gh)
            if (j, h) == (1, 0):
                step(reduce_out)
        both = jnp.concatenate([gk * SCALE, gv], axis=1)
        low, high = both[:OWN, :], both[OWN:, :]
        kv_own[j] = jnp.where(t == 0, low, high)
        kv_send[j] = jnp.where(t == 0, high, low).astype(BF)
        exchanges.append(links.send(kv_send.at[j], kv_recv.at[j], kv_sems.at[j], links.flip(dt=1)))
    for copy in mix_load:
        copy.wait()
    for i, to in ((0, 1), (1, 3)):
        mix_sent[i].wait_recv()
        half = pl.ds(128 * i, 128)
        keep = pl.ds(128 * (1 - i), 128)
        cot[half, :] = (cot[half, :].astype(F32) + mix_far[i].astype(F32)).astype(BF)
        mix_sent[2 + i] = links.send(mix.at[to, keep], mix_near.at[i, keep], mix_sems.at[2 + i], links.at(dy=to))
        mix_sent[4 + i] = links.send(cot.at[half], mix_near.at[i, half], mix_sems.at[4 + i], links.at(dy=to))

    step(reduce_experts)

    for j in (0, 1):
        exchanges[j].wait_recv()
        total = kv_own[j] + kv_recv[j].astype(F32)
        lin[j, :, HALF:PART] = unroped(total[:, :HD], cos_own, sin_own).astype(BF)
        lin[j, :, PART:] = total[:, HD:].astype(BF)

        def store_in(i, at, value, j=j):
            for half in (0, 1):
                in_refs[0][j, half, i, at] = value[..., 512 * half : 512 * (half + 1)]

        weight_rows(normed, lin[j], store_in)
        start(in_refs, in_twin_sems, in_sems, reduce_in)
        in_load.wait()
        for i in (0, 1):
            columns = slice(HALF * i, HALF * (i + 1))
            part = nt(lin[j, :, :512], wqkv[0, i]) + nt(lin[j, :, 512:], wqkv[1, i])
            flow[:, columns] = part if j == 0 else flow[:, columns] + part
        if j == 0:
            in_load = links.keep(w_in.at[1], wqkv)
        next(reduce_in[j])
    mix_last = links.keep(mix.at[0], normed)
    for copy in tok_load:
        copy.wait()

    gradient = flow[...]
    scaled = gradient * gains[0:1, :]
    value = jnp.concatenate([att[0], att[1]], axis=1).astype(F32)
    inverse = inverse_norm(value)
    mean = jnp.mean(scaled * value, axis=1, keepdims=True)
    grad_branch[...] = (
        grad_residual[...] + inverse * scaled - value * (inverse * inverse * inverse * mean)
    ).astype(BF)
    results = [links.keep(grad_branch, grad_input)]
    gain_one = jnp.sum(gradient * (value * inverse), axis=0, keepdims=True)
    rows = jnp.concatenate([router[...], gain_one, gain_two, jnp.zeros((6, D), F32)], axis=0)
    small[0] = rows[:, :HALF]
    small[1] = rows[:, HALF:]
    s_copy = links.send(small.at[1 - c], s_twin, small_sems.at[0], twin)
    def everyone(axis, at):
        copies = {}
        for k in (1, 2, 3):
            j = 4 - k
            copies[j] = links.send(
                small.at[c], s_land.at[at, j - 1], small_sems.at[3 * at + j], links.at(**{axis: k})
            )
        return copies

    def settle(copies, at):
        for copy in copies.values():
            copy.wait_recv()
            links.left(copy)
        small[c] = small[c] + s_land[at, 0] + s_land[at, 1] + s_land[at, 2]

    def around(refs, ring, base):
        copies = []
        for dyh, dt in ((1, 1), (1, 0), (0, 1)):
            index = dyh * 2 + dt - 1
            copies.append(
                links.send(
                    refs[7].at[up2(t, dt), up2(yh, dyh)], ring.at[index], ring_sems.at[base + index],
                    links.flip(dyh=dyh, dt=dt),
                )
            )
        return copies

    def collect(copies, refs, ring, own, theirs, mine, at):
        for copy in copies:
            copy.wait_recv()
        total = refs[7][t, yh].astype(F32)
        for i in range(3):
            total = total + ring[i].astype(F32)
        theirs[...] = jnp.where(c == 0, total[24:, :], total[:24, :])
        swap = links.send(theirs, mine, swap_sems.at[at], twin)
        own[...] = jnp.where(c == 0, total[:24, :], total[24:, :])
        return swap

    def halves(swap, own, mine):
        swap.wait_recv()
        return jnp.where(c == 0, own[...], mine[...]), jnp.where(c == 0, mine[...], own[...])

    step(reduce_out)
    s_copy.wait_recv()
    small[c] = small[c] + s_twin[...]
    copies = everyone("dz", 0)
    step(reduce_experts)
    step(reduce_in)
    step(reduce_out)
    settle(copies, 0)
    copies = everyone("dx", 1)
    step(reduce_experts)

    last, slot, back = expert_refs[6], (yh * 2 + t) * 2 + c, []
    for dyh in range(2):
        for dt in range(2):
            for dc in range(2):
                columns = pl.ds(pl.multiple_of(up2(t, dt) * 384, 384), 384)
                src = last.at[up2(yh, dyh), up2(c, dc), :, :, columns]
                if dyh + dt + dc == 0:
                    stay = links.keep(src, ge.at[slot])
                else:
                    index = (dyh * 2 + dt) * 2 + dc
                    back.append(
                        links.send(src, ge.at[slot], back_sems.at[index], links.flip(dyh=dyh, dt=dt, dc=dc))
                    )

    step(reduce_out)
    out_around = around(out_refs, ring_out, 0)
    settle(copies, 1)
    copies = everyone("dy", 2)
    step(reduce_in)
    for n in (2, 3, 4, 5):
        mix_sent[n].wait_recv()
    mix_last.wait()
    normed[...] = (
        residual[...] + normed[...].astype(F32) + mix_near[0].astype(F32) + mix_near[1].astype(F32)
    ).astype(BF)
    results.append(links.keep(normed, layer_output))
    step(reduce_in)
    out_swap = collect(out_around, out_refs, ring_out, swap_out_own, swap_out_out, swap_out_in, 0)
    settle(copies, 2)
    s_copy = links.send(small.at[c], s_back, small_sems.at[10], twin)
    step(reduce_in)
    in_around = around(in_refs, ring_in, 3)
    s_copy.wait_recv()
    small_out[c] = small[c]
    small_out[1 - c] = s_back[...]
    in_swap = collect(in_around, in_refs, ring_in, swap_in_own, swap_in_out, swap_in_in, 1)
    for copy in back:
        copy.wait_recv()
    for copy in results + [stay]:
        copy.wait()
    first, second = halves(out_swap, swap_out_own, swap_out_in)
    grad_o[:, :384] = first
    grad_o[:, 384:] = second
    first, second = halves(in_swap, swap_in_own, swap_in_in)
    grad_q[:, :512] = first
    grad_q[:, 512:] = second[:, :256]
    grad_k[...] = second[:, 256:384]
    grad_v[...] = second[:, 384:]
    links.finish()


def backward(*args):
    staged = args[5:6] + args[7:]
    return pl.pallas_call(
        backward_kernel,
        out_shape=(
            jax.ShapeDtypeStruct((8, 3, 24, 384), BF),
            jax.ShapeDtypeStruct((OWN, D), BF),
            jax.ShapeDtypeStruct((OWN, D), BF),
            jax.ShapeDtypeStruct((24, HALF), F32),
            jax.ShapeDtypeStruct((24, HD), F32),
            jax.ShapeDtypeStruct((24, HD), F32),
            jax.ShapeDtypeStruct((24, HALF), F32),
            jax.ShapeDtypeStruct((2, 16, HALF), F32),
        ),
        in_specs=[ANY] * len(args),
        out_specs=(ANY,) * 3 + (VMEM,) * 5,
        scratch_shapes=ExpertOps.SCRATCH
        + attention_scratch(512)
        + attention_scratch(384)
        + [pltpu.VMEM(v.shape, v.dtype) for v in staged]
        + [
            pltpu.VMEM((2, 2, HALF, 512), BF),
            pltpu.VMEM((OWN, D), F32),
            pltpu.VMEM((OWN, D), F32),
            pltpu.VMEM((OWN, D), BF),
            pltpu.VMEM((2, OWN, WIDE), BF),
            pltpu.VMEM((2, OWN, 2 * HD), F32),
            pltpu.VMEM((2, OWN, 2 * HD), BF),
            pltpu.VMEM((2, OWN, 2 * HD), BF),
            pltpu.VMEM((3, 48, 512), BF),
            pltpu.VMEM((3, 48, 384), BF),
            pltpu.VMEM((24, 512), F32),
            pltpu.VMEM((24, 512), F32),
            pltpu.VMEM((24, 512), F32),
            pltpu.VMEM((24, 384), F32),
            pltpu.VMEM((24, 384), F32),
            pltpu.VMEM((24, 384), F32),
            pltpu.VMEM((2, 16, HALF), F32),
            pltpu.VMEM((16, HALF), F32),
            pltpu.VMEM((3, 3, 16, HALF), F32),
            pltpu.VMEM((16, HALF), F32),
            pltpu.VMEM((2, OWN // 2, D), BF),
            pltpu.VMEM((2, OWN, D), BF),
        ]
        + [pltpu.SemaphoreType.DMA((n,)) for n in (112, 40, 16, 16, 16, 8, 8, 8, 2, 6, 2, 11, 6)],
        compiler_params=pltpu.CompilerParams(
            collective_id=6, has_side_effects=True, vmem_limit_bytes=60 * MIB
        ),
        name="backward",
    )(*args)


def rope_tables():
    half_size = HD // 2
    exponent = -(np.float32(2.0) * np.arange(half_size, dtype=np.float32)) / np.float32(HD)
    frequency = np.power(np.float32(ROPE_BASE), exponent, dtype=np.float32)
    angles = np.arange(SEQ, dtype=np.float32)[:, None] * frequency[None, :]
    cosine, sine = np.cos(angles), np.sin(angles)
    return np.concatenate([cosine, cosine], axis=1), np.concatenate([-sine, sine], axis=1)


def shards(
    tokens_in, routes, cotangent, attn_gain, query_proj, key_proj, value_proj, output_proj,
    ffn_gain, router_proj, expert_gate, expert_up, expert_down,
):
    d, t = lax.axis_index("dp"), lax.axis_index("tensor")
    blank = jnp.zeros((24, 128), BF)
    extra = jnp.concatenate([router_proj, attn_gain[:, None], ffn_gain[:, None], blank[:, 10:]], axis=1)
    e_block = jnp.stack([expert_gate, expert_up, expert_down]).transpose(2, 0, 1, 3)
    own_routes = lax.dynamic_slice(routes, (OWN * t, 0), (OWN, 4))
    chosen = jnp.any(own_routes[:, :, None] == jnp.arange(128)[None, None, :], axis=1).astype(F32)
    cosine, sine = (jnp.asarray(v) for v in rope_tables())
    (
        w_in, w_out, router, experts, tok_all, cot_all, gates, normed, queries, keys, values, attended, residual, gains
    ) = forward(
        query_proj, key_proj, value_proj, output_proj, extra, e_block, tokens_in, cotangent, chosen, cosine, sine
    )
    flow, mixture, grad_experts, grad_router = run_expert(
        experts.reshape(3, D, HALF), tok_all, cot_all, gates, router.reshape(D, 128)
    )
    ge, grad_input, layer_output, grad_q, grad_k, grad_v, grad_o, small = backward(
        grad_experts.reshape(3, 2, 4, 4, 48, HALF), w_in.reshape(2, 2, 2, HALF, 512), w_out.reshape(2, 2, 2, HALF, 384), mixture, flow, cotangent, tokens_in, residual,
        normed, queries, keys, values, attended,
        lax.dynamic_slice(cosine, (OWN * t, 0), (OWN, HD)), lax.dynamic_slice(sine, (OWN * t, 0), (OWN, HD)),
        gains, grad_router,
    )
    ge = ge.astype(F32).transpose(1, 2, 0, 3)
    small = jnp.concatenate([small[0], small[1]], axis=1)
    small = lax.dynamic_slice(small, (0, 24 * d + 12 * t), (16, 12))
    return (
        layer_output,
        grad_input,
        small[8],
        grad_q,
        grad_k,
        grad_v,
        grad_o,
        small[9],
        small[:8].T,
        ge[0],
        ge[1],
        ge[2],
    )


def solution(mesh):
    return jax.shard_map(
        shards,
        mesh=mesh,
        in_specs=(
            P(("dp", "tensor"), None),
            P("dp", None),
            P(("dp", "tensor"), None),
            P("dp"),
            P("dp", "tensor"),
            P("dp", "tensor"),
            P("dp", "tensor"),
            P("dp", "tensor"),
            P("dp"),
            P("dp", None),
            P("dp", None, "tensor"),
            P("dp", None, "tensor"),
            P("dp", None, "tensor"),
        ),
        out_specs=(
            P(("dp", "tensor"), None),
            P(("dp", "tensor"), None),
            P(("dp", "tensor")),
            P("dp", "tensor"),
            P("dp", "tensor"),
            P("dp", "tensor"),
            P("dp", "tensor"),
            P(("dp", "tensor")),
            P(("dp", "tensor"), None),
            P("dp", None, "tensor"),
            P("dp", None, "tensor"),
            P("dp", None, "tensor"),
        ),
        check_vma=False,
    )
```
